32 devices in a mesh: az: 8 (over z, x), rg: 4 (over y, core).
Axes of the slice: x: 2, y: 2, z: 4, core: 2. Of those that a mesh axis runs over, the one named last changes fastest.
Arguments:
- raw_echo: bfloat16 [2, 8192, 1536], P(None, 'az', 'rg'), may hold values from -6 to 6
- range_chirp: bfloat16 [2, 512], replicated, may hold values from -0.1875 to 0.1875
- migration_taps: bfloat16 [8, 1536], P(None, 'rg'), may hold values from -2.09375 to 2.09375
- block_shift: int32 [12], P('rg'), may hold values from -60 to 60, as said below
- azimuth_chirp: bfloat16 [12, 2, 512], P('rg'), may hold values from -0.1875 to 0.1875
Outputs:
- focused_image: float32 [2, 8192, 1536], P(None, 'az', 'rg')
The draws below stay inside these ranges and needn't reach their ends.
Inputs may be any that keep to these rules, and one draw needn't show every extreme that they name: `block_shift`: every range block of 128 cells has one shift; the values -60 and 60 both occur in every draw.
All inputs are finite; a program needn't handle non-finite values.
Results may differ from the reference program's by a relative error of at most 0.0041.
Values may be sent and summed in bfloat16 or wider, within the bound.
No kernel may reach another device: no remote copies, remote signals or barrier semaphores. Data moves between devices by JAX's collectives and lax.ppermute only.
A program may use at most 64 MiB of HBM per device.

```python
import jax
import jax.numpy as jnp
from jax import lax

AZ_DEV = 1024
RTAPS = 512
ATAPS = 512
TAPS = 8
MAXS = 60
BLK = 128
NA = 8192
NR = 1536
NRB = 12


def draw_block_shift(key, part):
    block_count = NR // BLK
    value_key = jax.random.fold_in(key, 11)
    order_key = jax.random.fold_in(key, 12)
    values = jax.random.randint(value_key, (block_count,), -MAXS, MAXS + 1, dtype=jnp.int32)
    placing = jax.random.permutation(order_key, block_count)
    values = values.at[placing[0]].set(-MAXS)
    return values.at[placing[1]].set(MAXS)


def levels(own_key, dims, split, low, largest):
    level = 1.0
    for axis_at, shards_of in split:
        steps = jax.random.uniform(jax.random.fold_in(jax.random.fold_in(own_key, 6), axis_at), (shards_of,), jnp.float32, low / len(split), largest / len(split))
        level = level * jnp.repeat(jnp.exp(steps), dims[axis_at] // shards_of).reshape((-1,) + (1,) * (len(dims) - 1 - axis_at))
    return level


def centred(key, extent, width, bound, shards=(), held_as=jnp.bfloat16):
    result = width * jax.random.normal(key, extent, jnp.float32)
    if shards:
        result = result * levels(key, extent, shards, -0.22, 0.18)
    return jnp.clip(result, -bound, bound).astype(held_as)


def setup_inputs(seed: int = 0) -> dict:
    keys = jax.random.split(jax.random.key(seed), 6)
    raw_echo = centred(keys[0], (2, NA, NR), 1.0, 6.0, ((1, 8), (2, 4)))
    range_chirp = centred(keys[1], (2, RTAPS), (2 * RTAPS) ** -0.5, 0.1875)
    migration_taps = centred(keys[2], (TAPS, NR), 0.35, 2.09375, ((1, 4),))
    block_shift = draw_block_shift(jax.random.fold_in(keys[5], 71), 0)
    azimuth_chirp = centred(keys[4], (NRB, 2, ATAPS), (2 * ATAPS) ** -0.5, 0.1875, ((0, 4),))
    return {"raw_echo": raw_echo, "range_chirp": range_chirp, "migration_taps": migration_taps, "block_shift": block_shift, "azimuth_chirp": azimuth_chirp}


def correlate(signal, tap_values):
    cell_total = signal.shape[-1]
    tap_count = tap_values.shape[0]
    length = cell_total + tap_count
    kernel = jnp.pad(jnp.conj(tap_values)[::-1], (0, length - tap_count))
    kernel = jnp.roll(kernel, -(tap_count // 2 - 1))
    spectrum = jnp.fft.fft(signal, n=length, axis=-1) * jnp.fft.fft(kernel)
    return jnp.fft.ifft(spectrum, axis=-1)[..., :cell_total]


def reference(raw_echo, range_chirp, migration_taps, block_shift, azimuth_chirp):
    margin = MAXS + TAPS // 2
    chirp_complex = range_chirp[0].astype(jnp.float32) + 1j * range_chirp[1].astype(jnp.float32)
    shift_cells = jnp.repeat(block_shift, BLK).astype(jnp.int32)
    cell_index = lax.iota(jnp.int32, NR)
    tap_float = migration_taps.astype(jnp.float32)

    def range_section(slab_index):
        slab_data = lax.dynamic_slice_in_dim(raw_echo, slab_index * AZ_DEV, AZ_DEV, 1).astype(jnp.float32)
        compressed = correlate(slab_data[0] + 1j * slab_data[1], chirp_complex)
        rounded = jnp.stack([compressed.real, compressed.imag]).astype(jnp.bfloat16)
        rounded = lax.optimization_barrier(rounded).astype(jnp.float32)
        padded = jnp.pad(rounded, ((0, 0), (0, 0), (margin, margin)))
        summed = jnp.zeros((2, AZ_DEV, NR), jnp.float32)
        for tap_index in range(TAPS):
            source = cell_index + margin + shift_cells + (tap_index - TAPS // 2)
            summed = summed + tap_float[tap_index] * jnp.take(padded, source, axis=2)
        return summed.astype(jnp.bfloat16)

    migrated = lax.map(range_section, lax.iota(jnp.int32, NA // AZ_DEV))
    migrated = jnp.transpose(migrated, (1, 0, 2, 3)).reshape(2, NA, NR)

    def azimuth_section(block_index):
        columns = lax.dynamic_slice_in_dim(migrated, block_index * BLK, BLK, 2).astype(jnp.float32)
        signal = jnp.transpose(columns[0] + 1j * columns[1])
        tap_pair = lax.dynamic_index_in_dim(azimuth_chirp, block_index, 0, keepdims=False).astype(jnp.float32)
        focused = jnp.transpose(correlate(signal, tap_pair[0] + 1j * tap_pair[1]))
        return jnp.stack([focused.real, focused.imag]).astype(jnp.float32)

    image_blocks = lax.map(azimuth_section, lax.iota(jnp.int32, NR // BLK))
    return jnp.transpose(image_blocks, (1, 2, 0, 3)).reshape(2, NA, NR)
```

```python
import functools

import jax
import jax.numpy as jnp
from jax import lax
from jax.experimental import pallas as pl
from jax.experimental.pallas import tpu as pltpu
from jax.sharding import PartitionSpec as P

MAXS = 60
LANES = 128
HALF = 64
CHUNK = 256
VMEM_LIMIT = 48 * 1024 * 1024
F32 = jnp.float32
BF16 = jnp.bfloat16


def params():
    return pltpu.CompilerParams(vmem_limit_bytes=VMEM_LIMIT)


def whole(shape):
    return pl.BlockSpec(shape, lambda *_: (0,) * len(shape))


def lane_roll(x):
    return pltpu.roll(x.astype(F32), HALF, 1).astype(x.dtype)


def swap_pairs(count, first):
    pairs = []
    for i in range(first, count - 1, 2):
        pairs += [(i, i + 1), (i + 1, i)]
    return pairs


def shifted_rows(row, lead, width):
    taps = row.shape[1]
    padded = jnp.concatenate([row, jnp.zeros((1, width - taps), F32)], axis=1)
    return pltpu.roll(
        jnp.broadcast_to(padded, (LANES, width)), lead, 1, stride=1, stride_axis=0
    )


def build_kernel(shift_ref, range_ref, taps_ref, azimuth_ref, w_ref, m_ref, a_ref):
    depth = w_ref.shape[0] // 2
    real = shifted_rows(range_ref[0:1, :].astype(F32), HALF, depth)
    imag = shifted_rows(range_ref[1:2, :].astype(F32), HALF, depth)
    real_t, imag_t = real.T.astype(BF16), imag.T.astype(BF16)
    w_ref[0:depth, 0:LANES] = real_t
    w_ref[0:depth, LANES:] = -imag_t
    w_ref[depth:, 0:LANES] = imag_t
    w_ref[depth:, LANES:] = real_t

    span = m_ref.shape[1]
    blocks = m_ref.shape[0]
    cells = taps_ref.shape[1]
    tap_count = taps_ref.shape[0]
    first = lax.axis_index("rg") * cells - HALF
    total = lax.axis_size("rg") * cells
    for b in range(blocks):
        source = lax.broadcasted_iota(jnp.int32, (span, LANES), 0)
        column = lax.broadcasted_iota(jnp.int32, (span, LANES), 1)
        tap = source - column - (HALF - tap_count // 2) - shift_ref[b]
        place = source + first + b * LANES
        tap = jnp.where((place >= 0) & (place < total), tap, -1)
        matrix = jnp.zeros((span, LANES), F32)
        for k in range(tap_count):
            row = taps_ref[k : k + 1, b * LANES : (b + 1) * LANES].astype(F32)
            matrix = jnp.where(tap == k, row, matrix)
        m_ref[b] = matrix.astype(BF16)

    width = a_ref.shape[2]
    for b in range(blocks):
        for part in range(2):
            row = azimuth_ref[b, part : part + 1, :].astype(F32)
            rows = shifted_rows(row, 0, width - LANES).astype(BF16)
            gap = jnp.zeros((LANES, LANES), BF16)
            base = part * CHUNK
            a_ref[b, base : base + LANES, 0 : width - LANES] = rows
            a_ref[b, base : base + LANES, width - LANES :] = gap
            a_ref[b, base + LANES : base + CHUNK, 0:LANES] = gap
            a_ref[b, base + LANES : base + CHUNK, LANES:] = rows


def build(block_shift, range_chirp, migration_taps, azimuth_chirp):
    blocks = block_shift.shape[0]
    depth = range_chirp.shape[1] + 2 * LANES
    width = azimuth_chirp.shape[2] + 2 * LANES
    return pl.pallas_call(
        build_kernel,
        out_shape=(
            jax.ShapeDtypeStruct((2 * depth, 2 * LANES), BF16),
            jax.ShapeDtypeStruct((blocks, 2 * LANES, LANES), BF16),
            jax.ShapeDtypeStruct((blocks, 2 * CHUNK, width), BF16),
        ),
        in_specs=[pl.BlockSpec(memory_space=pltpu.SMEM)]
        + [pl.BlockSpec(memory_space=pltpu.VMEM)] * 3,
        out_specs=(pl.BlockSpec(memory_space=pltpu.VMEM),) * 3,
        compiler_params=params(),
        name="build_weights",
    )(block_shift, range_chirp, migration_taps, azimuth_chirp)


def write_edge(out_ref, x_ref, side):
    rows = x_ref.shape[1]
    last = x_ref.shape[2] // LANES - 1
    low = lax.broadcasted_iota(jnp.int32, (rows // 2, LANES), 1) < HALF
    at = 0
    for part in range(2):
        for tile in ((0, 1) if side == 0 else (last - 1, last)):
            out_ref[0, at : at + rows, :] = x_ref[part, :, tile * LANES : (tile + 1) * LANES]
            at += rows
    for part in range(2):
        tile = 2 if side == 0 else last - 2
        cells = x_ref[part, :, tile * LANES : (tile + 1) * LANES].astype(F32)
        top, bottom = cells[: rows // 2], cells[rows // 2 :]
        if side == 0:
            packed = jnp.where(low, top, pltpu.roll(bottom, HALF, 1))
        else:
            packed = jnp.where(low, pltpu.roll(top, HALF, 1), bottom)
        out_ref[0, at : at + rows // 2, :] = packed.astype(BF16)
        at += rows // 2


def edges_kernel(x_ref, core_ref, far_ref):
    odd = lax.rem(lax.axis_index("rg"), 2)

    @pl.when(odd == 0)
    def _():
        write_edge(core_ref, x_ref, 1)
        write_edge(far_ref, x_ref, 0)

    @pl.when(odd == 1)
    def _():
        write_edge(core_ref, x_ref, 0)
        write_edge(far_ref, x_ref, 1)


def range_edges(raw, chunks, chunk_of, name):
    cells = raw.shape[2]
    edge = jax.ShapeDtypeStruct((chunks, 5 * CHUNK, LANES), BF16)
    spec = pl.BlockSpec((1, 5 * CHUNK, LANES), lambda g: (g, 0, 0))
    return pl.pallas_call(
        edges_kernel,
        grid=(chunks,),
        out_shape=(edge, edge),
        in_specs=[pl.BlockSpec((2, CHUNK, cells), lambda g: (0, chunk_of(g), 0))],
        out_specs=(spec, spec),
        compiler_params=params(),
        name=name,
    )(raw)


def read_edge(wide_ref, in_ref, side, rows, last):
    at = 0
    for part in range(2):
        for tile in ((1, 2) if side == 0 else (last - 2, last - 1)):
            wide_ref[part, :, tile * LANES : (tile + 1) * LANES] = in_ref[0, at : at + rows, :]
            at += rows
    for part in range(2):
        packed = in_ref[0, at : at + rows // 2, :]
        rolled = lane_roll(packed)
        top, bottom = (rolled, packed) if side == 0 else (packed, rolled)
        lanes = slice(0, LANES) if side == 0 else slice(last * LANES, (last + 1) * LANES)
        wide_ref[part, : rows // 2, lanes] = top
        wide_ref[part, rows // 2 :, lanes] = bottom
        at += rows // 2


def compress_chunk(x_ref, core_ref, far_ref, w_ref, m_ref, wide_ref, c_ref, store):
    rows, cells = x_ref.shape[1], x_ref.shape[2]
    last = wide_ref.shape[2] // LANES - 1
    depth = w_ref.shape[0] // 2
    odd = lax.rem(lax.axis_index("rg"), 2)

    @pl.when(odd == 0)
    def _():
        read_edge(wide_ref, far_ref, 0, rows, last)
        read_edge(wide_ref, core_ref, 1, rows, last)

    @pl.when(odd == 1)
    def _():
        read_edge(wide_ref, core_ref, 0, rows, last)
        read_edge(wide_ref, far_ref, 1, rows, last)

    wide_ref[:, :, 3 * LANES : 3 * LANES + cells] = x_ref[...]
    for j in range(c_ref.shape[1] // LANES):
        lanes = slice(j * LANES, j * LANES + depth)
        window = jnp.concatenate([wide_ref[0, :, lanes], wide_ref[1, :, lanes]], axis=1)
        result = jnp.dot(window, w_ref[...], preferred_element_type=F32).astype(BF16)
        c_ref[0:rows, j * LANES : (j + 1) * LANES] = result[:, :LANES]
        c_ref[rows:, j * LANES : (j + 1) * LANES] = result[:, LANES:]
    for b in range(m_ref.shape[0]):
        window = c_ref[:, b * LANES : b * LANES + 2 * LANES]
        result = jnp.dot(window, m_ref[b], preferred_element_type=F32).astype(BF16)
        store(b, result[:rows], result[rows:])


def outer_kernel(
    x_ref, core_ref, far_ref, w_ref, m_ref, out_ref, near_ref, away_ref, wide_ref, c_ref
):
    step = pl.program_id(0)
    odd = lax.rem(lax.axis_index("az"), 2)

    def store(b, real, imag):
        out_ref[0, :, b * LANES : (b + 1) * LANES] = real
        out_ref[1, :, b * LANES : (b + 1) * LANES] = imag

    compress_chunk(x_ref, core_ref, far_ref, w_ref, m_ref, wide_ref, c_ref, store)

    @pl.when(step + odd == 1)
    def _():
        near_ref[...] = out_ref[...]

    @pl.when(step + odd != 1)
    def _():
        away_ref[...] = out_ref[...]


def inner_kernel(
    x_ref, core_ref, far_ref, w_ref, m_ref, _, out_ref, wide_ref, c_ref
):
    def store(b, real, imag):
        out_ref[0, :, b * LANES : (b + 1) * LANES] = real
        out_ref[1, :, b * LANES : (b + 1) * LANES] = imag

    compress_chunk(x_ref, core_ref, far_ref, w_ref, m_ref, wide_ref, c_ref, store)


def compress(raw, core, far, w, m, chunks, chunk_of, before, name):
    rows, cells = raw.shape[1], raw.shape[2]
    chunk_spec = pl.BlockSpec((2, CHUNK, cells), lambda g: (0, chunk_of(g), 0))
    edge_spec = pl.BlockSpec((1, 5 * CHUNK, LANES), lambda g: (g, 0, 0))
    halo = jax.ShapeDtypeStruct((2, CHUNK, cells), BF16)
    full = jax.ShapeDtypeStruct((2, rows, cells), BF16)
    outer = before is None
    flops = chunks * CHUNK * 2 * LANES * (
        2 * w.shape[0] * (cells // LANES + 1) + 8 * LANES * m.shape[0]
    )
    return pl.pallas_call(
        outer_kernel if outer else inner_kernel,
        grid=(chunks,),
        out_shape=(full, halo, halo) if outer else full,
        in_specs=[chunk_spec, edge_spec, edge_spec, whole(w.shape), whole(m.shape)]
        + ([] if outer else [pl.BlockSpec(memory_space=pl.ANY)]),
        out_specs=(chunk_spec, whole(halo.shape), whole(halo.shape)) if outer else chunk_spec,
        scratch_shapes=[
            pltpu.VMEM((2, CHUNK, cells + 6 * LANES), BF16),
            pltpu.VMEM((2 * CHUNK, cells + LANES), BF16),
        ],
        input_output_aliases={} if outer else {5: 0},
        cost_estimate=pl.CostEstimate(
            flops=flops, bytes_accessed=chunks * CHUNK * cells * 16, transcendentals=0
        ),
        compiler_params=params(),
        name=name,
    )(raw, core, far, w, m, *(() if outer else (before,)))


def focus_window(a_ref, window, out_ref):
    for b in range(a_ref.shape[0]):
        lanes = slice(b * LANES, (b + 1) * LANES)
        both = jnp.concatenate([window(0, lanes), window(1, lanes)], axis=1)
        result = jnp.dot(a_ref[b], both, preferred_element_type=F32)
        top, bottom = result[:CHUNK], result[CHUNK:]
        out_ref[0, :, lanes] = top[:, :LANES] + bottom[:, LANES:]
        out_ref[1, :, lanes] = top[:, LANES:] - bottom[:, :LANES]


def focus_inner_kernel(a_ref, mig_ref, out_ref):
    start = pl.multiple_of(pl.program_id(0) * CHUNK, CHUNK)
    focus_window(
        a_ref, lambda part, lanes: mig_ref[part, pl.ds(start, 3 * CHUNK), lanes], out_ref
    )


def focus_inner(a, mig):
    rows, cells = mig.shape[1], mig.shape[2]
    chunks = rows // CHUNK - 2
    return pl.pallas_call(
        focus_inner_kernel,
        grid=(chunks,),
        out_shape=jax.ShapeDtypeStruct((2, rows, cells), F32),
        in_specs=[whole(a.shape), whole(mig.shape)],
        out_specs=pl.BlockSpec((2, CHUNK, cells), lambda g: (0, g + 1, 0)),
        cost_estimate=pl.CostEstimate(
            flops=2 * chunks * a.size * 2 * LANES,
            bytes_accessed=2 * (a.size + mig.size) + 8 * chunks * CHUNK * cells,
            transcendentals=0,
        ),
        compiler_params=params(),
        name="focus_inner",
    )(a, mig)


def focus_outer_kernel(a_ref, two_ref, near_ref, away_ref, _, out_ref, win_ref):
    step = pl.program_id(0)
    odd = lax.rem(lax.axis_index("az"), 2)

    @pl.when(step == 0)
    def _():
        win_ref[:, CHUNK:, :] = two_ref[...]

        @pl.when(odd == 1)
        def _():
            win_ref[:, :CHUNK, :] = near_ref[...]

        @pl.when(odd == 0)
        def _():
            win_ref[:, :CHUNK, :] = away_ref[...]

    @pl.when(step == 1)
    def _():
        win_ref[:, : 2 * CHUNK, :] = two_ref[...]

        @pl.when(odd == 0)
        def _():
            win_ref[:, 2 * CHUNK :, :] = near_ref[...]

        @pl.when(odd == 1)
        def _():
            win_ref[:, 2 * CHUNK :, :] = away_ref[...]

    focus_window(a_ref, lambda part, lanes: win_ref[part, :, lanes], out_ref)


def focus_outer(a, mig, near, away, image):
    rows, cells = mig.shape[1], mig.shape[2]
    last = rows // CHUNK - 1
    return pl.pallas_call(
        focus_outer_kernel,
        grid=(2,),
        out_shape=jax.ShapeDtypeStruct((2, rows, cells), F32),
        in_specs=[
            whole(a.shape),
            pl.BlockSpec((2, 2 * CHUNK, cells), lambda g: (0, g * (last // 2), 0)),
            whole(near.shape),
            whole(away.shape),
            pl.BlockSpec(memory_space=pl.ANY),
        ],
        out_specs=pl.BlockSpec((2, CHUNK, cells), lambda g: (0, g * last, 0)),
        scratch_shapes=[pltpu.VMEM((2, 3 * CHUNK, cells), BF16)],
        input_output_aliases={4: 0},
        cost_estimate=pl.CostEstimate(
            flops=4 * a.size * 2 * LANES, bytes_accessed=8 * CHUNK * cells, transcendentals=0
        ),
        compiler_params=params(),
        name="focus_outer",
    )(a, mig, near, away, image)


def per_device(raw_echo, range_chirp, migration_taps, block_shift, azimuth_chirp):
    chunks = raw_echo.shape[1] // CHUNK
    last = chunks - 1
    rg_count, az_count = lax.axis_size("rg"), lax.axis_size("az")
    rg_near, rg_far = swap_pairs(rg_count, 0), swap_pairs(rg_count, 1)
    az_near, az_far = swap_pairs(az_count, 0), swap_pairs(az_count, 1)

    outer_of = lambda g: g * last
    inner_of = lambda g: g + 1
    outer_core, outer_far = range_edges(raw_echo, 2, outer_of, "edges_outer")
    outer_far = lax.ppermute(outer_far, "rg", rg_far)
    outer_core = lax.ppermute(outer_core, "rg", rg_near)
    inner_core, inner_far = range_edges(raw_echo, chunks - 2, inner_of, "edges_inner")
    w, m, a = build(block_shift, range_chirp, migration_taps, azimuth_chirp)
    inner_far = lax.ppermute(inner_far, "rg", rg_far)
    inner_core = lax.ppermute(inner_core, "rg", rg_near)
    mig, near, away = compress(
        raw_echo, outer_core, outer_far, w, m, 2, outer_of, None, "compress_outer"
    )
    away = lax.ppermute(away, "az", az_far)
    near = lax.ppermute(near, "az", az_near)
    mig = compress(
        raw_echo, inner_core, inner_far, w, m, chunks - 2, inner_of, mig, "compress_inner"
    )
    image = focus_inner(a, mig)
    return focus_outer(a, mig, near, away, image)


def solution(mesh):
    placed = (P(None, "az", "rg"), P(), P(None, "rg"), P("rg"), P("rg", None, None))
    return jax.shard_map(
        per_device, mesh=mesh, in_specs=placed, out_specs=P(None, "az", "rg"), check_vma=False
    )
```

```python
import functools

import jax
import jax.numpy as jnp
from jax import lax
from jax.experimental import pallas as pl
from jax.experimental.pallas import tpu as pltpu
from jax.sharding import PartitionSpec as P

MAXS = 60
LANES = 128
HALF = 64
CHUNK = 256
VMEM_LIMIT = 48 * 1024 * 1024
F32 = jnp.float32
BF16 = jnp.bfloat16


def params():
    return pltpu.CompilerParams(vmem_limit_bytes=VMEM_LIMIT)


def whole(shape):
    return pl.BlockSpec(shape, lambda *_: (0,) * len(shape))


def lane_roll(x):
    return pltpu.roll(x.astype(F32), HALF, 1).astype(x.dtype)


def swap_pairs(count, first):
    pairs = []
    for i in range(first, count - 1, 2):
        pairs += [(i, i + 1), (i + 1, i)]
    return pairs


def shifted_rows(row, lead, width):
    taps = row.shape[1]
    padded = jnp.concatenate([row, jnp.zeros((1, width - taps), F32)], axis=1)
    return pltpu.roll(
        jnp.broadcast_to(padded, (LANES, width)), lead, 1, stride=1, stride_axis=0
    )


def build_kernel(shift_ref, range_ref, taps_ref, azimuth_ref, w_ref, m_ref, a_ref):
    depth = w_ref.shape[0] // 2
    real = shifted_rows(range_ref[0:1, :].astype(F32), HALF, depth)
    imag = shifted_rows(range_ref[1:2, :].astype(F32), HALF, depth)
    real_t, imag_t = real.T.astype(BF16), imag.T.astype(BF16)
    w_ref[0:depth, 0:LANES] = real_t
    w_ref[0:depth, LANES:] = -imag_t
    w_ref[depth:, 0:LANES] = imag_t
    w_ref[depth:, LANES:] = real_t

    span = m_ref.shape[1]
    blocks = m_ref.shape[0]
    cells = taps_ref.shape[1]
    tap_count = taps_ref.shape[0]
    first = lax.axis_index("rg") * cells - HALF
    total = lax.axis_size("rg") * cells
    for b in range(blocks):
        source = lax.broadcasted_iota(jnp.int32, (span, LANES), 0)
        column = lax.broadcasted_iota(jnp.int32, (span, LANES), 1)
        tap = source - column - (HALF - tap_count // 2) - shift_ref[b]
        place = source + first + b * LANES
        tap = jnp.where((place >= 0) & (place < total), tap, -1)
        matrix = jnp.zeros((span, LANES), F32)
        for k in range(tap_count):
            row = taps_ref[k : k + 1, b * LANES : (b + 1) * LANES].astype(F32)
            matrix = jnp.where(tap == k, row, matrix)
        m_ref[b] = matrix.astype(BF16)

    steps, depth = a_ref.shape[0], a_ref.shape[3]
    gap = jnp.zeros((LANES, LANES), BF16)
    for b in range(blocks):
        for part in range(2):
            row = azimuth_ref[b, part : part + 1, :].astype(F32)
            rows = shifted_rows(row, 0, steps * depth - LANES).astype(BF16)
            upper = jnp.concatenate([rows, gap], axis=1)
            lower = jnp.concatenate([gap, rows], axis=1)
            base = part * CHUNK
            for k in range(steps):
                a_ref[k, b, base : base + LANES] = upper[:, k * depth : (k + 1) * depth]
                a_ref[k, b, base + LANES : base + CHUNK] = lower[:, k * depth : (k + 1) * depth]


def build(block_shift, range_chirp, migration_taps, azimuth_chirp):
    blocks = block_shift.shape[0]
    depth = range_chirp.shape[1] + 2 * LANES
    steps = (azimuth_chirp.shape[2] + CHUNK) // CHUNK
    return pl.pallas_call(
        build_kernel,
        out_shape=(
            jax.ShapeDtypeStruct((2 * depth, 2 * LANES), BF16),
            jax.ShapeDtypeStruct((blocks, 2 * LANES, LANES), BF16),
            jax.ShapeDtypeStruct((steps, blocks, 2 * CHUNK, CHUNK), BF16),
        ),
        in_specs=[pl.BlockSpec(memory_space=pltpu.SMEM)]
        + [pl.BlockSpec(memory_space=pltpu.VMEM)] * 3,
        out_specs=(pl.BlockSpec(memory_space=pltpu.VMEM),) * 3,
        compiler_params=params(),
        name="build_weights",
    )(block_shift, range_chirp, migration_taps, azimuth_chirp)


def write_edge(out_ref, at_chunk, x_ref, start, side):
    rows = CHUNK
    last = x_ref.shape[2] // LANES - 1
    low = lax.broadcasted_iota(jnp.int32, (rows // 2, LANES), 1) < HALF
    picked = pl.ds(start, rows)
    at = 0
    for part in range(2):
        for tile in ((0, 1) if side == 0 else (last - 1, last)):
            out_ref[at_chunk, at : at + rows, :] = x_ref[
                part, picked, tile * LANES : (tile + 1) * LANES
            ]
            at += rows
    for part in range(2):
        tile = 2 if side == 0 else last - 2
        cells = x_ref[part, picked, tile * LANES : (tile + 1) * LANES].astype(F32)
        top, bottom = cells[: rows // 2], cells[rows // 2 :]
        if side == 0:
            packed = jnp.where(low, top, pltpu.roll(bottom, HALF, 1))
        else:
            packed = jnp.where(low, pltpu.roll(top, HALF, 1), bottom)
        out_ref[at_chunk, at : at + rows // 2, :] = packed.astype(BF16)
        at += rows // 2


def near_away_rows(rows):
    odd = lax.rem(lax.axis_index("az"), 2)
    last = rows - CHUNK
    near = pl.multiple_of((1 - odd) * last, CHUNK)
    away = pl.multiple_of(odd * last, CHUNK)
    return near, away


def edges_kernel(x_ref, far_near_ref, far_away_ref, far_mid_ref, core_near_ref, core_rest_ref):
    rows = x_ref.shape[1]
    near, away = near_away_rows(rows)
    mids = range(CHUNK, rows - CHUNK, CHUNK)

    def write(core_side):
        far_side = 1 - core_side
        write_edge(far_near_ref, 0, x_ref, near, far_side)
        write_edge(core_near_ref, 0, x_ref, near, core_side)
        write_edge(far_away_ref, 0, x_ref, away, far_side)
        write_edge(core_rest_ref, 0, x_ref, away, core_side)
        for i, start in enumerate(mids):
            write_edge(far_mid_ref, i, x_ref, start, far_side)
            write_edge(core_rest_ref, i + 1, x_ref, start, core_side)

    odd = lax.rem(lax.axis_index("rg"), 2)

    @pl.when(odd == 0)
    def _():
        write(1)

    @pl.when(odd == 1)
    def _():
        write(0)


def range_edges(raw):
    mids = raw.shape[1] // CHUNK - 2
    counts = (1, 1, mids, 1, 1 + mids)
    return pl.pallas_call(
        edges_kernel,
        out_shape=tuple(jax.ShapeDtypeStruct((n, 5 * CHUNK, LANES), BF16) for n in counts),
        in_specs=[pl.BlockSpec(memory_space=pltpu.VMEM)],
        out_specs=(pl.BlockSpec(memory_space=pltpu.VMEM),) * len(counts),
        compiler_params=params(),
        name="range_edges",
    )(raw)


def read_edge(wide_ref, in_ref, at_chunk, side, last):
    rows = CHUNK
    at = 0
    for part in range(2):
        for tile in ((1, 2) if side == 0 else (last - 2, last - 1)):
            wide_ref[part, :, tile * LANES : (tile + 1) * LANES] = in_ref[
                at_chunk, at : at + rows, :
            ]
            at += rows
    for part in range(2):
        packed = in_ref[at_chunk, at : at + rows // 2, :]
        rolled = lane_roll(packed)
        top, bottom = (rolled, packed) if side == 0 else (packed, rolled)
        lanes = slice(0, LANES) if side == 0 else slice(last * LANES, (last + 1) * LANES)
        wide_ref[part, : rows // 2, lanes] = top
        wide_ref[part, rows // 2 :, lanes] = bottom
        at += rows // 2


def compress_chunk(x_ref, start, core, far, w_ref, m_ref, out_ref, out_start, wide_ref, c_ref):
    rows, cells = CHUNK, x_ref.shape[2]
    last = wide_ref.shape[2] // LANES - 1
    depth = w_ref.shape[0] // 2
    odd = lax.rem(lax.axis_index("rg"), 2)

    @pl.when(odd == 0)
    def _():
        read_edge(wide_ref, *far, 0, last)
        read_edge(wide_ref, *core, 1, last)

    @pl.when(odd == 1)
    def _():
        read_edge(wide_ref, *core, 0, last)
        read_edge(wide_ref, *far, 1, last)

    wide_ref[:, :, 3 * LANES : 3 * LANES + cells] = x_ref[:, pl.ds(start, rows), :]
    for j in range(c_ref.shape[1] // LANES):
        lanes = slice(j * LANES, j * LANES + depth)
        window = jnp.concatenate([wide_ref[0, :, lanes], wide_ref[1, :, lanes]], axis=1)
        result = jnp.dot(window, w_ref[...], preferred_element_type=F32).astype(BF16)
        c_ref[0:rows, j * LANES : (j + 1) * LANES] = result[:, :LANES]
        c_ref[rows:, j * LANES : (j + 1) * LANES] = result[:, LANES:]
    for b in range(m_ref.shape[0]):
        window = c_ref[:, b * LANES : b * LANES + 2 * LANES]
        result = jnp.dot(window, m_ref[b], preferred_element_type=F32).astype(BF16)
        lanes = slice(b * LANES, (b + 1) * LANES)
        out_ref[0, out_start : out_start + rows, lanes] = result[:rows]
        out_ref[1, out_start : out_start + rows, lanes] = result[rows:]


def compress_kernel(which, x_ref, core_ref, far_ref, w_ref, m_ref, out_ref, wide_ref, c_ref):
    near, away = near_away_rows(x_ref.shape[1])
    if which == "mid":
        starts = [CHUNK * (i + 1) for i in range(out_ref.shape[1] // CHUNK)]
    else:
        starts = [near if which == "near" else away]
    skip = 1 if which == "mid" else 0
    for i, start in enumerate(starts):
        compress_chunk(
            x_ref, start, (core_ref, i + skip), (far_ref, i), w_ref, m_ref,
            out_ref, i * CHUNK, wide_ref, c_ref,
        )


def compress(which, raw, core, far, w, m):
    rows, cells = raw.shape[1], raw.shape[2]
    count = far.shape[0] * CHUNK
    flops = count * 2 * LANES * (
        2 * w.shape[0] * (cells // LANES + 1) + 8 * LANES * m.shape[0]
    )
    return pl.pallas_call(
        functools.partial(compress_kernel, which),
        out_shape=jax.ShapeDtypeStruct((2, count, cells), BF16),
        in_specs=[pl.BlockSpec(memory_space=pltpu.VMEM)] * 5,
        out_specs=pl.BlockSpec(memory_space=pltpu.VMEM),
        scratch_shapes=[
            pltpu.VMEM((2, CHUNK, cells + 6 * LANES), BF16),
            pltpu.VMEM((2 * CHUNK, cells + LANES), BF16),
        ],
        cost_estimate=pl.CostEstimate(
            flops=flops, bytes_accessed=count * cells * 16, transcendentals=0
        ),
        compiler_params=params(),
        name="compress_" + which,
    )(raw, core, far, w, m)


def correlate_block(a_ref, b, pairs):
    lanes = slice(b * LANES, (b + 1) * LANES)
    taps = [a_ref[k, b] for k, _ in pairs]
    lines = [
        jnp.concatenate([window(0, lanes), window(1, lanes)], axis=1) for _, window in pairs
    ]
    result = jnp.dot(
        jnp.concatenate(taps, axis=1), jnp.concatenate(lines, axis=0), preferred_element_type=F32
    )
    top, bottom = result[:CHUNK], result[CHUNK:]
    return top[:, :LANES] + bottom[:, LANES:], top[:, LANES:] - bottom[:, :LANES]


def focus_own_kernel(a_ref, near_ref, mid_ref, away_ref, image_ref, part_ref, seq_ref):
    step = pl.program_id(0)
    rows = seq_ref.shape[1]
    chunks = rows // CHUNK
    blocks, steps = a_ref.shape[1], a_ref.shape[0]

    @pl.when(step == 0)
    def _():
        near, away = near_away_rows(rows)
        seq_ref[:, pl.ds(near, CHUNK), :] = near_ref[...]
        seq_ref[:, pl.ds(away, CHUNK), :] = away_ref[...]
        seq_ref[:, CHUNK : rows - CHUNK, :] = mid_ref[...]

    def lines(chunk):
        start = pl.multiple_of(chunk * CHUNK, CHUNK)
        return lambda part, lanes: seq_ref[part, pl.ds(start, CHUNK), lanes]

    for b in range(blocks):
        lanes = slice(b * LANES, (b + 1) * LANES)
        real, imag = correlate_block(
            a_ref, b, [(k, lines(step + k)) for k in range(steps)]
        )
        image_ref[0, :, lanes] = real
        image_ref[1, :, lanes] = imag

    @pl.when(step == chunks - 3)
    def _():
        for end in range(2):
            base = 0 if end == 0 else chunks - 2
            for b in range(blocks):
                lanes = slice(b * LANES, (b + 1) * LANES)
                real, imag = correlate_block(
                    a_ref, b, [(1 - end + k, lines(base + k)) for k in range(2)]
                )
                part_ref[end, 0, :, lanes] = real
                part_ref[end, 1, :, lanes] = imag


def focus_own(a, near, mid, away):
    cells = mid.shape[2]
    rows = mid.shape[1] + 2 * CHUNK
    chunks = rows // CHUNK - 2
    return pl.pallas_call(
        focus_own_kernel,
        grid=(chunks,),
        out_shape=(
            jax.ShapeDtypeStruct((2, rows, cells), F32),
            jax.ShapeDtypeStruct((2, 2, CHUNK, cells), F32),
        ),
        in_specs=[whole(a.shape), whole(near.shape), whole(mid.shape), whole(away.shape)],
        out_specs=(
            pl.BlockSpec((2, CHUNK, cells), lambda g: (0, g + 1, 0)),
            whole((2, 2, CHUNK, cells)),
        ),
        scratch_shapes=[pltpu.VMEM((2, rows, cells), BF16)],
        cost_estimate=pl.CostEstimate(
            flops=2 * chunks * a.size * 4 * LANES,
            bytes_accessed=2 * (a.size + mid.size) + 8 * chunks * CHUNK * cells,
            transcendentals=0,
        ),
        compiler_params=params(),
        name="focus_own",
    )(a, near, mid, away)


def focus_end_kernel(which, a_ref, part_ref, halo_ref, _, image_ref, sum_ref, sem):
    near, away = near_away_rows(image_ref.shape[1])
    odd = lax.rem(lax.axis_index("az"), 2)
    after = 1 - odd if which == "near" else odd
    start = near if which == "near" else away
    for b in range(a_ref.shape[1]):
        lanes = slice(b * LANES, (b + 1) * LANES)
        real, imag = correlate_block(
            a_ref, b, [(2 * after, lambda part, at: halo_ref[part, :, at])]
        )
        sum_ref[0, :, lanes] = part_ref[after, 0, :, lanes] + real
        sum_ref[1, :, lanes] = part_ref[after, 1, :, lanes] + imag
    copy = pltpu.make_async_copy(sum_ref, image_ref.at[:, pl.ds(start, CHUNK), :], sem)
    copy.start()
    copy.wait()


def focus_end(which, a, part, halo, image):
    cells = halo.shape[2]
    return pl.pallas_call(
        functools.partial(focus_end_kernel, which),
        out_shape=jax.ShapeDtypeStruct(image.shape, F32),
        in_specs=[pl.BlockSpec(memory_space=pltpu.VMEM)] * 3
        + [pl.BlockSpec(memory_space=pl.ANY)],
        out_specs=pl.BlockSpec(memory_space=pl.ANY),
        scratch_shapes=[pltpu.VMEM((2, CHUNK, cells), F32), pltpu.SemaphoreType.DMA],
        input_output_aliases={3: 0},
        cost_estimate=pl.CostEstimate(
            flops=a.size * 2 * LANES, bytes_accessed=8 * CHUNK * cells, transcendentals=0
        ),
        compiler_params=params(),
        name="focus_" + which,
    )(a, part, halo, image)


def per_device(raw_echo, range_chirp, migration_taps, block_shift, azimuth_chirp):
    rg_count, az_count = lax.axis_size("rg"), lax.axis_size("az")
    rg_near, rg_far = swap_pairs(rg_count, 0), swap_pairs(rg_count, 1)
    az_near, az_far = swap_pairs(az_count, 0), swap_pairs(az_count, 1)

    far_near, far_away, far_mid, core_near, core_rest = range_edges(raw_echo)
    far_near = lax.ppermute(far_near, "rg", rg_far)
    core_near = lax.ppermute(core_near, "rg", rg_near)
    core_rest = lax.ppermute(core_rest, "rg", rg_near)
    far_away = lax.ppermute(far_away, "rg", rg_far)
    w, m, a = build(block_shift, range_chirp, migration_taps, azimuth_chirp)
    near = compress("near", raw_echo, core_near, far_near, w, m)
    near_halo = lax.ppermute(near, "az", az_near)
    far_mid, near = lax.optimization_barrier((far_mid, near))
    far_mid = lax.ppermute(far_mid, "rg", rg_far)
    away = compress("away", raw_echo, core_rest, far_away, w, m)
    away_halo = lax.ppermute(away, "az", az_far)
    mid = compress("mid", raw_echo, core_rest, far_mid, w, m)
    image, part = focus_own(a, near, mid, away)
    image = focus_end("near", a, part, near_halo, image)
    return focus_end("away", a, part, away_halo, image)


def solution(mesh):
    placed = (P(None, "az", "rg"), P(), P(None, "rg"), P("rg"), P("rg", None, None))
    return jax.shard_map(
        per_device, mesh=mesh, in_specs=placed, out_specs=P(None, "az", "rg"), check_vma=False
    )
```

```python
import functools

import jax
import jax.numpy as jnp
from jax import lax
from jax.experimental import pallas as pl
from jax.experimental.pallas import tpu as pltpu
from jax.sharding import PartitionSpec as P

MAXS = 60
LANES = 128
HALF = 64
CHUNK = 256
VMEM_LIMIT = 48 * 1024 * 1024
F32 = jnp.float32
BF16 = jnp.bfloat16


def params():
    return pltpu.CompilerParams(vmem_limit_bytes=VMEM_LIMIT)


def whole(shape):
    return pl.BlockSpec(shape, lambda *_: (0,) * len(shape))


def in_hbm(x):
    return pltpu.with_memory_space_constraint(x, pltpu.HBM)


def lane_roll(x):
    return pltpu.roll(x.astype(F32), HALF, 1).astype(x.dtype)


def swap_pairs(count, first):
    pairs = []
    for i in range(first, count - 1, 2):
        pairs += [(i, i + 1), (i + 1, i)]
    return pairs


def shifted_rows(row, lead, width):
    taps = row.shape[1]
    padded = jnp.concatenate([row, jnp.zeros((1, width - taps), F32)], axis=1)
    return pltpu.roll(
        jnp.broadcast_to(padded, (LANES, width)), lead, 1, stride=1, stride_axis=0
    )


def build_kernel(
    shift_hbm, range_hbm, taps_hbm, azimuth_hbm, w_ref, m_ref, a_ref,
    shift_ref, range_ref, taps_ref, azimuth_ref, sems,
):
    copies = [
        pltpu.make_async_copy(source, target, sems.at[i])
        for i, (source, target) in enumerate(
            [
                (range_hbm, range_ref),
                (azimuth_hbm, azimuth_ref),
                (taps_hbm, taps_ref),
                (shift_hbm, shift_ref),
            ]
        )
    ]
    for copy in copies:
        copy.start()
    for copy in copies:
        copy.wait()
    depth = w_ref.shape[0] // 2
    real = shifted_rows(range_ref[0:1, :].astype(F32), HALF, depth)
    imag = shifted_rows(range_ref[1:2, :].astype(F32), HALF, depth)
    real_t, imag_t = real.T.astype(BF16), imag.T.astype(BF16)
    w_ref[0:depth, 0:LANES] = real_t
    w_ref[0:depth, LANES:] = -imag_t
    w_ref[depth:, 0:LANES] = imag_t
    w_ref[depth:, LANES:] = real_t

    span = m_ref.shape[1]
    blocks = m_ref.shape[0]
    cells = taps_ref.shape[1]
    tap_count = taps_ref.shape[0]
    first = lax.axis_index("rg") * cells - HALF
    total = lax.axis_size("rg") * cells
    for b in range(blocks):
        source = lax.broadcasted_iota(jnp.int32, (span, LANES), 0)
        column = lax.broadcasted_iota(jnp.int32, (span, LANES), 1)
        tap = source - column - (HALF - tap_count // 2) - shift_ref[b]
        place = source + first + b * LANES
        tap = jnp.where((place >= 0) & (place < total), tap, -1)
        matrix = jnp.zeros((span, LANES), F32)
        for k in range(tap_count):
            row = taps_ref[k : k + 1, b * LANES : (b + 1) * LANES].astype(F32)
            matrix = jnp.where(tap == k, row, matrix)
        m_ref[b] = matrix.astype(BF16)

    steps, depth = a_ref.shape[0], a_ref.shape[3]
    gap = jnp.zeros((LANES, LANES), BF16)
    for b in range(blocks):
        for part in range(2):
            row = azimuth_ref[b, part : part + 1, :].astype(F32)
            rows = shifted_rows(row, 0, steps * depth - LANES).astype(BF16)
            upper = jnp.concatenate([rows, gap], axis=1)
            lower = jnp.concatenate([gap, rows], axis=1)
            base = part * CHUNK
            for k in range(steps):
                a_ref[k, b, base : base + LANES] = upper[:, k * depth : (k + 1) * depth]
                a_ref[k, b, base + LANES : base + CHUNK] = lower[:, k * depth : (k + 1) * depth]


def build(block_shift, range_chirp, migration_taps, azimuth_chirp):
    blocks = block_shift.shape[0]
    depth = range_chirp.shape[1] + 2 * LANES
    steps = (azimuth_chirp.shape[2] + CHUNK) // CHUNK
    return pl.pallas_call(
        build_kernel,
        out_shape=(
            jax.ShapeDtypeStruct((2 * depth, 2 * LANES), BF16),
            jax.ShapeDtypeStruct((blocks, 2 * LANES, LANES), BF16),
            jax.ShapeDtypeStruct((steps, blocks, 2 * CHUNK, CHUNK), BF16),
        ),
        in_specs=[pl.BlockSpec(memory_space=pltpu.HBM)] * 4,
        out_specs=(pl.BlockSpec(memory_space=pltpu.VMEM),) * 3,
        scratch_shapes=[
            pltpu.SMEM(block_shift.shape, jnp.int32),
            pltpu.VMEM(range_chirp.shape, BF16),
            pltpu.VMEM(migration_taps.shape, BF16),
            pltpu.VMEM(azimuth_chirp.shape, BF16),
            pltpu.SemaphoreType.DMA((4,)),
        ],
        compiler_params=params(),
        name="build_weights",
    )(*(in_hbm(x) for x in (block_shift, range_chirp, migration_taps, azimuth_chirp)))


def write_edge(out_ref, at_chunk, x_ref, start, side):
    rows = CHUNK
    last = x_ref.shape[2] // LANES - 1
    low = lax.broadcasted_iota(jnp.int32, (rows // 2, LANES), 1) < HALF
    picked = pl.ds(start, rows)
    at = 0
    for part in range(2):
        for tile in ((0, 1) if side == 0 else (last - 1, last)):
            out_ref[at_chunk, at : at + rows, :] = x_ref[
                part, picked, tile * LANES : (tile + 1) * LANES
            ]
            at += rows
    for part in range(2):
        tile = 2 if side == 0 else last - 2
        cells = x_ref[part, picked, tile * LANES : (tile + 1) * LANES].astype(F32)
        top, bottom = cells[: rows // 2], cells[rows // 2 :]
        if side == 0:
            packed = jnp.where(low, top, pltpu.roll(bottom, HALF, 1))
        else:
            packed = jnp.where(low, pltpu.roll(top, HALF, 1), bottom)
        out_ref[at_chunk, at : at + rows // 2, :] = packed.astype(BF16)
        at += rows // 2


def near_away_rows(rows):
    odd = lax.rem(lax.axis_index("az"), 2)
    last = rows - CHUNK
    near = pl.multiple_of((1 - odd) * last, CHUNK)
    away = pl.multiple_of(odd * last, CHUNK)
    return near, away


def edges_kernel(x_hbm, x_ref, far_outer_ref, far_mid_ref, core_ref, sems):
    rows = x_ref.shape[1]
    near, away = near_away_rows(rows)
    pieces = [(near, CHUNK), (away, CHUNK), (CHUNK, rows - 2 * CHUNK)]
    copies = []
    for i, (start, size) in enumerate(pieces):
        picked = pl.ds(start, size)
        copies.append(
            pltpu.make_async_copy(x_hbm.at[:, picked, :], x_ref.at[:, picked, :], sems.at[i])
        )
        copies[-1].start()
    starts = [near, away] + list(range(CHUNK, rows - CHUNK, CHUNK))
    odd = lax.rem(lax.axis_index("rg"), 2)
    for i, start in enumerate(starts):
        if i < 3:
            copies[i].wait()
        far_ref, at_chunk = (far_outer_ref, i) if i < 2 else (far_mid_ref, i - 2)

        def write(core_side):
            write_edge(core_ref, i, x_ref, start, core_side)
            write_edge(far_ref, at_chunk, x_ref, start, 1 - core_side)

        pl.when(odd == 0)(lambda: write(1))
        pl.when(odd == 1)(lambda: write(0))


def range_edges(raw):
    chunks = raw.shape[1] // CHUNK
    return pl.pallas_call(
        edges_kernel,
        out_shape=(jax.ShapeDtypeStruct(raw.shape, BF16),)
        + tuple(
            jax.ShapeDtypeStruct((n, 5 * CHUNK, LANES), BF16) for n in (2, chunks - 2, chunks)
        ),
        in_specs=[pl.BlockSpec(memory_space=pltpu.HBM)],
        out_specs=(pl.BlockSpec(memory_space=pltpu.VMEM),) * 4,
        scratch_shapes=[pltpu.SemaphoreType.DMA((3,))],
        compiler_params=params(),
        name="range_edges",
    )(in_hbm(raw))


def read_edge(wide_ref, in_ref, at_chunk, side, last):
    rows = CHUNK
    at = 0
    for part in range(2):
        for tile in ((1, 2) if side == 0 else (last - 2, last - 1)):
            wide_ref[part, :, tile * LANES : (tile + 1) * LANES] = in_ref[
                at_chunk, at : at + rows, :
            ]
            at += rows
    for part in range(2):
        packed = in_ref[at_chunk, at : at + rows // 2, :]
        rolled = lane_roll(packed)
        top, bottom = (rolled, packed) if side == 0 else (packed, rolled)
        lanes = slice(0, LANES) if side == 0 else slice(last * LANES, (last + 1) * LANES)
        wide_ref[part, : rows // 2, lanes] = top
        wide_ref[part, rows // 2 :, lanes] = bottom
        at += rows // 2


def compress_chunk(x_ref, start, core, far, w_ref, m_ref, out_ref, out_start, wide_ref, c_ref):
    rows, cells = CHUNK, x_ref.shape[2]
    last = wide_ref.shape[2] // LANES - 1
    depth = w_ref.shape[0] // 2
    odd = lax.rem(lax.axis_index("rg"), 2)

    @pl.when(odd == 0)
    def _():
        read_edge(wide_ref, *far, 0, last)
        read_edge(wide_ref, *core, 1, last)

    @pl.when(odd == 1)
    def _():
        read_edge(wide_ref, *core, 0, last)
        read_edge(wide_ref, *far, 1, last)

    wide_ref[:, :, 3 * LANES : 3 * LANES + cells] = x_ref[:, pl.ds(start, rows), :]
    for j in range(c_ref.shape[1] // LANES):
        lanes = slice(j * LANES, j * LANES + depth)
        window = jnp.concatenate([wide_ref[0, :, lanes], wide_ref[1, :, lanes]], axis=1)
        result = jnp.dot(window, w_ref[...], preferred_element_type=F32).astype(BF16)
        c_ref[0:rows, j * LANES : (j + 1) * LANES] = result[:, :LANES]
        c_ref[rows:, j * LANES : (j + 1) * LANES] = result[:, LANES:]
    for b in range(m_ref.shape[0]):
        window = c_ref[:, b * LANES : b * LANES + 2 * LANES]
        result = jnp.dot(window, m_ref[b], preferred_element_type=F32).astype(BF16)
        lanes = slice(b * LANES, (b + 1) * LANES)
        out_ref[0, out_start : out_start + rows, lanes] = result[:rows]
        out_ref[1, out_start : out_start + rows, lanes] = result[rows:]


def compress_kernel(which, x_ref, core_ref, far_ref, w_ref, m_ref, out_ref, wide_ref, c_ref):
    near, away = near_away_rows(x_ref.shape[1])
    if which == "mid":
        jobs = [(CHUNK * (i + 1), i + 2, i) for i in range(out_ref.shape[1] // CHUNK)]
    else:
        jobs = [(near, 0, 0) if which == "near" else (away, 1, 1)]
    for i, (start, core_chunk, far_chunk) in enumerate(jobs):
        compress_chunk(
            x_ref, start, (core_ref, core_chunk), (far_ref, far_chunk), w_ref, m_ref,
            out_ref, i * CHUNK, wide_ref, c_ref,
        )


def compress(which, raw, core, far, w, m):
    rows, cells = raw.shape[1], raw.shape[2]
    count = rows - 2 * CHUNK if which == "mid" else CHUNK
    flops = count * 2 * LANES * (
        2 * w.shape[0] * (cells // LANES + 1) + 8 * LANES * m.shape[0]
    )
    return pl.pallas_call(
        functools.partial(compress_kernel, which),
        out_shape=jax.ShapeDtypeStruct((2, count, cells), BF16),
        in_specs=[pl.BlockSpec(memory_space=pltpu.VMEM)] * 5,
        out_specs=pl.BlockSpec(memory_space=pltpu.VMEM),
        scratch_shapes=[
            pltpu.VMEM((2, CHUNK, cells + 6 * LANES), BF16),
            pltpu.VMEM((2 * CHUNK, cells + LANES), BF16),
        ],
        cost_estimate=pl.CostEstimate(
            flops=flops, bytes_accessed=count * cells * 16, transcendentals=0
        ),
        compiler_params=params(),
        name="compress_" + which,
    )(raw, core, far, w, m)


def correlate_block(a_ref, b, pairs):
    lanes = slice(b * LANES, (b + 1) * LANES)
    taps = [a_ref[k, b] for k, _ in pairs]
    lines = [
        jnp.concatenate([window(0, lanes), window(1, lanes)], axis=1) for _, window in pairs
    ]
    result = jnp.dot(
        jnp.concatenate(taps, axis=1), jnp.concatenate(lines, axis=0), preferred_element_type=F32
    )
    top, bottom = result[:CHUNK], result[CHUNK:]
    return top[:, :LANES] + bottom[:, LANES:], top[:, LANES:] - bottom[:, :LANES]


def focus_own_kernel(a_ref, near_ref, mid_ref, away_ref, image_ref, part_ref, seq_ref):
    step = pl.program_id(0)
    rows = seq_ref.shape[1]
    chunks = rows // CHUNK
    blocks, steps = a_ref.shape[1], a_ref.shape[0]

    @pl.when(step == 0)
    def _():
        near, away = near_away_rows(rows)
        seq_ref[:, pl.ds(near, CHUNK), :] = near_ref[...]
        seq_ref[:, pl.ds(away, CHUNK), :] = away_ref[...]
        seq_ref[:, CHUNK : rows - CHUNK, :] = mid_ref[...]

    def lines(chunk):
        start = pl.multiple_of(chunk * CHUNK, CHUNK)
        return lambda part, lanes: seq_ref[part, pl.ds(start, CHUNK), lanes]

    for b in range(blocks):
        lanes = slice(b * LANES, (b + 1) * LANES)
        real, imag = correlate_block(
            a_ref, b, [(k, lines(step + k)) for k in range(steps)]
        )
        image_ref[0, :, lanes] = real
        image_ref[1, :, lanes] = imag

    @pl.when(step == chunks - 3)
    def _():
        for end in range(2):
            base = 0 if end == 0 else chunks - 2
            for b in range(blocks):
                lanes = slice(b * LANES, (b + 1) * LANES)
                real, imag = correlate_block(
                    a_ref, b, [(1 - end + k, lines(base + k)) for k in range(2)]
                )
                part_ref[end, 0, :, lanes] = real
                part_ref[end, 1, :, lanes] = imag


def focus_own(a, near, mid, away):
    cells = mid.shape[2]
    rows = mid.shape[1] + 2 * CHUNK
    chunks = rows // CHUNK - 2
    return pl.pallas_call(
        focus_own_kernel,
        grid=(chunks,),
        out_shape=(
            jax.ShapeDtypeStruct((2, rows, cells), F32),
            jax.ShapeDtypeStruct((2, 2, CHUNK, cells), F32),
        ),
        in_specs=[whole(a.shape), whole(near.shape), whole(mid.shape), whole(away.shape)],
        out_specs=(
            pl.BlockSpec((2, CHUNK, cells), lambda g: (0, g + 1, 0)),
            whole((2, 2, CHUNK, cells)),
        ),
        scratch_shapes=[pltpu.VMEM((2, rows, cells), BF16)],
        cost_estimate=pl.CostEstimate(
            flops=2 * chunks * a.size * 4 * LANES,
            bytes_accessed=2 * (a.size + mid.size) + 8 * chunks * CHUNK * cells,
            transcendentals=0,
        ),
        compiler_params=params(),
        name="focus_own",
    )(a, near, mid, away)


def focus_end_kernel(which, a_ref, part_ref, halo_ref, _, image_ref, sum_ref, sem):
    near, away = near_away_rows(image_ref.shape[1])
    odd = lax.rem(lax.axis_index("az"), 2)
    after = 1 - odd if which == "near" else odd
    start = near if which == "near" else away
    for b in range(a_ref.shape[1]):
        lanes = slice(b * LANES, (b + 1) * LANES)
        real, imag = correlate_block(
            a_ref, b, [(2 * after, lambda part, at: halo_ref[part, :, at])]
        )
        sum_ref[0, :, lanes] = part_ref[after, 0, :, lanes] + real
        sum_ref[1, :, lanes] = part_ref[after, 1, :, lanes] + imag
    copy = pltpu.make_async_copy(sum_ref, image_ref.at[:, pl.ds(start, CHUNK), :], sem)
    copy.start()
    copy.wait()


def focus_end(which, a, part, halo, image):
    cells = halo.shape[2]
    return pl.pallas_call(
        functools.partial(focus_end_kernel, which),
        out_shape=jax.ShapeDtypeStruct(image.shape, F32),
        in_specs=[pl.BlockSpec(memory_space=pltpu.VMEM)] * 3
        + [pl.BlockSpec(memory_space=pl.ANY)],
        out_specs=pl.BlockSpec(memory_space=pl.ANY),
        scratch_shapes=[pltpu.VMEM((2, CHUNK, cells), F32), pltpu.SemaphoreType.DMA],
        input_output_aliases={3: 0},
        cost_estimate=pl.CostEstimate(
            flops=a.size * 2 * LANES, bytes_accessed=8 * CHUNK * cells, transcendentals=0
        ),
        compiler_params=params(),
        name="focus_" + which,
    )(a, part, halo, image)


def per_device(raw_echo, range_chirp, migration_taps, block_shift, azimuth_chirp):
    rg_count, az_count = lax.axis_size("rg"), lax.axis_size("az")
    rg_near, rg_far = swap_pairs(rg_count, 0), swap_pairs(rg_count, 1)
    az_near, az_far = swap_pairs(az_count, 0), swap_pairs(az_count, 1)

    raw, far_outer, far_mid, core = range_edges(raw_echo)
    core = lax.ppermute(core, "rg", rg_near)
    far_outer = lax.ppermute(far_outer, "rg", rg_far)
    far_mid = lax.ppermute(far_mid, "rg", rg_far)
    w, m, a = build(block_shift, range_chirp, migration_taps, azimuth_chirp)
    near = compress("near", raw, core, far_outer, w, m)
    near_halo = lax.ppermute(near, "az", az_near)
    away = compress("away", raw, core, far_outer, w, m)
    away_halo = lax.ppermute(away, "az", az_far)
    mid = compress("mid", raw, core, far_mid, w, m)
    image, part = focus_own(a, near, mid, away)
    image = focus_end("near", a, part, near_halo, image)
    return focus_end("away", a, part, away_halo, image)


def solution(mesh):
    placed = (P(None, "az", "rg"), P(), P(None, "rg"), P("rg"), P("rg", None, None))
    return jax.shard_map(
        per_device, mesh=mesh, in_specs=placed, out_specs=P(None, "az", "rg"), check_vma=False
    )
```

```python
import functools

import jax
import jax.numpy as jnp
from jax import lax
from jax.experimental import pallas as pl
from jax.experimental.pallas import tpu as pltpu
from jax.sharding import PartitionSpec as P

MAXS = 60
LANES = 128
HALF = 64
CHUNK = 256
VMEM_LIMIT = 48 * 1024 * 1024
F32 = jnp.float32
BF16 = jnp.bfloat16


def params():
    return pltpu.CompilerParams(vmem_limit_bytes=VMEM_LIMIT)


def whole(shape):
    return pl.BlockSpec(shape, lambda *_: (0,) * len(shape))


def in_hbm(x):
    return pltpu.with_memory_space_constraint(x, pltpu.HBM)


def lane_roll(x):
    return pltpu.roll(x.astype(F32), HALF, 1).astype(x.dtype)


def swap_pairs(count, first):
    pairs = []
    for i in range(first, count - 1, 2):
        pairs += [(i, i + 1), (i + 1, i)]
    return pairs


def swap_or_keep(x, axis, first):
    count = lax.axis_size(axis)
    pairs = swap_pairs(count, first)
    paired = {i for i, _ in pairs}
    return lax.ppermute(x, axis, pairs + [(i, i) for i in range(count) if i not in paired])


def shifted_rows(row, lead, width):
    taps = row.shape[1]
    padded = jnp.concatenate([row, jnp.zeros((1, width - taps), F32)], axis=1)
    return pltpu.roll(
        jnp.broadcast_to(padded, (LANES, width)), lead, 1, stride=1, stride_axis=0
    )


def range_weights_kernel(range_ref, taps_ref, shift_hbm, w_ref, m_ref, shift_ref, sem):
    copy = pltpu.make_async_copy(shift_hbm, shift_ref, sem)
    copy.start()
    depth = w_ref.shape[0] // 2
    real = shifted_rows(range_ref[0:1, :].astype(F32), 0, depth)
    imag = shifted_rows(range_ref[1:2, :].astype(F32), 0, depth)
    real_t, imag_t = real.T.astype(BF16), imag.T.astype(BF16)
    w_ref[0:depth, 0:LANES] = real_t
    w_ref[0:depth, LANES:] = -imag_t
    w_ref[depth:, 0:LANES] = imag_t
    w_ref[depth:, LANES:] = real_t

    span = m_ref.shape[1]
    blocks = m_ref.shape[0]
    cells = taps_ref.shape[1]
    tap_count = taps_ref.shape[0]
    first = lax.axis_index("rg") * cells - HALF
    total = lax.axis_size("rg") * cells
    copy.wait()
    for b in range(blocks):
        source = lax.broadcasted_iota(jnp.int32, (span, LANES), 0)
        column = lax.broadcasted_iota(jnp.int32, (span, LANES), 1)
        tap = source - column - (HALF - tap_count // 2) - shift_ref[b]
        place = source + first + b * LANES
        tap = jnp.where((place >= 0) & (place < total), tap, -1)
        matrix = jnp.zeros((span, LANES), F32)
        for k in range(tap_count):
            row = taps_ref[k : k + 1, b * LANES : (b + 1) * LANES].astype(F32)
            matrix = jnp.where(tap == k, row, matrix)
        m_ref[b] = matrix.astype(BF16)


def range_weights(range_chirp, migration_taps, block_shift):
    blocks = block_shift.shape[0]
    depth = range_chirp.shape[1] + LANES
    return pl.pallas_call(
        range_weights_kernel,
        out_shape=(
            jax.ShapeDtypeStruct((2 * depth, 2 * LANES), BF16),
            jax.ShapeDtypeStruct((blocks, 2 * LANES, LANES), BF16),
        ),
        in_specs=[pl.BlockSpec(memory_space=pltpu.VMEM)] * 2
        + [pl.BlockSpec(memory_space=pltpu.HBM)],
        out_specs=(pl.BlockSpec(memory_space=pltpu.VMEM),) * 2,
        scratch_shapes=[pltpu.SMEM(block_shift.shape, jnp.int32), pltpu.SemaphoreType.DMA],
        compiler_params=params(),
        name="range_weights",
    )(range_chirp, migration_taps, in_hbm(block_shift))


def azimuth_weights_kernel(azimuth_ref, a_ref):
    steps, blocks, depth = a_ref.shape[0], a_ref.shape[1], a_ref.shape[3]
    gap = jnp.zeros((LANES, LANES), BF16)
    for b in range(blocks):
        for part in range(2):
            row = azimuth_ref[b, part : part + 1, :].astype(F32)
            rows = shifted_rows(row, 0, steps * depth - LANES).astype(BF16)
            upper = jnp.concatenate([rows, gap], axis=1)
            lower = jnp.concatenate([gap, rows], axis=1)
            base = part * CHUNK
            for k in range(steps):
                a_ref[k, b, base : base + LANES] = upper[:, k * depth : (k + 1) * depth]
                a_ref[k, b, base + LANES : base + CHUNK] = lower[:, k * depth : (k + 1) * depth]


def azimuth_weights(azimuth_chirp):
    blocks = azimuth_chirp.shape[0]
    steps = (azimuth_chirp.shape[2] + CHUNK) // CHUNK
    return pl.pallas_call(
        azimuth_weights_kernel,
        out_shape=jax.ShapeDtypeStruct((steps, blocks, 2 * CHUNK, CHUNK), BF16),
        in_specs=[pl.BlockSpec(memory_space=pltpu.VMEM)],
        out_specs=pl.BlockSpec(memory_space=pltpu.VMEM),
        compiler_params=params(),
        name="azimuth_weights",
    )(azimuth_chirp)


def pack_halves(out_ref, at_chunk, at, tile, side):
    rows = tile.shape[0]
    low = lax.broadcasted_iota(jnp.int32, (rows // 2, LANES), 1) < HALF
    top, bottom = tile[: rows // 2], tile[rows // 2 :]
    if side == 0:
        packed = jnp.where(low, pltpu.roll(top, HALF, 1), bottom)
    else:
        packed = jnp.where(low, top, pltpu.roll(bottom, HALF, 1))
    out_ref[at_chunk, at : at + rows // 2, :] = packed.astype(BF16)


def shift_chunk(x_ref, s_ref, start):
    picked = pl.ds(start, CHUNK)
    low = lax.broadcasted_iota(jnp.int32, (CHUNK, LANES), 1) < HALF
    for part in range(2):
        before = None
        for tile in range(x_ref.shape[2] // LANES):
            cells = x_ref[part, picked, tile * LANES : (tile + 1) * LANES].astype(F32)
            rolled = pltpu.roll(cells, HALF, 1)
            joined = rolled if before is None else jnp.where(low, before, rolled)
            s_ref[part, picked, tile * LANES : (tile + 1) * LANES] = joined.astype(BF16)
            before = rolled
        s_ref[part, picked, x_ref.shape[2] :] = before.astype(BF16)


def write_edge(out_ref, at_chunk, s_ref, start, side):
    last = s_ref.shape[2] // LANES - 1
    picked = pl.ds(start, CHUNK)
    at = 0
    for part in range(2):
        for tile in ((1, 2) if side == 0 else (last - 2, last - 1)):
            out_ref[at_chunk, at : at + CHUNK, :] = s_ref[
                part, picked, tile * LANES : (tile + 1) * LANES
            ]
            at += CHUNK
    for part in range(2):
        tile = 0 if side == 0 else last
        cells = s_ref[part, picked, tile * LANES : (tile + 1) * LANES].astype(F32)
        pack_halves(out_ref, at_chunk, at, cells, side)
        at += CHUNK // 2


def near_away_rows(rows):
    odd = lax.rem(lax.axis_index("az"), 2)
    last = rows - CHUNK
    near = pl.multiple_of((1 - odd) * last, CHUNK)
    away = pl.multiple_of(odd * last, CHUNK)
    return near, away


def edges_kernel(
    x_hbm, range_hbm, taps_hbm, azimuth_hbm,
    s_ref, far_near_ref, far_away_ref, far_mid_ref, core_ref, range_ref, taps_ref, azimuth_ref,
    x_ref, sems,
):
    rows = x_ref.shape[1]
    near, away = near_away_rows(rows)
    starts = [near, away] + list(range(CHUNK, rows - CHUNK, CHUNK))
    moves = []
    for start in starts:
        picked = pl.ds(start, CHUNK)
        moves.append((x_hbm.at[:, picked, :], x_ref.at[:, picked, :]))
    moves += [(range_hbm, range_ref), (taps_hbm, taps_ref), (azimuth_hbm, azimuth_ref)]
    copies = [
        pltpu.make_async_copy(source, target, sems.at[i])
        for i, (source, target) in enumerate(moves)
    ]
    for copy in copies:
        copy.start()
    odd = lax.rem(lax.axis_index("rg"), 2)
    for i, start in enumerate(starts):
        copies[i].wait()
        shift_chunk(x_ref, s_ref, start)
        far_ref, at_chunk = [(far_near_ref, 0), (far_away_ref, 0)][i] if i < 2 else (
            far_mid_ref, i - 2
        )

        def write(core_side):
            write_edge(core_ref, i, s_ref, start, core_side)
            write_edge(far_ref, at_chunk, s_ref, start, 1 - core_side)

        pl.when(odd == 0)(lambda: write(1))
        pl.when(odd == 1)(lambda: write(0))
    for copy in copies[len(starts) :]:
        copy.wait()


def range_edges(raw, range_chirp, migration_taps, azimuth_chirp):
    chunks = raw.shape[1] // CHUNK
    small = (range_chirp, migration_taps, azimuth_chirp)
    return pl.pallas_call(
        edges_kernel,
        out_shape=(jax.ShapeDtypeStruct(raw.shape[:2] + (raw.shape[2] + LANES,), BF16),)
        + tuple(
            jax.ShapeDtypeStruct((n, 5 * CHUNK, LANES), BF16) for n in (1, 1, chunks - 2, chunks)
        )
        + tuple(jax.ShapeDtypeStruct(x.shape, x.dtype) for x in small),
        in_specs=[pl.BlockSpec(memory_space=pltpu.HBM)] * 4,
        out_specs=(pl.BlockSpec(memory_space=pltpu.VMEM),) * 8,
        scratch_shapes=[
            pltpu.VMEM(raw.shape, BF16),
            pltpu.SemaphoreType.DMA((chunks + len(small),)),
        ],
        compiler_params=params(),
        name="range_edges",
    )(*(in_hbm(x) for x in (raw,) + small))


def place_half(wide_ref, tile, packed, own, side):
    rows = own.shape[1] if own.ndim == 3 else own.shape[0]
    low = lax.broadcasted_iota(jnp.int32, (rows, LANES), 1) < HALF
    rolled = pltpu.roll(packed, HALF, 1)
    halo = jnp.concatenate([packed, rolled] if side == 0 else [rolled, packed], axis=0)
    joined = jnp.where(low, halo, own) if side == 0 else jnp.where(low, own, halo)
    return joined.astype(BF16)


def read_edge(wide_ref, s_ref, start, in_ref, at_chunk, side, present):
    rows = CHUNK
    last = wide_ref.shape[2] // LANES - 1
    own_last = s_ref.shape[2] // LANES - 1
    keep = jnp.where(present, 1.0, 0.0)
    at = 0
    for part in range(2):
        for tile in ((0, 1) if side == 0 else (last - 1, last)):
            wide_ref[part, :, tile * LANES : (tile + 1) * LANES] = in_ref[
                at_chunk, at : at + rows, :
            ]
            at += rows
    for part in range(2):
        tile, own_tile = (2, 0) if side == 0 else (last - 2, own_last)
        packed = in_ref[at_chunk, at : at + rows // 2, :].astype(F32) * keep
        own = s_ref[
            part, pl.ds(start, rows), own_tile * LANES : (own_tile + 1) * LANES
        ].astype(F32)
        wide_ref[part, :, tile * LANES : (tile + 1) * LANES] = place_half(
            wide_ref, tile, packed, own, side
        )
        at += rows // 2

    @pl.when(jnp.logical_not(present))
    def _():
        for tile in (0, 1) if side == 0 else (last - 1, last):
            wide_ref[:, :, tile * LANES : (tile + 1) * LANES] = jnp.zeros((2, rows, LANES), BF16)


def compress_chunk(x_ref, start, core, far, w_ref, m_ref, out_ref, out_start, wide_ref, c_ref):
    rows, full = CHUNK, x_ref.shape[2] - 2 * LANES
    depth = w_ref.shape[0] // 2
    index = lax.axis_index("rg")
    odd = lax.rem(index, 2)
    left, right = index > 0, index < lax.axis_size("rg") - 1

    @pl.when(odd == 0)
    def _():
        read_edge(wide_ref, x_ref, start, *far, 0, left)
        read_edge(wide_ref, x_ref, start, *core, 1, right)

    @pl.when(odd == 1)
    def _():
        read_edge(wide_ref, x_ref, start, *core, 0, left)
        read_edge(wide_ref, x_ref, start, *far, 1, right)

    wide_ref[:, :, 3 * LANES : 3 * LANES + full] = x_ref[:, pl.ds(start, rows), LANES : LANES + full]
    for j in range(c_ref.shape[1] // LANES):
        lanes = slice(j * LANES, j * LANES + depth)
        window = jnp.concatenate([wide_ref[0, :, lanes], wide_ref[1, :, lanes]], axis=1)
        result = jnp.dot(window, w_ref[...], preferred_element_type=F32).astype(BF16)
        c_ref[0:rows, j * LANES : (j + 1) * LANES] = result[:, :LANES]
        c_ref[rows:, j * LANES : (j + 1) * LANES] = result[:, LANES:]
    for b in range(m_ref.shape[0]):
        window = c_ref[:, b * LANES : b * LANES + 2 * LANES]
        result = jnp.dot(window, m_ref[b], preferred_element_type=F32).astype(BF16)
        lanes = slice(b * LANES, (b + 1) * LANES)
        out_ref[0, out_start : out_start + rows, lanes] = result[:rows]
        out_ref[1, out_start : out_start + rows, lanes] = result[rows:]


def compress_kernel(which, x_ref, core_ref, far_ref, w_ref, m_ref, out_ref, wide_ref, c_ref):
    near, away = near_away_rows(x_ref.shape[1])
    if which == "mid":
        jobs = [(CHUNK * (i + 1), i + 2, i) for i in range(out_ref.shape[1] // CHUNK)]
    else:
        jobs = [(near, 0, 0) if which == "near" else (away, 1, 0)]
    for i, (start, core_chunk, far_chunk) in enumerate(jobs):
        compress_chunk(
            x_ref, start, (core_ref, core_chunk), (far_ref, far_chunk), w_ref, m_ref,
            out_ref, i * CHUNK, wide_ref, c_ref,
        )


def compress(which, raw, core, far, w, m):
    rows, cells = raw.shape[1], raw.shape[2] - LANES
    count = rows - 2 * CHUNK if which == "mid" else CHUNK
    return pl.pallas_call(
        functools.partial(compress_kernel, which),
        out_shape=jax.ShapeDtypeStruct((2, count, cells), BF16),
        in_specs=[pl.BlockSpec(memory_space=pltpu.VMEM)] * 5,
        out_specs=pl.BlockSpec(memory_space=pltpu.VMEM),
        scratch_shapes=[
            pltpu.VMEM((2, CHUNK, cells + 5 * LANES), BF16),
            pltpu.VMEM((2 * CHUNK, cells + LANES), BF16),
        ],
        compiler_params=params(),
        name="compress_" + which,
    )(raw, core, far, w, m)


def correlate_block(a_ref, b, pairs):
    lanes = slice(b * LANES, (b + 1) * LANES)
    taps = [a_ref[k, b] for k, _ in pairs]
    lines = [
        jnp.concatenate([window(0, lanes), window(1, lanes)], axis=1) for _, window in pairs
    ]
    result = jnp.dot(
        jnp.concatenate(taps, axis=1), jnp.concatenate(lines, axis=0), preferred_element_type=F32
    )
    top, bottom = result[:CHUNK], result[CHUNK:]
    return top[:, :LANES] + bottom[:, LANES:], top[:, LANES:] - bottom[:, :LANES]


def focus_own_kernel(a_ref, near_ref, mid_ref, away_ref, image_ref, part_ref, seq_ref):
    step = pl.program_id(0)
    rows = seq_ref.shape[1]
    chunks = rows // CHUNK
    blocks, steps = a_ref.shape[1], a_ref.shape[0]

    @pl.when(step == 0)
    def _():
        near, away = near_away_rows(rows)
        seq_ref[:, pl.ds(near, CHUNK), :] = near_ref[...]
        seq_ref[:, pl.ds(away, CHUNK), :] = away_ref[...]
        seq_ref[:, CHUNK : rows - CHUNK, :] = mid_ref[...]

    def lines(chunk):
        start = pl.multiple_of(chunk * CHUNK, CHUNK)
        return lambda part, lanes: seq_ref[part, pl.ds(start, CHUNK), lanes]

    for b in range(blocks):
        lanes = slice(b * LANES, (b + 1) * LANES)
        real, imag = correlate_block(
            a_ref, b, [(k, lines(step + k)) for k in range(steps)]
        )
        image_ref[0, :, lanes] = real
        image_ref[1, :, lanes] = imag

    @pl.when(step == chunks - 3)
    def _():
        for end in range(2):
            base = 0 if end == 0 else chunks - 2
            for b in range(blocks):
                lanes = slice(b * LANES, (b + 1) * LANES)
                real, imag = correlate_block(
                    a_ref, b, [(1 - end + k, lines(base + k)) for k in range(2)]
                )
                part_ref[end, 0, :, lanes] = real
                part_ref[end, 1, :, lanes] = imag


def focus_own(a, near, mid, away):
    cells = mid.shape[2]
    rows = mid.shape[1] + 2 * CHUNK
    chunks = rows // CHUNK - 2
    return pl.pallas_call(
        focus_own_kernel,
        grid=(chunks,),
        out_shape=(
            jax.ShapeDtypeStruct((2, rows, cells), F32),
            jax.ShapeDtypeStruct((2, 2, CHUNK, cells), F32),
        ),
        in_specs=[whole(a.shape), whole(near.shape), whole(mid.shape), whole(away.shape)],
        out_specs=(
            pl.BlockSpec((2, CHUNK, cells), lambda g: (0, g + 1, 0)),
            whole((2, 2, CHUNK, cells)),
        ),
        scratch_shapes=[pltpu.VMEM((2, rows, cells), BF16)],
        compiler_params=params(),
        name="focus_own",
    )(a, near, mid, away)


def focus_end_kernel(which, a_ref, part_ref, halo_ref, _, image_ref, sum_ref, sems):
    near, away = near_away_rows(image_ref.shape[1])
    odd = lax.rem(lax.axis_index("az"), 2)
    after = 1 - odd if which == "near" else odd
    start = near if which == "near" else away
    copies = []
    for b in range(a_ref.shape[1]):
        lanes = slice(b * LANES, (b + 1) * LANES)
        real, imag = correlate_block(
            a_ref, b, [(2 * after, lambda part, at: halo_ref[part, :, at])]
        )
        sum_ref[0, :, lanes] = part_ref[after, 0, :, lanes] + real
        sum_ref[1, :, lanes] = part_ref[after, 1, :, lanes] + imag
        copies.append(
            pltpu.make_async_copy(
                sum_ref.at[:, :, lanes], image_ref.at[:, pl.ds(start, CHUNK), lanes], sems.at[b]
            )
        )
        copies[-1].start()
    for copy in copies:
        copy.wait()


def focus_end(which, a, part, halo, image):
    cells = halo.shape[2]
    return pl.pallas_call(
        functools.partial(focus_end_kernel, which),
        out_shape=jax.ShapeDtypeStruct(image.shape, F32),
        in_specs=[pl.BlockSpec(memory_space=pltpu.VMEM)] * 3
        + [pl.BlockSpec(memory_space=pl.ANY)],
        out_specs=pl.BlockSpec(memory_space=pl.ANY),
        scratch_shapes=[pltpu.VMEM((2, CHUNK, cells), F32), pltpu.SemaphoreType.DMA((a.shape[1],))],
        input_output_aliases={3: 0},
        compiler_params=params(),
        name="focus_" + which,
    )(a, part, halo, image)


def per_device(raw_echo, range_chirp, migration_taps, block_shift, azimuth_chirp):
    az_count = lax.axis_size("az")
    raw, far_near, far_away, far_mid, core, range_chirp, migration_taps, azimuth_chirp = range_edges(
        raw_echo, range_chirp, migration_taps, azimuth_chirp
    )
    core = swap_or_keep(core, "rg", 0)
    far_near = swap_or_keep(far_near, "rg", 1)
    far_away = swap_or_keep(far_away, "rg", 1)
    w, m = range_weights(range_chirp, migration_taps, block_shift)
    far_mid, w = lax.optimization_barrier((far_mid, w))
    far_mid = swap_or_keep(far_mid, "rg", 1)
    near = compress("near", raw, core, far_near, w, m)
    near_halo = lax.ppermute(near, "az", swap_pairs(az_count, 0))
    away = compress("away", raw, core, far_away, w, m)
    away_halo = lax.ppermute(away, "az", swap_pairs(az_count, 1))
    away, azimuth_chirp = lax.optimization_barrier((away, azimuth_chirp))
    a = azimuth_weights(azimuth_chirp)
    mid = compress("mid", raw, core, far_mid, w, m)
    image, part = focus_own(a, near, mid, away)
    image = focus_end("near", a, part, near_halo, image)
    return focus_end("away", a, part, away_halo, image)


def solution(mesh):
    placed = (P(None, "az", "rg"), P(), P(None, "rg"), P("rg"), P("rg", None, None))
    return jax.shard_map(
        per_device, mesh=mesh, in_specs=placed, out_specs=P(None, "az", "rg"), check_vma=False
    )
```

```python
import functools

import jax
import jax.numpy as jnp
from jax import lax
from jax.experimental import pallas as pl
from jax.experimental.pallas import tpu as pltpu
from jax.sharding import PartitionSpec as P

MAXS = 60
LANES = 128
HALF = 64
CHUNK = 256
VMEM_LIMIT = 48 * 1024 * 1024
F32 = jnp.float32
BF16 = jnp.bfloat16


def params():
    return pltpu.CompilerParams(vmem_limit_bytes=VMEM_LIMIT)


def whole(shape):
    return pl.BlockSpec(shape, lambda *_: (0,) * len(shape))


def in_hbm(x):
    return pltpu.with_memory_space_constraint(x, pltpu.HBM)


def lane_roll(x):
    return pltpu.roll(x, HALF, 1)


def low_lanes(rows):
    return lax.broadcasted_iota(jnp.int32, (rows, LANES), 1) < HALF


def swap_pairs(count, first):
    pairs = []
    for i in range(first, count - 1, 2):
        pairs += [(i, i + 1), (i + 1, i)]
    return pairs


def swap(x, axis, first):
    return lax.ppermute(x, axis, swap_pairs(lax.axis_size(axis), first))


def by_parity(axis, body):
    odd = lax.rem(lax.axis_index(axis), 2)
    pl.when(odd == 0)(lambda: body(0))
    pl.when(odd == 1)(lambda: body(1))


def shifted_rows(row, lead, width):
    taps = row.shape[1]
    padded = jnp.concatenate([row, jnp.zeros((1, width - taps), F32)], axis=1)
    return pltpu.roll(
        jnp.broadcast_to(padded, (LANES, width)), lead, 1, stride=1, stride_axis=0
    )


def range_weights_kernel(range_ref, taps_ref, shift_hbm, w_ref, m_ref, shift_ref, sem):
    copy = pltpu.make_async_copy(shift_hbm, shift_ref, sem)
    copy.start()
    depth = w_ref.shape[0] // 2
    real = shifted_rows(range_ref[0:1, :].astype(F32), 0, depth)
    imag = shifted_rows(range_ref[1:2, :].astype(F32), 0, depth)
    real_t, imag_t = real.T.astype(BF16), imag.T.astype(BF16)
    w_ref[0:depth, 0:LANES] = real_t
    w_ref[0:depth, LANES:] = -imag_t
    w_ref[depth:, 0:LANES] = imag_t
    w_ref[depth:, LANES:] = real_t

    span = m_ref.shape[1]
    blocks = m_ref.shape[0]
    cells = taps_ref.shape[1]
    tap_count = taps_ref.shape[0]
    first = lax.axis_index("rg") * cells - HALF
    total = lax.axis_size("rg") * cells
    copy.wait()
    for b in range(blocks):
        source = lax.broadcasted_iota(jnp.int32, (span, LANES), 0)
        column = lax.broadcasted_iota(jnp.int32, (span, LANES), 1)
        tap = source - column - (HALF - tap_count // 2) - shift_ref[b]
        place = source + first + b * LANES
        tap = jnp.where((place >= 0) & (place < total), tap, -1)
        matrix = jnp.zeros((span, LANES), F32)
        for k in range(tap_count):
            row = taps_ref[k : k + 1, b * LANES : (b + 1) * LANES].astype(F32)
            matrix = jnp.where(tap == k, row, matrix)
        m_ref[b] = matrix.astype(BF16)


def range_weights(range_chirp, migration_taps, block_shift):
    blocks = block_shift.shape[0]
    depth = range_chirp.shape[1] + LANES
    return pl.pallas_call(
        range_weights_kernel,
        out_shape=(
            jax.ShapeDtypeStruct((2 * depth, 2 * LANES), BF16),
            jax.ShapeDtypeStruct((blocks, 2 * LANES, LANES), BF16),
        ),
        in_specs=[pl.BlockSpec(memory_space=pltpu.VMEM)] * 2
        + [pl.BlockSpec(memory_space=pltpu.HBM)],
        out_specs=(pl.BlockSpec(memory_space=pltpu.VMEM),) * 2,
        scratch_shapes=[pltpu.SMEM(block_shift.shape, jnp.int32), pltpu.SemaphoreType.DMA],
        compiler_params=params(),
        name="range_weights",
    )(range_chirp, migration_taps, in_hbm(block_shift))


def azimuth_weights_kernel(azimuth_ref, a_ref):
    steps, blocks, depth = a_ref.shape[0], a_ref.shape[1], a_ref.shape[3]
    gap = jnp.zeros((LANES, LANES), BF16)
    for b in range(blocks):
        for part in range(2):
            row = azimuth_ref[b, part : part + 1, :].astype(F32)
            rows = shifted_rows(row, 0, steps * depth - LANES).astype(BF16)
            upper = jnp.concatenate([rows, gap], axis=1)
            lower = jnp.concatenate([gap, rows], axis=1)
            base = part * CHUNK
            for k in range(steps):
                a_ref[k, b, base : base + LANES] = upper[:, k * depth : (k + 1) * depth]
                a_ref[k, b, base + LANES : base + CHUNK] = lower[:, k * depth : (k + 1) * depth]


def azimuth_weights(azimuth_chirp):
    blocks = azimuth_chirp.shape[0]
    steps = (azimuth_chirp.shape[2] + CHUNK) // CHUNK
    return pl.pallas_call(
        azimuth_weights_kernel,
        out_shape=jax.ShapeDtypeStruct((steps, blocks, 2 * CHUNK, CHUNK), BF16),
        in_specs=[pl.BlockSpec(memory_space=pltpu.VMEM)],
        out_specs=pl.BlockSpec(memory_space=pltpu.VMEM),
        compiler_params=params(),
        name="azimuth_weights",
    )(azimuth_chirp)


def tile_of(t):
    return slice(t * LANES, (t + 1) * LANES)


def edge_chunk(x_ref, s_ref, start, targets):
    picked = pl.ds(start, CHUNK)
    half = CHUNK // 2
    low, low_half = low_lanes(CHUNK), low_lanes(half)
    count = x_ref.shape[2] // LANES
    for part in range(2):
        cells = [x_ref[part, picked, tile_of(t)].astype(F32) for t in range(count)]
        rolled = [lane_roll(c) for c in cells]
        tiles = [rolled[0]]
        tiles += [jnp.where(low, rolled[t], rolled[t + 1]) for t in range(count - 1)]
        tiles += [rolled[-1]]
        tiles = [t.astype(BF16) for t in tiles]
        for t, tile in enumerate(tiles):
            s_ref[part, picked, tile_of(t)] = tile
        for out_ref, chunk, side in targets:
            inner = (1, 2) if side == 0 else (count - 2, count - 1)
            for i, t in enumerate(inner):
                at = (2 * part + i) * CHUNK
                out_ref[chunk, at : at + CHUNK, :] = tiles[t]
            at = 4 * CHUNK + part * half
            if side == 0:
                packed = jnp.where(low_half, cells[0][:half], rolled[0][half:])
            else:
                packed = jnp.where(low_half, rolled[-1][:half], cells[-1][half:])
            out_ref[chunk, at : at + half, :] = packed.astype(BF16)


def near_away_rows(rows):
    odd = lax.rem(lax.axis_index("az"), 2)
    last = rows - CHUNK
    near = pl.multiple_of((1 - odd) * last, CHUNK)
    away = pl.multiple_of(odd * last, CHUNK)
    return near, away


def edges_kernel(
    x_hbm, range_hbm, taps_hbm, azimuth_hbm,
    s_ref, far_near_ref, far_away_ref, far_mid_ref, core_ref, range_ref, taps_ref, azimuth_ref,
    x_ref, sems,
):
    rows = x_ref.shape[1]
    near, away = near_away_rows(rows)
    starts = [near, away] + list(range(CHUNK, rows - CHUNK, CHUNK))
    moves = []
    for start in starts:
        picked = pl.ds(start, CHUNK)
        moves.append((x_hbm.at[:, picked, :], x_ref.at[:, picked, :]))
    moves += [(range_hbm, range_ref), (taps_hbm, taps_ref), (azimuth_hbm, azimuth_ref)]
    copies = [
        pltpu.make_async_copy(source, target, sems.at[i])
        for i, (source, target) in enumerate(moves)
    ]
    for copy in copies:
        copy.start()

    def body(odd):
        for i, start in enumerate(starts):
            copies[i].wait()
            far = [(far_near_ref, 0), (far_away_ref, 0)][i] if i < 2 else (far_mid_ref, i - 2)
            edge_chunk(
                x_ref, s_ref, start, [(core_ref, i, 1 - odd), (far[0], far[1], odd)]
            )
        for copy in copies[len(starts) :]:
            copy.wait()

    by_parity("rg", body)


def range_edges(raw, range_chirp, migration_taps, azimuth_chirp):
    chunks = raw.shape[1] // CHUNK
    small = (range_chirp, migration_taps, azimuth_chirp)
    return pl.pallas_call(
        edges_kernel,
        out_shape=(jax.ShapeDtypeStruct(raw.shape[:2] + (raw.shape[2] + LANES,), BF16),)
        + tuple(
            jax.ShapeDtypeStruct((n, 5 * CHUNK, LANES), BF16) for n in (1, 1, chunks - 2, chunks)
        )
        + tuple(jax.ShapeDtypeStruct(x.shape, x.dtype) for x in small),
        in_specs=[pl.BlockSpec(memory_space=pltpu.HBM)] * 4,
        out_specs=(pl.BlockSpec(memory_space=pltpu.VMEM),) * 8,
        scratch_shapes=[
            pltpu.VMEM(raw.shape, BF16),
            pltpu.SemaphoreType.DMA((chunks + len(small),)),
        ],
        compiler_params=params(),
        name="range_edges",
    )(*(in_hbm(x) for x in (raw,) + small))


def window_tiles(s_ref, start, left, right, part):
    half = CHUNK // 2
    low = low_lanes(CHUNK)
    picked = pl.ds(start, CHUNK)
    last = s_ref.shape[2] // LANES - 1
    inner = slice(4 * CHUNK + part * half, 4 * CHUNK + (part + 1) * half)

    def full(halo):
        ref, chunk = halo
        return [
            ref[chunk, (2 * part + i) * CHUNK : (2 * part + i + 1) * CHUNK, :] for i in range(2)
        ]

    packed = left[0][left[1], inner, :].astype(F32)
    halo = jnp.concatenate([packed, lane_roll(packed)], axis=0)
    first = jnp.where(low, halo, s_ref[part, picked, tile_of(0)].astype(F32))
    packed = right[0][right[1], inner, :].astype(F32)
    halo = jnp.concatenate([lane_roll(packed), packed], axis=0)
    final = jnp.where(low, s_ref[part, picked, tile_of(last)].astype(F32), halo)
    own = [s_ref[part, picked, tile_of(t)] for t in range(1, last)]
    return full(left) + [first.astype(BF16)] + own + [final.astype(BF16)] + full(right)


def compress_chunk(s_ref, start, left, right, w_ref, m_ref, out_ref, out_start, c_ref):
    rows = CHUNK
    taps = w_ref.shape[0] // (2 * LANES)
    tiles = [window_tiles(s_ref, start, left, right, part) for part in range(2)]
    for j in range(c_ref.shape[1] // LANES):
        window = jnp.concatenate(tiles[0][j : j + taps] + tiles[1][j : j + taps], axis=1)
        result = jnp.dot(window, w_ref[...], preferred_element_type=F32).astype(BF16)
        c_ref[0:rows, tile_of(j)] = result[:, :LANES]
        c_ref[rows:, tile_of(j)] = result[:, LANES:]
    for b in range(m_ref.shape[0]):
        window = c_ref[:, b * LANES : b * LANES + 2 * LANES]
        result = jnp.dot(window, m_ref[b], preferred_element_type=F32).astype(BF16)
        out_ref[0, out_start : out_start + rows, tile_of(b)] = result[:rows]
        out_ref[1, out_start : out_start + rows, tile_of(b)] = result[rows:]


def compress_kernel(which, s_ref, core_ref, far_ref, w_ref, m_ref, out_ref, *c_refs):
    near, away = near_away_rows(s_ref.shape[1])
    if which == "mid":
        jobs = [(CHUNK * (i + 1), i + 2, i) for i in range(out_ref.shape[1] // CHUNK)]
    else:
        jobs = [(near, 0, 0) if which == "near" else (away, 1, 0)]

    def body(odd):
        for i, (start, core_chunk, far_chunk) in enumerate(jobs):
            core, far = (core_ref, core_chunk), (far_ref, far_chunk)
            left, right = (core, far) if odd else (far, core)
            compress_chunk(
                s_ref, start, left, right, w_ref, m_ref, out_ref, i * CHUNK, c_refs[i]
            )

    by_parity("rg", body)


def compress(which, shifted, core, far, w, m):
    rows, cells = shifted.shape[1], shifted.shape[2] - LANES
    count = rows // CHUNK - 2 if which == "mid" else 1
    return pl.pallas_call(
        functools.partial(compress_kernel, which),
        out_shape=jax.ShapeDtypeStruct((2, count * CHUNK, cells), BF16),
        in_specs=[pl.BlockSpec(memory_space=pltpu.VMEM)] * 5,
        out_specs=pl.BlockSpec(memory_space=pltpu.VMEM),
        scratch_shapes=[pltpu.VMEM((2 * CHUNK, cells + LANES), BF16)] * count,
        compiler_params=params(),
        name="compress_" + which,
    )(shifted, core, far, w, m)


def lines(ref, chunk):
    return lambda part, lanes: ref[part, chunk * CHUNK : (chunk + 1) * CHUNK, lanes]


def correlate_block(a_ref, b, pairs):
    taps = [a_ref[k, b] for k, _ in pairs]
    windows = [
        jnp.concatenate([window(0, tile_of(b)), window(1, tile_of(b))], axis=1)
        for _, window in pairs
    ]
    result = jnp.dot(
        jnp.concatenate(taps, axis=1),
        jnp.concatenate(windows, axis=0),
        preferred_element_type=F32,
    )
    top, bottom = result[:CHUNK], result[CHUNK:]
    return top[:, :LANES] + bottom[:, LANES:], top[:, LANES:] - bottom[:, :LANES]


def focus_own_kernel(a_ref, near_ref, mid_ref, away_ref, image_ref, part_ref, sum_ref, sems):
    mids = mid_ref.shape[1] // CHUNK
    steps, blocks = a_ref.shape[0], a_ref.shape[1]

    def body(odd):
        first, final = (near_ref, away_ref) if odd else (away_ref, near_ref)
        order = [lines(first, 0)] + [lines(mid_ref, i) for i in range(mids)] + [lines(final, 0)]
        copies = []
        for i in range(mids):
            for b in range(blocks):
                real, imag = correlate_block(a_ref, b, [(k, order[i + k]) for k in range(steps)])
                sum_ref[i, 0, :, tile_of(b)] = real
                sum_ref[i, 1, :, tile_of(b)] = imag
            copies.append(
                pltpu.make_async_copy(
                    sum_ref.at[i], image_ref.at[:, pl.ds((i + 1) * CHUNK, CHUNK), :], sems.at[i]
                )
            )
            copies[-1].start()
        for end in range(2):
            base = 0 if end == 0 else mids
            for b in range(blocks):
                real, imag = correlate_block(
                    a_ref, b, [(1 - end + k, order[base + k]) for k in range(2)]
                )
                part_ref[end, 0, :, tile_of(b)] = real
                part_ref[end, 1, :, tile_of(b)] = imag
        for copy in copies:
            copy.wait()

    by_parity("az", body)


def focus_own(a, near, mid, away):
    cells = mid.shape[2]
    mids = mid.shape[1] // CHUNK
    return pl.pallas_call(
        focus_own_kernel,
        out_shape=(
            jax.ShapeDtypeStruct((2, mid.shape[1] + 2 * CHUNK, cells), F32),
            jax.ShapeDtypeStruct((2, 2, CHUNK, cells), F32),
        ),
        in_specs=[pl.BlockSpec(memory_space=pltpu.VMEM)] * 4,
        out_specs=(pl.BlockSpec(memory_space=pl.ANY), pl.BlockSpec(memory_space=pltpu.VMEM)),
        scratch_shapes=[
            pltpu.VMEM((mids, 2, CHUNK, cells), F32),
            pltpu.SemaphoreType.DMA((mids,)),
        ],
        compiler_params=params(),
        name="focus_own",
    )(a, near, mid, away)


def focus_ends_kernel(a_ref, part_ref, near_ref, away_ref, _, image_ref, sum_ref, sems):
    rows = image_ref.shape[1]

    def body(odd):
        before, after = (near_ref, away_ref) if odd else (away_ref, near_ref)
        copies = []
        for end, halo_ref in enumerate((before, after)):
            for b in range(a_ref.shape[1]):
                real, imag = correlate_block(a_ref, b, [(2 * end, lines(halo_ref, 0))])
                sum_ref[end, 0, :, tile_of(b)] = part_ref[end, 0, :, tile_of(b)] + real
                sum_ref[end, 1, :, tile_of(b)] = part_ref[end, 1, :, tile_of(b)] + imag
            target = image_ref.at[:, pl.ds(end * (rows - CHUNK), CHUNK), :]
            copies.append(pltpu.make_async_copy(sum_ref.at[end], target, sems.at[end]))
            copies[-1].start()
        for copy in copies:
            copy.wait()

    by_parity("az", body)


def focus_ends(a, part, near, away, image):
    return pl.pallas_call(
        focus_ends_kernel,
        out_shape=jax.ShapeDtypeStruct(image.shape, F32),
        in_specs=[pl.BlockSpec(memory_space=pltpu.VMEM)] * 4
        + [pl.BlockSpec(memory_space=pl.ANY)],
        out_specs=pl.BlockSpec(memory_space=pl.ANY),
        scratch_shapes=[pltpu.VMEM(part.shape, F32), pltpu.SemaphoreType.DMA((2,))],
        input_output_aliases={4: 0},
        compiler_params=params(),
        name="focus_ends",
    )(a, part, near, away, image)


def per_device(raw_echo, range_chirp, migration_taps, block_shift, azimuth_chirp):
    shifted, far_near, far_away, far_mid, core, range_chirp, migration_taps, azimuth_chirp = (
        range_edges(raw_echo, range_chirp, migration_taps, azimuth_chirp)
    )
    core = swap(core, "rg", 0)
    far_near = swap(far_near, "rg", 1)
    far_away = swap(far_away, "rg", 1)
    w, m = range_weights(range_chirp, migration_taps, block_shift)
    far_mid, w = lax.optimization_barrier((far_mid, w))
    far_mid = swap(far_mid, "rg", 1)
    near = compress("near", shifted, core, far_near, w, m)
    near_halo = swap(near, "az", 0)
    away = compress("away", shifted, core, far_away, w, m)
    away_halo = swap(away, "az", 1)
    away, azimuth_chirp = lax.optimization_barrier((away, azimuth_chirp))
    a = azimuth_weights(azimuth_chirp)
    mid = compress("mid", shifted, core, far_mid, w, m)
    image, part = focus_own(a, near, mid, away)
    return focus_ends(a, part, near_halo, away_halo, image)


def solution(mesh):
    placed = (P(None, "az", "rg"), P(), P(None, "rg"), P("rg"), P("rg", None, None))
    return jax.shard_map(
        per_device, mesh=mesh, in_specs=placed, out_specs=P(None, "az", "rg"), check_vma=False
    )
```

```python
import functools

import jax
import jax.numpy as jnp
from jax import lax
from jax.experimental import pallas as pl
from jax.experimental.pallas import tpu as pltpu
from jax.sharding import PartitionSpec as P

MAXS = 60
LANES = 128
HALF = 64
CHUNK = 256
VMEM_LIMIT = 48 * 1024 * 1024
F32 = jnp.float32
BF16 = jnp.bfloat16


def params():
    return pltpu.CompilerParams(vmem_limit_bytes=VMEM_LIMIT)


def whole(shape):
    return pl.BlockSpec(shape, lambda *_: (0,) * len(shape))


def in_hbm(x):
    return pltpu.with_memory_space_constraint(x, pltpu.HBM)


def lane_roll(x):
    return pltpu.roll(x, HALF, 1)


def low_lanes(rows):
    return lax.broadcasted_iota(jnp.int32, (rows, LANES), 1) < HALF


def swap_pairs(count, first):
    pairs = []
    for i in range(first, count - 1, 2):
        pairs += [(i, i + 1), (i + 1, i)]
    return pairs


def swap(x, axis, first):
    return lax.ppermute(x, axis, swap_pairs(lax.axis_size(axis), first))


def by_parity(axis, body):
    odd = lax.rem(lax.axis_index(axis), 2)
    pl.when(odd == 0)(lambda: body(0))
    pl.when(odd == 1)(lambda: body(1))


def shifted_rows(row, lead, width):
    taps = row.shape[1]
    padded = jnp.concatenate([row, jnp.zeros((1, width - taps), F32)], axis=1)
    return pltpu.roll(
        jnp.broadcast_to(padded, (LANES, width)), lead, 1, stride=1, stride_axis=0
    )


def range_toeplitz(range_ref, w_ref):
    depth = w_ref.shape[0] // 2
    real = shifted_rows(range_ref[0:1, :].astype(F32), 0, depth)
    imag = shifted_rows(range_ref[1:2, :].astype(F32), 0, depth)
    real_t, imag_t = real.T.astype(BF16), imag.T.astype(BF16)
    w_ref[0:depth, 0:LANES] = real_t
    w_ref[0:depth, LANES:] = -imag_t
    w_ref[depth:, 0:LANES] = imag_t
    w_ref[depth:, LANES:] = real_t


def migration_bands(taps_ref, shift_ref, m_ref):
    span = m_ref.shape[1]
    blocks = m_ref.shape[0]
    cells = taps_ref.shape[1]
    tap_count = taps_ref.shape[0]
    first = lax.axis_index("rg") * cells - HALF
    total = lax.axis_size("rg") * cells
    for b in range(blocks):
        source = lax.broadcasted_iota(jnp.int32, (span, LANES), 0)
        column = lax.broadcasted_iota(jnp.int32, (span, LANES), 1)
        tap = source - column - (HALF - tap_count // 2) - shift_ref[b]
        place = source + first + b * LANES
        tap = jnp.where((place >= 0) & (place < total), tap, -1)
        matrix = jnp.zeros((span, LANES), F32)
        for k in range(tap_count):
            row = taps_ref[k : k + 1, b * LANES : (b + 1) * LANES].astype(F32)
            matrix = jnp.where(tap == k, row, matrix)
        m_ref[b] = matrix.astype(BF16)


def azimuth_weights_kernel(azimuth_ref, a_ref):
    steps, blocks, depth = a_ref.shape[0], a_ref.shape[1], a_ref.shape[3]
    gap = jnp.zeros((LANES, LANES), BF16)
    for b in range(blocks):
        for part in range(2):
            row = azimuth_ref[b, part : part + 1, :].astype(F32)
            rows = shifted_rows(row, 0, steps * depth - LANES).astype(BF16)
            upper = jnp.concatenate([rows, gap], axis=1)
            lower = jnp.concatenate([gap, rows], axis=1)
            base = part * CHUNK
            for k in range(steps):
                a_ref[k, b, base : base + LANES] = upper[:, k * depth : (k + 1) * depth]
                a_ref[k, b, base + LANES : base + CHUNK] = lower[:, k * depth : (k + 1) * depth]


def azimuth_weights(azimuth_chirp):
    blocks = azimuth_chirp.shape[0]
    steps = (azimuth_chirp.shape[2] + CHUNK) // CHUNK
    return pl.pallas_call(
        azimuth_weights_kernel,
        out_shape=jax.ShapeDtypeStruct((steps, blocks, 2 * CHUNK, CHUNK), BF16),
        in_specs=[pl.BlockSpec(memory_space=pltpu.VMEM)],
        out_specs=pl.BlockSpec(memory_space=pltpu.VMEM),
        compiler_params=params(),
        name="azimuth_weights",
    )(azimuth_chirp)


def tile_of(t):
    return slice(t * LANES, (t + 1) * LANES)


def edge_chunk(x_ref, s_ref, start, targets):
    picked = pl.ds(start, CHUNK)
    half = CHUNK // 2
    low, low_half = low_lanes(CHUNK), low_lanes(half)
    count = x_ref.shape[2] // LANES
    for part in range(2):
        cells = [x_ref[part, picked, tile_of(t)].astype(F32) for t in range(count)]
        rolled = [lane_roll(c) for c in cells]
        tiles = [rolled[0]]
        tiles += [jnp.where(low, rolled[t], rolled[t + 1]) for t in range(count - 1)]
        tiles += [rolled[-1]]
        tiles = [t.astype(BF16) for t in tiles]
        for t, tile in enumerate(tiles):
            s_ref[part, picked, tile_of(t)] = tile
        for out_ref, chunk, side in targets:
            inner = (1, 2) if side == 0 else (count - 2, count - 1)
            for i, t in enumerate(inner):
                at = (2 * part + i) * CHUNK
                out_ref[chunk, at : at + CHUNK, :] = tiles[t]
            at = 4 * CHUNK + part * half
            if side == 0:
                packed = jnp.where(low_half, cells[0][:half], rolled[0][half:])
            else:
                packed = jnp.where(low_half, rolled[-1][:half], cells[-1][half:])
            out_ref[chunk, at : at + half, :] = packed.astype(BF16)


def near_away_rows(rows):
    odd = lax.rem(lax.axis_index("az"), 2)
    last = rows - CHUNK
    near = pl.multiple_of((1 - odd) * last, CHUNK)
    away = pl.multiple_of(odd * last, CHUNK)
    return near, away


def edges_kernel(
    x_hbm, range_hbm, taps_hbm, shift_hbm, azimuth_hbm,
    s_ref, far_outer_ref, far_mid_ref, core_ref, w_ref, m_ref, azimuth_ref,
    x_ref, range_ref, taps_ref, shift_ref, sems,
):
    rows = x_ref.shape[1]
    near, away = near_away_rows(rows)
    starts = [near, away] + list(range(CHUNK, rows - CHUNK, CHUNK))
    moves = [
        (range_hbm, range_ref),
        (taps_hbm, taps_ref),
        (shift_hbm, shift_ref),
        (azimuth_hbm, azimuth_ref),
    ]
    small = len(moves)
    for start in starts:
        picked = pl.ds(start, CHUNK)
        moves.append((x_hbm.at[:, picked, :], x_ref.at[:, picked, :]))
    copies = [
        pltpu.make_async_copy(source, target, sems.at[i])
        for i, (source, target) in enumerate(moves)
    ]
    for copy in copies:
        copy.start()
    for copy in copies[:small]:
        copy.wait()
    range_toeplitz(range_ref, w_ref)
    migration_bands(taps_ref, shift_ref, m_ref)

    def body(odd):
        for i, start in enumerate(starts):
            copies[small + i].wait()
            far_ref, chunk = (far_outer_ref, i) if i < 2 else (far_mid_ref, i - 2)
            edge_chunk(
                x_ref, s_ref, start, [(core_ref, i, 1 - odd), (far_ref, chunk, odd)]
            )

    by_parity("rg", body)


def range_edges(raw, range_chirp, migration_taps, block_shift, azimuth_chirp):
    chunks = raw.shape[1] // CHUNK
    blocks = block_shift.shape[0]
    depth = range_chirp.shape[1] + LANES
    args = (raw, range_chirp, migration_taps, block_shift, azimuth_chirp)
    return pl.pallas_call(
        edges_kernel,
        out_shape=(jax.ShapeDtypeStruct(raw.shape[:2] + (raw.shape[2] + LANES,), BF16),)
        + tuple(
            jax.ShapeDtypeStruct((n, 5 * CHUNK, LANES), BF16) for n in (2, chunks - 2, chunks)
        )
        + (
            jax.ShapeDtypeStruct((2 * depth, 2 * LANES), BF16),
            jax.ShapeDtypeStruct((blocks, 2 * LANES, LANES), BF16),
            jax.ShapeDtypeStruct(azimuth_chirp.shape, BF16),
        ),
        in_specs=[pl.BlockSpec(memory_space=pltpu.HBM)] * len(args),
        out_specs=(pl.BlockSpec(memory_space=pltpu.VMEM),) * 7,
        scratch_shapes=[
            pltpu.VMEM(raw.shape, BF16),
            pltpu.VMEM(range_chirp.shape, BF16),
            pltpu.VMEM(migration_taps.shape, BF16),
            pltpu.SMEM(block_shift.shape, jnp.int32),
            pltpu.SemaphoreType.DMA((chunks + len(args) - 1,)),
        ],
        compiler_params=params(),
        name="range_edges",
    )(*(in_hbm(x) for x in args))


def window_tiles(s_ref, start, left, right, part):
    half = CHUNK // 2
    low = low_lanes(CHUNK)
    picked = pl.ds(start, CHUNK)
    last = s_ref.shape[2] // LANES - 1
    inner = slice(4 * CHUNK + part * half, 4 * CHUNK + (part + 1) * half)

    def full(halo):
        ref, chunk = halo
        return [
            ref[chunk, (2 * part + i) * CHUNK : (2 * part + i + 1) * CHUNK, :] for i in range(2)
        ]

    packed = left[0][left[1], inner, :].astype(F32)
    halo = jnp.concatenate([packed, lane_roll(packed)], axis=0)
    first = jnp.where(low, halo, s_ref[part, picked, tile_of(0)].astype(F32))
    packed = right[0][right[1], inner, :].astype(F32)
    halo = jnp.concatenate([lane_roll(packed), packed], axis=0)
    final = jnp.where(low, s_ref[part, picked, tile_of(last)].astype(F32), halo)
    own = [s_ref[part, picked, tile_of(t)] for t in range(1, last)]
    return full(left) + [first.astype(BF16)] + own + [final.astype(BF16)] + full(right)


def compress_chunk(s_ref, start, left, right, w_ref, m_ref, out_ref, out_start, c_ref):
    rows = CHUNK
    taps = w_ref.shape[0] // (2 * LANES)
    tiles = [window_tiles(s_ref, start, left, right, part) for part in range(2)]
    for j in range(c_ref.shape[1] // LANES):
        window = jnp.concatenate(tiles[0][j : j + taps] + tiles[1][j : j + taps], axis=1)
        result = jnp.dot(window, w_ref[...], preferred_element_type=F32).astype(BF16)
        c_ref[0:rows, tile_of(j)] = result[:, :LANES]
        c_ref[rows:, tile_of(j)] = result[:, LANES:]
    for b in range(m_ref.shape[0]):
        window = c_ref[:, b * LANES : b * LANES + 2 * LANES]
        result = jnp.dot(window, m_ref[b], preferred_element_type=F32).astype(BF16)
        out_ref[0, out_start : out_start + rows, tile_of(b)] = result[:rows]
        out_ref[1, out_start : out_start + rows, tile_of(b)] = result[rows:]


def compress_kernel(which, s_ref, core_ref, far_ref, w_ref, m_ref, out_ref, *c_refs):
    near, away = near_away_rows(s_ref.shape[1])
    if which == "mid":
        jobs = [(CHUNK * (i + 1), i + 2, i) for i in range(out_ref.shape[1] // CHUNK)]
    else:
        jobs = [(near, 0, 0) if which == "near" else (away, 1, 1)]

    def body(odd):
        for i, (start, core_chunk, far_chunk) in enumerate(jobs):
            core, far = (core_ref, core_chunk), (far_ref, far_chunk)
            left, right = (core, far) if odd else (far, core)
            compress_chunk(
                s_ref, start, left, right, w_ref, m_ref, out_ref, i * CHUNK, c_refs[i]
            )

    by_parity("rg", body)


def compress(which, shifted, core, far, w, m):
    rows, cells = shifted.shape[1], shifted.shape[2] - LANES
    count = rows // CHUNK - 2 if which == "mid" else 1
    return pl.pallas_call(
        functools.partial(compress_kernel, which),
        out_shape=jax.ShapeDtypeStruct((2, count * CHUNK, cells), BF16),
        in_specs=[pl.BlockSpec(memory_space=pltpu.VMEM)] * 5,
        out_specs=pl.BlockSpec(memory_space=pltpu.VMEM),
        scratch_shapes=[pltpu.VMEM((2 * CHUNK, cells + LANES), BF16)] * count,
        compiler_params=params(),
        name="compress_" + which,
    )(shifted, core, far, w, m)


def lines(ref, chunk):
    return lambda part, lanes: ref[part, chunk * CHUNK : (chunk + 1) * CHUNK, lanes]


def correlate_block(a_ref, b, pairs):
    taps = [a_ref[k, b] for k, _ in pairs]
    windows = [
        jnp.concatenate([window(0, tile_of(b)), window(1, tile_of(b))], axis=1)
        for _, window in pairs
    ]
    result = jnp.dot(
        jnp.concatenate(taps, axis=1),
        jnp.concatenate(windows, axis=0),
        preferred_element_type=F32,
    )
    top, bottom = result[:CHUNK], result[CHUNK:]
    return top[:, :LANES] + bottom[:, LANES:], top[:, LANES:] - bottom[:, :LANES]


def focus_own_kernel(a_ref, near_ref, mid_ref, away_ref, image_ref, part_ref, sum_ref, sems):
    mids = mid_ref.shape[1] // CHUNK
    steps, blocks = a_ref.shape[0], a_ref.shape[1]

    def body(odd):
        first, final = (near_ref, away_ref) if odd else (away_ref, near_ref)
        order = [lines(first, 0)] + [lines(mid_ref, i) for i in range(mids)] + [lines(final, 0)]
        copies = []
        for i in range(mids):
            for b in range(blocks):
                real, imag = correlate_block(a_ref, b, [(k, order[i + k]) for k in range(steps)])
                sum_ref[i, 0, :, tile_of(b)] = real
                sum_ref[i, 1, :, tile_of(b)] = imag
            copies.append(
                pltpu.make_async_copy(
                    sum_ref.at[i], image_ref.at[:, pl.ds((i + 1) * CHUNK, CHUNK), :], sems.at[i]
                )
            )
            copies[-1].start()
        for end in range(2):
            base = 0 if end == 0 else mids
            for b in range(blocks):
                real, imag = correlate_block(
                    a_ref, b, [(1 - end + k, order[base + k]) for k in range(2)]
                )
                part_ref[end, 0, :, tile_of(b)] = real
                part_ref[end, 1, :, tile_of(b)] = imag
        for copy in copies:
            copy.wait()

    by_parity("az", body)


def focus_own(a, near, mid, away):
    cells = mid.shape[2]
    mids = mid.shape[1] // CHUNK
    return pl.pallas_call(
        focus_own_kernel,
        out_shape=(
            jax.ShapeDtypeStruct((2, mid.shape[1] + 2 * CHUNK, cells), F32),
            jax.ShapeDtypeStruct((2, 2, CHUNK, cells), F32),
        ),
        in_specs=[pl.BlockSpec(memory_space=pltpu.VMEM)] * 4,
        out_specs=(pl.BlockSpec(memory_space=pl.ANY), pl.BlockSpec(memory_space=pltpu.VMEM)),
        scratch_shapes=[
            pltpu.VMEM((mids, 2, CHUNK, cells), F32),
            pltpu.SemaphoreType.DMA((mids,)),
        ],
        compiler_params=params(),
        name="focus_own",
    )(a, near, mid, away)


def focus_end_kernel(which, a_ref, part_ref, halo_ref, _, image_ref, sum_ref, sem):
    rows = image_ref.shape[1]

    def body(odd):
        end = 1 - odd if which == "near" else odd
        for b in range(a_ref.shape[1]):
            real, imag = correlate_block(a_ref, b, [(2 * end, lines(halo_ref, 0))])
            sum_ref[0, :, tile_of(b)] = part_ref[end, 0, :, tile_of(b)] + real
            sum_ref[1, :, tile_of(b)] = part_ref[end, 1, :, tile_of(b)] + imag
        target = image_ref.at[:, pl.ds(end * (rows - CHUNK), CHUNK), :]
        copy = pltpu.make_async_copy(sum_ref, target, sem)
        copy.start()
        copy.wait()

    by_parity("az", body)


def focus_end(which, a, part, halo, image):
    return pl.pallas_call(
        functools.partial(focus_end_kernel, which),
        out_shape=jax.ShapeDtypeStruct(image.shape, F32),
        in_specs=[pl.BlockSpec(memory_space=pltpu.VMEM)] * 3
        + [pl.BlockSpec(memory_space=pl.ANY)],
        out_specs=pl.BlockSpec(memory_space=pl.ANY),
        scratch_shapes=[pltpu.VMEM(part.shape[1:], F32), pltpu.SemaphoreType.DMA],
        input_output_aliases={3: 0},
        compiler_params=params(),
        name="focus_" + which,
    )(a, part, halo, image)


def per_device(raw_echo, range_chirp, migration_taps, block_shift, azimuth_chirp):
    shifted, far_outer, far_mid, core, w, m, azimuth_chirp = range_edges(
        raw_echo, range_chirp, migration_taps, block_shift, azimuth_chirp
    )
    core = swap(core, "rg", 0)
    far_outer = swap(far_outer, "rg", 1)
    far_mid = swap(far_mid, "rg", 1)
    near = compress("near", shifted, core, far_outer, w, m)
    near_halo = swap(near, "az", 0)
    away = compress("away", shifted, core, far_outer, w, m)
    away_halo = swap(away, "az", 1)
    away, azimuth_chirp = lax.optimization_barrier((away, azimuth_chirp))
    a = azimuth_weights(azimuth_chirp)
    mid = compress("mid", shifted, core, far_mid, w, m)
    image, part = focus_own(a, near, mid, away)
    image = focus_end("near", a, part, near_halo, image)
    return focus_end("away", a, part, away_halo, image)


def solution(mesh):
    placed = (P(None, "az", "rg"), P(), P(None, "rg"), P("rg"), P("rg", None, None))
    return jax.shard_map(
        per_device, mesh=mesh, in_specs=placed, out_specs=P(None, "az", "rg"), check_vma=False
    )
```

```python
import functools

import jax
import jax.numpy as jnp
from jax import lax
from jax.experimental import pallas as pl
from jax.experimental.pallas import tpu as pltpu
from jax.sharding import PartitionSpec as P

MAXS = 60
LANES = 128
HALF = 64
CHUNK = 256
PAD = 16
VMEM_LIMIT = 20 * 1024 * 1024
F32 = jnp.float32
BF16 = jnp.bfloat16


def params():
    return pltpu.CompilerParams(vmem_limit_bytes=VMEM_LIMIT)


def whole(shape):
    return pl.BlockSpec(shape, lambda *_: (0,) * len(shape))


def in_hbm(x):
    return pltpu.with_memory_space_constraint(x, pltpu.HBM)


def lane_roll(x):
    return pltpu.roll(x, HALF, 1)


def low_lanes(rows):
    return lax.broadcasted_iota(jnp.int16, (rows, LANES), 1) < HALF


def swap_pairs(count, first):
    pairs = []
    for i in range(first, count - 1, 2):
        pairs += [(i, i + 1), (i + 1, i)]
    return pairs


def swap(x, axis, first):
    return lax.ppermute(x, axis, swap_pairs(lax.axis_size(axis), first))


def by_parity(axis, body):
    odd = lax.rem(lax.axis_index(axis), 2)
    pl.when(odd == 0)(lambda: body(0))
    pl.when(odd == 1)(lambda: body(1))


def shifted_rows(row, lead, width):
    taps = row.shape[1]
    padded = jnp.concatenate([row, jnp.zeros((1, width - taps), F32)], axis=1)
    return pltpu.roll(
        jnp.broadcast_to(padded, (LANES, width)), lead, 1, stride=1, stride_axis=0
    )


def range_toeplitz(range_ref, w_ref):
    depth = w_ref.shape[0] // 2
    real = shifted_rows(range_ref[0:1, :].astype(F32), 0, depth)
    imag = shifted_rows(range_ref[1:2, :].astype(F32), 0, depth)
    real_t, imag_t = real.T.astype(BF16), imag.T.astype(BF16)
    w_ref[0:depth, 0:LANES] = real_t
    w_ref[0:depth, LANES:] = -imag_t
    w_ref[depth:, 0:LANES] = imag_t
    w_ref[depth:, LANES:] = real_t


def migration_bands(taps_ref, shift_ref, m_ref):
    span = m_ref.shape[1]
    blocks = m_ref.shape[0]
    cells = taps_ref.shape[1]
    tap_count = taps_ref.shape[0]
    first = lax.axis_index("rg") * cells - HALF
    total = lax.axis_size("rg") * cells
    for b in range(blocks):
        source = lax.broadcasted_iota(jnp.int32, (span, LANES), 0)
        column = lax.broadcasted_iota(jnp.int32, (span, LANES), 1)
        tap = source - column - (HALF - tap_count // 2) - shift_ref[b][:1, :]
        place = source + first + b * LANES
        tap = jnp.where((place >= 0) & (place < total), tap, -1)
        matrix = jnp.zeros((span, LANES), F32)
        for k in range(tap_count):
            row = taps_ref[k : k + 1, b * LANES : (b + 1) * LANES].astype(F32)
            matrix = jnp.where(tap == k, row, matrix)
        m_ref[b] = matrix.astype(BF16)


def azimuth_weights_kernel(azimuth_ref, a_ref):
    steps, blocks, depth = a_ref.shape[0], a_ref.shape[1], a_ref.shape[3]
    gap = jnp.zeros((LANES, LANES), BF16)
    for b in range(blocks):
        for part in range(2):
            row = azimuth_ref[b, part : part + 1, :].astype(F32)
            rows = shifted_rows(row, 0, steps * depth - LANES).astype(BF16)
            upper = jnp.concatenate([rows, gap], axis=1)
            lower = jnp.concatenate([gap, rows], axis=1)
            base = part * CHUNK
            for k in range(steps):
                a_ref[k, b, base : base + LANES] = upper[:, k * depth : (k + 1) * depth]
                a_ref[k, b, base + LANES : base + CHUNK] = lower[:, k * depth : (k + 1) * depth]


def azimuth_weights(azimuth_chirp):
    blocks = azimuth_chirp.shape[0]
    steps = (azimuth_chirp.shape[2] + CHUNK) // CHUNK
    return pl.pallas_call(
        azimuth_weights_kernel,
        out_shape=jax.ShapeDtypeStruct((steps, blocks, 2 * CHUNK, CHUNK), BF16),
        in_specs=[pl.BlockSpec(memory_space=pltpu.VMEM)],
        out_specs=pl.BlockSpec(memory_space=pltpu.VMEM),
        compiler_params=params(),
        name="azimuth_weights",
    )(azimuth_chirp)


def tile_of(t):
    return slice(t * LANES, (t + 1) * LANES)


def edge_chunk(x_ref, s_ref, start, targets):
    picked = pl.ds(start, CHUNK)
    half = CHUNK // 2
    low, low_half = low_lanes(CHUNK), low_lanes(half)
    count = x_ref.shape[2] // LANES
    for part in range(2):
        cells = [x_ref[part, picked, tile_of(t)] for t in range(count)]
        rolled = [lane_roll(c) for c in cells]
        tiles = [rolled[0]]
        tiles += [jnp.where(low, rolled[t], rolled[t + 1]) for t in range(count - 1)]
        tiles += [rolled[-1]]
        for t, tile in enumerate(tiles):
            s_ref[part, picked, tile_of(t)] = tile
        for out_ref, chunk, side in targets:
            inner = (1, 2) if side == 0 else (count - 2, count - 1)
            for i, t in enumerate(inner):
                at = (2 * part + i) * CHUNK
                out_ref[chunk, at : at + CHUNK, :] = tiles[t]
            at = 4 * CHUNK + part * half
            if side == 0:
                packed = jnp.where(low_half, cells[0][:half], rolled[0][half:])
            else:
                packed = jnp.where(low_half, rolled[-1][:half], cells[-1][half:])
            out_ref[chunk, at : at + half, :] = packed


def near_away_rows(rows):
    odd = lax.rem(lax.axis_index("az"), 2)
    last = rows - CHUNK
    near = pl.multiple_of((1 - odd) * last, CHUNK)
    away = pl.multiple_of(odd * last, CHUNK)
    return near, away


def edges_kernel(
    x_hbm, range_hbm, taps_hbm, shift_hbm, azimuth_hbm,
    s_ref, far_outer_ref, far_mid_ref, core_outer_ref, core_mid_ref,
    w_ref, taps_ref, splat_ref, azimuth_ref, x_ref, range_ref, shift_ref, sems,
):
    rows = x_ref.shape[1]
    near, away = near_away_rows(rows)
    starts = [near, away] + list(range(CHUNK, rows - CHUNK, CHUNK))
    moves = [
        (range_hbm, range_ref),
        (taps_hbm, taps_ref),
        (shift_hbm, shift_ref),
        (azimuth_hbm, azimuth_ref),
    ]
    small = len(moves)
    for start in starts:
        for part in range(2):
            picked = pl.ds(start, CHUNK)
            moves.append((x_hbm.at[part, picked, :], x_ref.at[part, picked, :]))
    copies = [
        pltpu.make_async_copy(source, target, sems.at[i])
        for i, (source, target) in enumerate(moves)
    ]
    for copy in copies:
        copy.start()
    for copy in copies[:small]:
        copy.wait()
    for ref in (core_outer_ref, core_mid_ref):
        extra = ref.shape[1] - 5 * CHUNK
        ref[:, 5 * CHUNK :, :] = jnp.zeros((ref.shape[0], extra, LANES), BF16)
    range_toeplitz(range_ref, w_ref)
    for b in range(splat_ref.shape[0]):
        splat_ref[b] = jnp.full(splat_ref.shape[1:], shift_ref[b], jnp.int32)

    def body(odd):
        for i, start in enumerate(starts):
            copies[small + 2 * i].wait()
            copies[small + 2 * i + 1].wait()
            outer = (core_outer_ref, far_outer_ref, i)
            core_ref, far_ref, chunk = outer if i < 2 else (core_mid_ref, far_mid_ref, i - 2)
            edge_chunk(x_ref, s_ref, start, [(core_ref, chunk, 1 - odd), (far_ref, chunk, odd)])

    by_parity("rg", body)


def range_edges(raw, range_chirp, migration_taps, block_shift, azimuth_chirp):
    chunks = raw.shape[1] // CHUNK
    blocks = block_shift.shape[0]
    depth = range_chirp.shape[1] + LANES
    args = (raw, range_chirp, migration_taps, block_shift, azimuth_chirp)
    return pl.pallas_call(
        edges_kernel,
        out_shape=(jax.ShapeDtypeStruct(raw.shape[:2] + (raw.shape[2] + LANES,), BF16),)
        + tuple(
            jax.ShapeDtypeStruct((n, 5 * CHUNK + extra, LANES), BF16)
            for n, extra in ((2, 0), (chunks - 2, 0), (2, 2 * PAD), (chunks - 2, PAD))
        )
        + (
            jax.ShapeDtypeStruct((2 * depth, 2 * LANES), BF16),
            jax.ShapeDtypeStruct(migration_taps.shape, BF16),
            jax.ShapeDtypeStruct((blocks, 8, LANES), jnp.int32),
            jax.ShapeDtypeStruct(azimuth_chirp.shape, BF16),
        ),
        in_specs=[pl.BlockSpec(memory_space=pltpu.HBM)] * len(args),
        out_specs=(pl.BlockSpec(memory_space=pltpu.VMEM),) * 9,
        scratch_shapes=[
            pltpu.VMEM(raw.shape, BF16),
            pltpu.VMEM(range_chirp.shape, BF16),
            pltpu.SMEM(block_shift.shape, jnp.int32),
            pltpu.SemaphoreType.DMA((2 * chunks + len(args) - 1,)),
        ],
        compiler_params=params(),
        name="range_edges",
    )(*(in_hbm(x) for x in args))


def window_tiles(s_ref, start, left, right, part):
    half = CHUNK // 2
    low = low_lanes(CHUNK)
    picked = pl.ds(start, CHUNK)
    last = s_ref.shape[2] // LANES - 1
    inner = slice(4 * CHUNK + part * half, 4 * CHUNK + (part + 1) * half)

    def full(halo):
        ref, chunk = halo
        return [
            ref[chunk, (2 * part + i) * CHUNK : (2 * part + i + 1) * CHUNK, :] for i in range(2)
        ]

    packed = left[0][left[1], inner, :]
    halo = jnp.concatenate([packed, lane_roll(packed)], axis=0)
    first = jnp.where(low, halo, s_ref[part, picked, tile_of(0)])
    packed = right[0][right[1], inner, :]
    halo = jnp.concatenate([lane_roll(packed), packed], axis=0)
    final = jnp.where(low, s_ref[part, picked, tile_of(last)], halo)
    own = [s_ref[part, picked, tile_of(t)] for t in range(1, last)]
    return full(left) + [first] + own + [final] + full(right)


def compress_chunk(s_ref, start, left, right, w_ref, m_ref, out_ref, out_start, c_ref):
    rows = CHUNK
    taps = w_ref.shape[0] // (2 * LANES)
    tiles = [window_tiles(s_ref, start, left, right, part) for part in range(2)]
    for j in range(c_ref.shape[1] // LANES):
        window = jnp.concatenate(tiles[0][j : j + taps] + tiles[1][j : j + taps], axis=1)
        result = jnp.dot(window, w_ref[...], preferred_element_type=F32).astype(BF16)
        c_ref[0:rows, tile_of(j)] = result[:, :LANES]
        c_ref[rows:, tile_of(j)] = result[:, LANES:]
    for b in range(m_ref.shape[0]):
        window = c_ref[:, b * LANES : b * LANES + 2 * LANES]
        result = jnp.dot(window, m_ref[b], preferred_element_type=F32).astype(BF16)
        out_ref[0, out_start : out_start + rows, tile_of(b)] = result[:rows]
        out_ref[1, out_start : out_start + rows, tile_of(b)] = result[rows:]


def compress_kernel(which, s_ref, core_ref, far_ref, w_ref, *refs):
    near, away = near_away_rows(s_ref.shape[1])
    if which == "near":
        taps_ref, splat_ref, out_ref, m_ref, *c_refs = refs
        jobs = [(near, 0)]
    else:
        m_ref, out_ref, *c_refs = refs
        jobs = [(CHUNK * (i + 1), i) for i in range(out_ref.shape[1] // CHUNK)]
        if which == "away":
            jobs = [(away, 1)]

    def body(odd):
        if which == "near":
            migration_bands(taps_ref, splat_ref, m_ref)
        for i, (start, chunk) in enumerate(jobs):
            core, far = (core_ref, chunk), (far_ref, chunk)
            left, right = (core, far) if odd else (far, core)
            compress_chunk(
                s_ref, start, left, right, w_ref, m_ref, out_ref, i * CHUNK, c_refs[i]
            )

    by_parity("rg", body)


def compress(which, shifted, core, far, w, *bands):
    rows, cells = shifted.shape[1], shifted.shape[2] - LANES
    count = rows // CHUNK - 2 if which == "mid" else 1
    args = (shifted, core, far, w) + bands
    out = (jax.ShapeDtypeStruct((2, count * CHUNK, cells), BF16),)
    if which == "near":
        out += (jax.ShapeDtypeStruct((cells // LANES, 2 * LANES, LANES), BF16),)
    result = pl.pallas_call(
        functools.partial(compress_kernel, which),
        out_shape=out,
        in_specs=[pl.BlockSpec(memory_space=pltpu.VMEM)] * len(args),
        out_specs=(pl.BlockSpec(memory_space=pltpu.VMEM),) * len(out),
        scratch_shapes=[pltpu.VMEM((2 * CHUNK, cells + LANES), BF16)] * count,
        compiler_params=params(),
        name="compress_" + which,
    )(*args)
    return result if which == "near" else result[0]


def lines(ref, chunk):
    return lambda part, lanes: ref[part, chunk * CHUNK : (chunk + 1) * CHUNK, lanes]


def correlate_block(a_ref, b, pairs):
    taps = [a_ref[k, b] for k, _ in pairs]
    windows = [
        jnp.concatenate([window(0, tile_of(b)), window(1, tile_of(b))], axis=1)
        for _, window in pairs
    ]
    result = jnp.dot(
        jnp.concatenate(taps, axis=1),
        jnp.concatenate(windows, axis=0),
        preferred_element_type=F32,
    )
    top, bottom = result[:CHUNK], result[CHUNK:]
    return top[:, :LANES] + bottom[:, LANES:], top[:, LANES:] - bottom[:, :LANES]


def focus_outer_kernel(a_ref, near_ref, away_ref, part_ref, mid_part_ref):
    mids, steps, blocks = mid_part_ref.shape[0], a_ref.shape[0], a_ref.shape[1]

    def body(odd):
        first, final = (near_ref, away_ref) if odd else (away_ref, near_ref)
        order = {0: lines(first, 0), mids + 1: lines(final, 0)}
        jobs = [(part_ref.at[0], 0), (part_ref.at[1], mids + 1)]
        jobs += [(mid_part_ref.at[i], i + 1) for i in range(mids)]
        for out_ref, chunk in jobs:
            pairs = [
                (k, order[chunk + k - 1]) for k in range(steps) if chunk + k - 1 in order
            ]
            for b in range(blocks):
                out_ref[0, :, tile_of(b)], out_ref[1, :, tile_of(b)] = correlate_block(
                    a_ref, b, pairs
                )

    by_parity("az", body)


def focus_outer(a, near, away, mids):
    cells = near.shape[2]
    return pl.pallas_call(
        focus_outer_kernel,
        out_shape=(
            jax.ShapeDtypeStruct((2, 2, CHUNK, cells), F32),
            jax.ShapeDtypeStruct((mids, 2, CHUNK, cells), F32),
        ),
        in_specs=[pl.BlockSpec(memory_space=pltpu.VMEM)] * 3,
        out_specs=(pl.BlockSpec(memory_space=pltpu.VMEM),) * 2,
        compiler_params=params(),
        name="focus_outer",
    )(a, near, away)


def focus_mid_kernel(a_ref, mid_ref, part_ref, mid_part_ref, image_ref, end_ref, sum_ref, sems):
    mids, steps, blocks = mid_part_ref.shape[0], a_ref.shape[0], a_ref.shape[1]
    order = {i + 1: lines(mid_ref, i) for i in range(mids)}
    jobs = [(mid_part_ref.at[i], sum_ref.at[i], i + 1) for i in range(mids)]
    jobs += [(part_ref.at[0], end_ref.at[0], 0), (part_ref.at[1], end_ref.at[1], mids + 1)]
    copies = []
    for i, (before_ref, out_ref, chunk) in enumerate(jobs):
        pairs = [(k, order[chunk + k - 1]) for k in range(steps) if chunk + k - 1 in order]
        for b in range(blocks):
            real, imag = correlate_block(a_ref, b, pairs)
            out_ref[0, :, tile_of(b)] = before_ref[0, :, tile_of(b)] + real
            out_ref[1, :, tile_of(b)] = before_ref[1, :, tile_of(b)] + imag
        if i < mids:
            target = image_ref.at[:, pl.ds(chunk * CHUNK, CHUNK), :]
            copies.append(pltpu.make_async_copy(out_ref, target, sems.at[i]))
            copies[-1].start()
    for copy in copies:
        copy.wait()


def focus_mid(a, mid, part, mid_part):
    cells = mid.shape[2]
    mids = mid_part.shape[0]
    return pl.pallas_call(
        focus_mid_kernel,
        out_shape=(
            jax.ShapeDtypeStruct((2, (mids + 2) * CHUNK, cells), F32),
            jax.ShapeDtypeStruct(part.shape, F32),
        ),
        in_specs=[pl.BlockSpec(memory_space=pltpu.VMEM)] * 4,
        out_specs=(pl.BlockSpec(memory_space=pl.ANY), pl.BlockSpec(memory_space=pltpu.VMEM)),
        scratch_shapes=[pltpu.VMEM(mid_part.shape, F32), pltpu.SemaphoreType.DMA((mids,))],
        compiler_params=params(),
        name="focus_mid",
    )(a, mid, part, mid_part)


def focus_end_kernel(which, a_ref, part_ref, halo_ref, _, image_ref, sum_ref, sem):
    rows = image_ref.shape[1]

    def body(odd):
        end = 1 - odd if which == "near" else odd
        for b in range(a_ref.shape[1]):
            real, imag = correlate_block(a_ref, b, [(2 * end, lines(halo_ref, 0))])
            sum_ref[0, :, tile_of(b)] = part_ref[end, 0, :, tile_of(b)] + real
            sum_ref[1, :, tile_of(b)] = part_ref[end, 1, :, tile_of(b)] + imag
        target = image_ref.at[:, pl.ds(end * (rows - CHUNK), CHUNK), :]
        copy = pltpu.make_async_copy(sum_ref, target, sem)
        copy.start()
        copy.wait()

    by_parity("az", body)


def focus_end(which, a, part, halo, image):
    return pl.pallas_call(
        functools.partial(focus_end_kernel, which),
        out_shape=jax.ShapeDtypeStruct(image.shape, F32),
        in_specs=[pl.BlockSpec(memory_space=pltpu.VMEM)] * 3
        + [pl.BlockSpec(memory_space=pl.ANY)],
        out_specs=pl.BlockSpec(memory_space=pl.ANY),
        scratch_shapes=[pltpu.VMEM(part.shape[1:], F32), pltpu.SemaphoreType.DMA],
        input_output_aliases={3: 0},
        compiler_params=params(),
        name="focus_" + which,
    )(a, part, halo, image)


def per_device(raw_echo, range_chirp, migration_taps, block_shift, azimuth_chirp):
    shifted, far_outer, far_mid, core_outer, core_mid, w, taps, splat, azimuth_chirp = range_edges(
        raw_echo, range_chirp, migration_taps, block_shift, azimuth_chirp
    )
    core_outer = swap(core_outer, "rg", 0)
    core_mid = swap(core_mid, "rg", 0)
    far_outer = swap(far_outer, "rg", 1)
    far_mid = swap(far_mid, "rg", 1)
    near, m = compress("near", shifted, core_outer, far_outer, w, taps, splat)
    near_halo = swap(near, "az", 0)
    core_outer, core_mid, near = lax.optimization_barrier((core_outer, core_mid, near))
    away = compress("away", shifted, core_outer, far_outer, w, m)
    away_halo = swap(away, "az", 1)
    away, azimuth_chirp = lax.optimization_barrier((away, azimuth_chirp))
    a = azimuth_weights(azimuth_chirp)
    part, mid_part = focus_outer(a, near, away, raw_echo.shape[1] // CHUNK - 2)
    far_mid, part = lax.optimization_barrier((far_mid, part))
    mid = compress("mid", shifted, core_mid, far_mid, w, m)
    image, part = focus_mid(a, mid, part, mid_part)
    image = focus_end("near", a, part, near_halo, image)
    return focus_end("away", a, part, away_halo, image)


def solution(mesh):
    placed = (P(None, "az", "rg"), P(), P(None, "rg"), P("rg"), P("rg", None, None))
    return jax.shard_map(
        per_device, mesh=mesh, in_specs=placed, out_specs=P(None, "az", "rg"), check_vma=False
    )
```

```python
import functools

import jax
import jax.numpy as jnp
from jax import lax
from jax.experimental import pallas as pl
from jax.experimental.pallas import tpu as pltpu
from jax.sharding import PartitionSpec as P

MAXS = 60
LANES = 128
HALF = 64
CHUNK = 256
PAD = 16
VMEM_LIMIT = 20 * 1024 * 1024
F32 = jnp.float32
BF16 = jnp.bfloat16


def params():
    return pltpu.CompilerParams(vmem_limit_bytes=VMEM_LIMIT)


def whole(shape):
    return pl.BlockSpec(shape, lambda *_: (0,) * len(shape))


def in_hbm(x):
    return pltpu.with_memory_space_constraint(x, pltpu.HBM)


def lane_roll(x):
    return pltpu.roll(x, HALF, 1)


def low_lanes(rows):
    return lax.broadcasted_iota(jnp.int16, (rows, LANES), 1) < HALF


def swap_pairs(count, first):
    pairs = []
    for i in range(first, count - 1, 2):
        pairs += [(i, i + 1), (i + 1, i)]
    return pairs


def swap(x, axis, first):
    return lax.ppermute(x, axis, swap_pairs(lax.axis_size(axis), first))


def by_parity(axis, body):
    odd = lax.rem(lax.axis_index(axis), 2)
    pl.when(odd == 0)(lambda: body(0))
    pl.when(odd == 1)(lambda: body(1))


def shifted_rows(row, lead, width):
    taps = row.shape[1]
    padded = jnp.concatenate([row, jnp.zeros((1, width - taps), F32)], axis=1)
    return pltpu.roll(
        jnp.broadcast_to(padded, (LANES, width)), lead, 1, stride=1, stride_axis=0
    )


def range_toeplitz(range_ref, w_ref):
    depth = w_ref.shape[0] // 2
    real = shifted_rows(range_ref[0:1, :].astype(F32), 0, depth)
    imag = shifted_rows(range_ref[1:2, :].astype(F32), 0, depth)
    real_t, imag_t = real.T.astype(BF16), imag.T.astype(BF16)
    w_ref[0:depth, 0:LANES] = real_t
    w_ref[0:depth, LANES:] = -imag_t
    w_ref[depth:, 0:LANES] = imag_t
    w_ref[depth:, LANES:] = real_t


def migration_bands(taps_ref, shift_ref, m_ref):
    span = m_ref.shape[1]
    blocks = m_ref.shape[0]
    cells = taps_ref.shape[1]
    tap_count = taps_ref.shape[0]
    first = lax.axis_index("rg") * cells - HALF
    total = lax.axis_size("rg") * cells
    for b in range(blocks):
        source = lax.broadcasted_iota(jnp.int32, (span, LANES), 0)
        column = lax.broadcasted_iota(jnp.int32, (span, LANES), 1)
        tap = source - column - (HALF - tap_count // 2) - shift_ref[b][:1, :]
        place = source + first + b * LANES
        tap = jnp.where((place >= 0) & (place < total), tap, -1)
        matrix = jnp.zeros((span, LANES), F32)
        for k in range(tap_count):
            row = taps_ref[k : k + 1, b * LANES : (b + 1) * LANES].astype(F32)
            matrix = jnp.where(tap == k, row, matrix)
        m_ref[b] = matrix.astype(BF16)


def range_weights_kernel(range_ref, taps_ref, splat_ref, w_ref, m_ref):
    range_toeplitz(range_ref, w_ref)
    migration_bands(taps_ref, splat_ref, m_ref)


def range_weights(range_chirp, migration_taps, splat):
    depth = range_chirp.shape[1] + LANES
    return pl.pallas_call(
        range_weights_kernel,
        out_shape=(
            jax.ShapeDtypeStruct((2 * depth, 2 * LANES), BF16),
            jax.ShapeDtypeStruct((splat.shape[0], 2 * LANES, LANES), BF16),
        ),
        in_specs=[pl.BlockSpec(memory_space=pltpu.VMEM)] * 3,
        out_specs=(pl.BlockSpec(memory_space=pltpu.VMEM),) * 2,
        compiler_params=params(),
        name="range_weights",
    )(range_chirp, migration_taps, splat)


def azimuth_weights_kernel(azimuth_ref, a_ref):
    steps, blocks, depth = a_ref.shape[0], a_ref.shape[1], a_ref.shape[3]
    gap = jnp.zeros((LANES, LANES), BF16)
    for b in range(blocks):
        for part in range(2):
            row = azimuth_ref[b, part : part + 1, :].astype(F32)
            rows = shifted_rows(row, 0, steps * depth - LANES).astype(BF16)
            upper = jnp.concatenate([rows, gap], axis=1)
            lower = jnp.concatenate([gap, rows], axis=1)
            base = part * CHUNK
            for k in range(steps):
                a_ref[k, b, base : base + LANES] = upper[:, k * depth : (k + 1) * depth]
                a_ref[k, b, base + LANES : base + CHUNK] = lower[:, k * depth : (k + 1) * depth]


def azimuth_weights(azimuth_chirp):
    blocks = azimuth_chirp.shape[0]
    steps = (azimuth_chirp.shape[2] + CHUNK) // CHUNK
    return pl.pallas_call(
        azimuth_weights_kernel,
        out_shape=jax.ShapeDtypeStruct((steps, blocks, 2 * CHUNK, CHUNK), BF16),
        in_specs=[pl.BlockSpec(memory_space=pltpu.VMEM)],
        out_specs=pl.BlockSpec(memory_space=pltpu.VMEM),
        compiler_params=params(),
        name="azimuth_weights",
    )(azimuth_chirp)


def tile_of(t):
    return slice(t * LANES, (t + 1) * LANES)


def edge_chunk(x_ref, s_ref, start, targets):
    picked = pl.ds(start, CHUNK)
    half = CHUNK // 2
    low, low_half = low_lanes(CHUNK), low_lanes(half)
    count = x_ref.shape[2] // LANES
    for part in range(2):
        cells = [x_ref[part, picked, tile_of(t)] for t in range(count)]
        rolled = [lane_roll(c) for c in cells]
        tiles = [rolled[0]]
        tiles += [jnp.where(low, rolled[t], rolled[t + 1]) for t in range(count - 1)]
        tiles += [rolled[-1]]
        for t, tile in enumerate(tiles):
            s_ref[part, picked, tile_of(t)] = tile
        for out_ref, chunk, side in targets:
            inner = (1, 2) if side == 0 else (count - 2, count - 1)
            for i, t in enumerate(inner):
                at = (2 * part + i) * CHUNK
                out_ref[chunk, at : at + CHUNK, :] = tiles[t]
            at = 4 * CHUNK + part * half
            if side == 0:
                packed = jnp.where(low_half, cells[0][:half], rolled[0][half:])
            else:
                packed = jnp.where(low_half, rolled[-1][:half], cells[-1][half:])
            out_ref[chunk, at : at + half, :] = packed


def near_away_rows(rows):
    odd = lax.rem(lax.axis_index("az"), 2)
    last = rows - CHUNK
    near = pl.multiple_of((1 - odd) * last, CHUNK)
    away = pl.multiple_of(odd * last, CHUNK)
    return near, away


def edges_kernel(
    x_hbm, range_hbm, taps_hbm, shift_hbm, azimuth_hbm,
    s_ref, far_near_ref, far_away_ref, far_mid_ref, core_outer_ref, core_mid_ref,
    range_ref, taps_ref, splat_ref, azimuth_ref, x_ref, shift_ref, sems,
):
    rows = x_ref.shape[1]
    near, away = near_away_rows(rows)
    starts = [near, away] + list(range(CHUNK, rows - CHUNK, CHUNK))
    moves = []
    for start in starts:
        for part in range(2):
            picked = pl.ds(start, CHUNK)
            moves.append((x_hbm.at[part, picked, :], x_ref.at[part, picked, :]))
    large = len(moves)
    moves += [
        (range_hbm, range_ref),
        (taps_hbm, taps_ref),
        (shift_hbm, shift_ref),
        (azimuth_hbm, azimuth_ref),
    ]
    copies = [
        pltpu.make_async_copy(source, target, sems.at[i])
        for i, (source, target) in enumerate(moves)
    ]
    for copy in copies:
        copy.start()
    for ref in (core_outer_ref, core_mid_ref):
        extra = ref.shape[1] - 5 * CHUNK
        ref[:, 5 * CHUNK :, :] = jnp.zeros((ref.shape[0], extra, LANES), BF16)

    def body(odd):
        for i, start in enumerate(starts):
            copies[2 * i].wait()
            copies[2 * i + 1].wait()
            far = [(far_near_ref, 0), (far_away_ref, 0)][i] if i < 2 else (far_mid_ref, i - 2)
            core = (core_outer_ref, i) if i < 2 else (core_mid_ref, i - 2)
            edge_chunk(x_ref, s_ref, start, [core + (1 - odd,), far + (odd,)])

    by_parity("rg", body)
    for copy in copies[large:]:
        copy.wait()
    for b in range(splat_ref.shape[0]):
        splat_ref[b] = jnp.full(splat_ref.shape[1:], shift_ref[b], jnp.int32)


def range_edges(raw, range_chirp, migration_taps, block_shift, azimuth_chirp):
    chunks = raw.shape[1] // CHUNK
    blocks = block_shift.shape[0]
    args = (raw, range_chirp, migration_taps, block_shift, azimuth_chirp)
    return pl.pallas_call(
        edges_kernel,
        out_shape=(jax.ShapeDtypeStruct(raw.shape[:2] + (raw.shape[2] + LANES,), BF16),)
        + tuple(
            jax.ShapeDtypeStruct((n, 5 * CHUNK + extra, LANES), BF16)
            for n, extra in ((1, 0), (1, 0), (chunks - 2, 0), (2, 2 * PAD), (chunks - 2, PAD))
        )
        + (
            jax.ShapeDtypeStruct(range_chirp.shape, BF16),
            jax.ShapeDtypeStruct(migration_taps.shape, BF16),
            jax.ShapeDtypeStruct((blocks, 8, LANES), jnp.int32),
            jax.ShapeDtypeStruct(azimuth_chirp.shape, BF16),
        ),
        in_specs=[pl.BlockSpec(memory_space=pltpu.HBM)] * len(args),
        out_specs=(pl.BlockSpec(memory_space=pltpu.VMEM),) * 10,
        scratch_shapes=[
            pltpu.VMEM(raw.shape, BF16),
            pltpu.SMEM(block_shift.shape, jnp.int32),
            pltpu.SemaphoreType.DMA((2 * chunks + len(args) - 1,)),
        ],
        compiler_params=params(),
        name="range_edges",
    )(*(in_hbm(x) for x in args))


def window_tiles(s_ref, start, left, right, part):
    half = CHUNK // 2
    low = low_lanes(CHUNK)
    picked = pl.ds(start, CHUNK)
    last = s_ref.shape[2] // LANES - 1
    inner = slice(4 * CHUNK + part * half, 4 * CHUNK + (part + 1) * half)

    def full(halo):
        ref, chunk = halo
        return [
            ref[chunk, (2 * part + i) * CHUNK : (2 * part + i + 1) * CHUNK, :] for i in range(2)
        ]

    packed = left[0][left[1], inner, :]
    halo = jnp.concatenate([packed, lane_roll(packed)], axis=0)
    first = jnp.where(low, halo, s_ref[part, picked, tile_of(0)])
    packed = right[0][right[1], inner, :]
    halo = jnp.concatenate([lane_roll(packed), packed], axis=0)
    final = jnp.where(low, s_ref[part, picked, tile_of(last)], halo)
    own = [s_ref[part, picked, tile_of(t)] for t in range(1, last)]
    return full(left) + [first] + own + [final] + full(right)


def compress_chunk(s_ref, start, left, right, w_ref, m_ref, out_ref, out_start, c_ref):
    rows = CHUNK
    taps = w_ref.shape[0] // (2 * LANES)
    tiles = [window_tiles(s_ref, start, left, right, part) for part in range(2)]
    for j in range(c_ref.shape[1] // LANES):
        window = jnp.concatenate(tiles[0][j : j + taps] + tiles[1][j : j + taps], axis=1)
        result = jnp.dot(window, w_ref[...], preferred_element_type=F32).astype(BF16)
        c_ref[0:rows, tile_of(j)] = result[:, :LANES]
        c_ref[rows:, tile_of(j)] = result[:, LANES:]
    for b in range(m_ref.shape[0]):
        window = c_ref[:, b * LANES : b * LANES + 2 * LANES]
        result = jnp.dot(window, m_ref[b], preferred_element_type=F32).astype(BF16)
        out_ref[0, out_start : out_start + rows, tile_of(b)] = result[:rows]
        out_ref[1, out_start : out_start + rows, tile_of(b)] = result[rows:]


def compress_kernel(which, s_ref, core_ref, far_ref, w_ref, m_ref, out_ref, c_ref):
    near, away = near_away_rows(s_ref.shape[1])
    start, chunk = (near, 0) if which == "near" else (away, 1)

    def body(odd):
        core, far = (core_ref, chunk), (far_ref, 0)
        left, right = (core, far) if odd else (far, core)
        compress_chunk(s_ref, start, left, right, w_ref, m_ref, out_ref, 0, c_ref)

    by_parity("rg", body)


def compress(which, shifted, core, far, w, m):
    cells = shifted.shape[2] - LANES
    return pl.pallas_call(
        functools.partial(compress_kernel, which),
        out_shape=jax.ShapeDtypeStruct((2, CHUNK, cells), BF16),
        in_specs=[pl.BlockSpec(memory_space=pltpu.VMEM)] * 5,
        out_specs=pl.BlockSpec(memory_space=pltpu.VMEM),
        scratch_shapes=[pltpu.VMEM((2 * CHUNK, cells + LANES), BF16)],
        compiler_params=params(),
        name="compress_" + which,
    )(shifted, core, far, w, m)


def lines(ref, chunk):
    return lambda part, lanes: ref[part, chunk * CHUNK : (chunk + 1) * CHUNK, lanes]


def correlate_block(a_ref, b, pairs):
    taps = [a_ref[k, b] for k, _ in pairs]
    windows = [
        jnp.concatenate([window(0, tile_of(b)), window(1, tile_of(b))], axis=1)
        for _, window in pairs
    ]
    result = jnp.dot(
        jnp.concatenate(taps, axis=1),
        jnp.concatenate(windows, axis=0),
        preferred_element_type=F32,
    )
    top, bottom = result[:CHUNK], result[CHUNK:]
    return top[:, :LANES] + bottom[:, LANES:], top[:, LANES:] - bottom[:, :LANES]


def focus_outer_kernel(a_ref, near_ref, away_ref, part_ref, mid_part_ref):
    mids, steps, blocks = mid_part_ref.shape[0], a_ref.shape[0], a_ref.shape[1]

    def body(odd):
        first, final = (near_ref, away_ref) if odd else (away_ref, near_ref)
        order = {0: lines(first, 0), mids + 1: lines(final, 0)}
        jobs = [(part_ref.at[0], 0), (part_ref.at[1], mids + 1)]
        jobs += [(mid_part_ref.at[i], i + 1) for i in range(mids)]
        for out_ref, chunk in jobs:
            pairs = [
                (k, order[chunk + k - 1]) for k in range(steps) if chunk + k - 1 in order
            ]
            for b in range(blocks):
                out_ref[0, :, tile_of(b)], out_ref[1, :, tile_of(b)] = correlate_block(
                    a_ref, b, pairs
                )

    by_parity("az", body)


def focus_outer(a, near, away, mids):
    cells = near.shape[2]
    return pl.pallas_call(
        focus_outer_kernel,
        out_shape=(
            jax.ShapeDtypeStruct((2, 2, CHUNK, cells), F32),
            jax.ShapeDtypeStruct((mids, 2, CHUNK, cells), F32),
        ),
        in_specs=[pl.BlockSpec(memory_space=pltpu.VMEM)] * 3,
        out_specs=(pl.BlockSpec(memory_space=pltpu.VMEM),) * 2,
        compiler_params=params(),
        name="focus_outer",
    )(a, near, away)


def middle_kernel(
    s_ref, core_ref, far_ref, w_ref, m_ref, a_ref, part_ref, mid_part_ref, near_ref,
    image_ref, away_part_ref, mid_ref, sum_ref, sems, *c_refs,
):
    mids, steps, blocks = mid_part_ref.shape[0], a_ref.shape[0], a_ref.shape[1]

    def correlate_range(odd):
        for i in range(mids):
            core, far = (core_ref, i), (far_ref, i)
            left, right = (core, far) if odd else (far, core)
            compress_chunk(
                s_ref, CHUNK * (i + 1), left, right, w_ref, m_ref, mid_ref, i * CHUNK, c_refs[i]
            )

    by_parity("rg", correlate_range)

    def correlate_azimuth(odd):
        order = {i + 1: lines(mid_ref, i) for i in range(mids)}
        near_chunk, away_chunk = (0, mids + 1) if odd else (mids + 1, 0)
        order[-1 if odd else mids + 2] = lines(near_ref, 0)
        jobs = [(mid_part_ref.at[i], sum_ref.at[i], i + 1) for i in range(mids)]
        jobs.append((part_ref.at[1 - odd], sum_ref.at[mids], near_chunk))
        jobs.append((part_ref.at[odd], away_part_ref, away_chunk))
        copies = []
        for i, (before_ref, out_ref, chunk) in enumerate(jobs):
            pairs = [(k, order[chunk + k - 1]) for k in range(steps) if chunk + k - 1 in order]
            for b in range(blocks):
                real, imag = correlate_block(a_ref, b, pairs)
                out_ref[0, :, tile_of(b)] = before_ref[0, :, tile_of(b)] + real
                out_ref[1, :, tile_of(b)] = before_ref[1, :, tile_of(b)] + imag
            if i <= mids:
                target = image_ref.at[:, pl.ds(chunk * CHUNK, CHUNK), :]
                copies.append(pltpu.make_async_copy(out_ref, target, sems.at[i]))
                copies[-1].start()
        for copy in copies:
            copy.wait()

    by_parity("az", correlate_azimuth)


def middle(shifted, core, far, w, m, a, part, mid_part, near_halo):
    rows, cells = shifted.shape[1], part.shape[3]
    mids = mid_part.shape[0]
    args = (shifted, core, far, w, m, a, part, mid_part, near_halo)
    return pl.pallas_call(
        middle_kernel,
        out_shape=(
            jax.ShapeDtypeStruct((2, rows, cells), F32),
            jax.ShapeDtypeStruct(part.shape[1:], F32),
        ),
        in_specs=[pl.BlockSpec(memory_space=pltpu.VMEM)] * len(args),
        out_specs=(pl.BlockSpec(memory_space=pl.ANY), pl.BlockSpec(memory_space=pltpu.VMEM)),
        scratch_shapes=[
            pltpu.VMEM((2, mids * CHUNK, cells), BF16),
            pltpu.VMEM((mids + 1, 2, CHUNK, cells), F32),
            pltpu.SemaphoreType.DMA((mids + 1,)),
        ]
        + [pltpu.VMEM((2 * CHUNK, cells + LANES), BF16)] * mids,
        compiler_params=params(),
        name="middle",
    )(*args)


def away_end_kernel(a_ref, part_ref, halo_ref, _, image_ref, sum_ref, sem):
    rows = image_ref.shape[1]

    def body(odd):
        for b in range(a_ref.shape[1]):
            real, imag = correlate_block(a_ref, b, [(2 * odd, lines(halo_ref, 0))])
            sum_ref[0, :, tile_of(b)] = part_ref[0, :, tile_of(b)] + real
            sum_ref[1, :, tile_of(b)] = part_ref[1, :, tile_of(b)] + imag
        target = image_ref.at[:, pl.ds(odd * (rows - CHUNK), CHUNK), :]
        copy = pltpu.make_async_copy(sum_ref, target, sem)
        copy.start()
        copy.wait()

    by_parity("az", body)


def away_end(a, part, halo, image):
    return pl.pallas_call(
        away_end_kernel,
        out_shape=jax.ShapeDtypeStruct(image.shape, F32),
        in_specs=[pl.BlockSpec(memory_space=pltpu.VMEM)] * 3
        + [pl.BlockSpec(memory_space=pl.ANY)],
        out_specs=pl.BlockSpec(memory_space=pl.ANY),
        scratch_shapes=[pltpu.VMEM(part.shape, F32), pltpu.SemaphoreType.DMA],
        input_output_aliases={3: 0},
        compiler_params=params(),
        name="away_end",
    )(a, part, halo, image)


def per_device(raw_echo, range_chirp, migration_taps, block_shift, azimuth_chirp):
    (
        shifted, far_near, far_away, far_mid, core_outer, core_mid,
        range_chirp, migration_taps, splat, azimuth_chirp,
    ) = range_edges(raw_echo, range_chirp, migration_taps, block_shift, azimuth_chirp)
    core_outer = swap(core_outer, "rg", 0)
    core_mid = swap(core_mid, "rg", 0)
    far_near = swap(far_near, "rg", 1)
    far_away = swap(far_away, "rg", 1)
    far_mid = swap(far_mid, "rg", 1)
    w, m = range_weights(range_chirp, migration_taps, splat)
    near = compress("near", shifted, core_outer, far_near, w, m)
    near_halo = swap(near, "az", 0)
    core_outer, core_mid, near = lax.optimization_barrier((core_outer, core_mid, near))
    away = compress("away", shifted, core_outer, far_away, w, m)
    away_halo = swap(away, "az", 1)
    away, azimuth_chirp = lax.optimization_barrier((away, azimuth_chirp))
    a = azimuth_weights(azimuth_chirp)
    part, mid_part = focus_outer(a, near, away, raw_echo.shape[1] // CHUNK - 2)
    far_mid, part = lax.optimization_barrier((far_mid, part))
    image, part = middle(shifted, core_mid, far_mid, w, m, a, part, mid_part, near_halo)
    return away_end(a, part, away_halo, image)


def solution(mesh):
    placed = (P(None, "az", "rg"), P(), P(None, "rg"), P("rg"), P("rg", None, None))
    return jax.shard_map(
        per_device, mesh=mesh, in_specs=placed, out_specs=P(None, "az", "rg"), check_vma=False
    )
```

```python
import functools

import jax
import jax.numpy as jnp
from jax import lax
from jax.experimental import pallas as pl
from jax.experimental.pallas import tpu as pltpu
from jax.sharding import PartitionSpec as P

MAXS = 60
LANES = 128
HALF = 64
CHUNK = 256
PAD = 16
VMEM_LIMIT = 20 * 1024 * 1024
F32 = jnp.float32
BF16 = jnp.bfloat16


def params():
    return pltpu.CompilerParams(vmem_limit_bytes=VMEM_LIMIT)


def whole(shape):
    return pl.BlockSpec(shape, lambda *_: (0,) * len(shape))


def in_hbm(x):
    return pltpu.with_memory_space_constraint(x, pltpu.HBM)


def lane_roll(x):
    return pltpu.roll(x, HALF, 1)


def low_lanes(rows):
    return lax.broadcasted_iota(jnp.int16, (rows, LANES), 1) < HALF


def swap_pairs(count, first):
    pairs = []
    for i in range(first, count - 1, 2):
        pairs += [(i, i + 1), (i + 1, i)]
    return pairs


def swap(x, axis, first):
    return lax.ppermute(x, axis, swap_pairs(lax.axis_size(axis), first))


def by_parity(axis, body):
    odd = lax.rem(lax.axis_index(axis), 2)
    pl.when(odd == 0)(lambda: body(0))
    pl.when(odd == 1)(lambda: body(1))


def shifted_rows(row, lead, width):
    taps = row.shape[1]
    padded = jnp.concatenate([row, jnp.zeros((1, width - taps), F32)], axis=1)
    return pltpu.roll(
        jnp.broadcast_to(padded, (LANES, width)), lead, 1, stride=1, stride_axis=0
    )


def range_toeplitz(range_ref, w_ref):
    depth = w_ref.shape[0] // 2
    real = shifted_rows(range_ref[0:1, :].astype(F32), 0, depth)
    imag = shifted_rows(range_ref[1:2, :].astype(F32), 0, depth)
    real_t, imag_t = real.T.astype(BF16), imag.T.astype(BF16)
    w_ref[0:depth, 0:LANES] = real_t
    w_ref[0:depth, LANES:] = -imag_t
    w_ref[depth:, 0:LANES] = imag_t
    w_ref[depth:, LANES:] = real_t


def migration_bands(taps_ref, shift_ref, m_ref):
    span = m_ref.shape[1]
    blocks = m_ref.shape[0]
    cells = taps_ref.shape[1]
    tap_count = taps_ref.shape[0]
    first = lax.axis_index("rg") * cells - HALF
    total = lax.axis_size("rg") * cells
    for b in range(blocks):
        source = lax.broadcasted_iota(jnp.int32, (span, LANES), 0)
        column = lax.broadcasted_iota(jnp.int32, (span, LANES), 1)
        tap = source - column - (HALF - tap_count // 2) - shift_ref[b][:1, :]
        place = source + first + b * LANES
        tap = jnp.where((place >= 0) & (place < total), tap, -1)
        matrix = jnp.zeros((span, LANES), F32)
        for k in range(tap_count):
            row = taps_ref[k : k + 1, b * LANES : (b + 1) * LANES].astype(F32)
            matrix = jnp.where(tap == k, row, matrix)
        m_ref[b] = matrix.astype(BF16)


def azimuth_weights_kernel(azimuth_ref, a_ref):
    steps, blocks, depth = a_ref.shape[0], a_ref.shape[1], a_ref.shape[3]
    gap = jnp.zeros((LANES, LANES), BF16)
    for b in range(blocks):
        for part in range(2):
            row = azimuth_ref[b, part : part + 1, :].astype(F32)
            rows = shifted_rows(row, 0, steps * depth - LANES).astype(BF16)
            upper = jnp.concatenate([rows, gap], axis=1)
            lower = jnp.concatenate([gap, rows], axis=1)
            base = part * CHUNK
            for k in range(steps):
                a_ref[k, b, base : base + LANES] = upper[:, k * depth : (k + 1) * depth]
                a_ref[k, b, base + LANES : base + CHUNK] = lower[:, k * depth : (k + 1) * depth]


def azimuth_weights(azimuth_chirp):
    blocks = azimuth_chirp.shape[0]
    steps = (azimuth_chirp.shape[2] + CHUNK) // CHUNK
    return pl.pallas_call(
        azimuth_weights_kernel,
        out_shape=jax.ShapeDtypeStruct((steps, blocks, 2 * CHUNK, CHUNK), BF16),
        in_specs=[pl.BlockSpec(memory_space=pltpu.VMEM)],
        out_specs=pl.BlockSpec(memory_space=pltpu.VMEM),
        compiler_params=params(),
        name="azimuth_weights",
    )(azimuth_chirp)


def tile_of(t):
    return slice(t * LANES, (t + 1) * LANES)


def edge_chunk(x_ref, s_ref, start, targets):
    picked = pl.ds(start, CHUNK)
    half = CHUNK // 2
    low, low_half = low_lanes(CHUNK), low_lanes(half)
    count = x_ref.shape[2] // LANES
    for part in range(2):
        cells = [x_ref[part, picked, tile_of(t)] for t in range(count)]
        rolled = [lane_roll(c) for c in cells]
        tiles = [rolled[0]]
        tiles += [jnp.where(low, rolled[t], rolled[t + 1]) for t in range(count - 1)]
        tiles += [rolled[-1]]
        for t, tile in enumerate(tiles):
            s_ref[part, picked, tile_of(t)] = tile
        for out_ref, chunk, side in targets:
            inner = (1, 2) if side == 0 else (count - 2, count - 1)
            for i, t in enumerate(inner):
                at = (2 * part + i) * CHUNK
                out_ref[chunk, at : at + CHUNK, :] = tiles[t]
            at = 4 * CHUNK + part * half
            if side == 0:
                packed = jnp.where(low_half, cells[0][:half], rolled[0][half:])
            else:
                packed = jnp.where(low_half, rolled[-1][:half], cells[-1][half:])
            out_ref[chunk, at : at + half, :] = packed


def near_away_rows(rows):
    odd = lax.rem(lax.axis_index("az"), 2)
    last = rows - CHUNK
    near = pl.multiple_of((1 - odd) * last, CHUNK)
    away = pl.multiple_of(odd * last, CHUNK)
    return near, away


def edges_kernel(
    x_hbm, range_hbm, taps_hbm, shift_hbm, azimuth_hbm,
    s_ref, far_near_ref, far_away_ref, far_mid_ref, core_outer_ref, core_mid_ref,
    w_ref, taps_ref, splat_ref, azimuth_ref, x_ref, range_ref, shift_ref, sems,
):
    rows = x_ref.shape[1]
    near, away = near_away_rows(rows)
    starts = [near, away] + list(range(CHUNK, rows - CHUNK, CHUNK))
    moves = [
        (range_hbm, range_ref),
        (taps_hbm, taps_ref),
        (shift_hbm, shift_ref),
        (azimuth_hbm, azimuth_ref),
    ]
    small = len(moves)
    for start in starts:
        picked = pl.ds(start, CHUNK)
        moves.append((x_hbm.at[:, picked, :], x_ref.at[:, picked, :]))
    copies = [
        pltpu.make_async_copy(source, target, sems.at[i])
        for i, (source, target) in enumerate(moves)
    ]
    for copy in copies:
        copy.start()
    for copy in copies[:small]:
        copy.wait()
    for ref in (core_outer_ref, core_mid_ref):
        extra = ref.shape[1] - 5 * CHUNK
        ref[:, 5 * CHUNK :, :] = jnp.zeros((ref.shape[0], extra, LANES), BF16)
    range_toeplitz(range_ref, w_ref)
    for b in range(splat_ref.shape[0]):
        splat_ref[b] = jnp.full(splat_ref.shape[1:], shift_ref[b], jnp.int32)

    def body(odd):
        for i, start in enumerate(starts):
            copies[small + i].wait()
            far = [(far_near_ref, 0), (far_away_ref, 0)][i] if i < 2 else (far_mid_ref, i - 2)
            core = (core_outer_ref, i) if i < 2 else (core_mid_ref, i - 2)
            edge_chunk(x_ref, s_ref, start, [core + (1 - odd,), far + (odd,)])

    by_parity("rg", body)


def range_edges(raw, range_chirp, migration_taps, block_shift, azimuth_chirp):
    chunks = raw.shape[1] // CHUNK
    blocks = block_shift.shape[0]
    depth = range_chirp.shape[1] + LANES
    args = (raw, range_chirp, migration_taps, block_shift, azimuth_chirp)
    return pl.pallas_call(
        edges_kernel,
        out_shape=(jax.ShapeDtypeStruct(raw.shape[:2] + (raw.shape[2] + LANES,), BF16),)
        + tuple(
            jax.ShapeDtypeStruct((n, 5 * CHUNK + extra, LANES), BF16)
            for n, extra in ((1, 0), (1, 0), (chunks - 2, 0), (2, 2 * PAD), (chunks - 2, PAD))
        )
        + (
            jax.ShapeDtypeStruct((2 * depth, 2 * LANES), BF16),
            jax.ShapeDtypeStruct(migration_taps.shape, BF16),
            jax.ShapeDtypeStruct((blocks, 8, LANES), jnp.int32),
            jax.ShapeDtypeStruct(azimuth_chirp.shape, BF16),
        ),
        in_specs=[pl.BlockSpec(memory_space=pltpu.HBM)] * len(args),
        out_specs=(pl.BlockSpec(memory_space=pltpu.VMEM),) * 10,
        scratch_shapes=[
            pltpu.VMEM(raw.shape, BF16),
            pltpu.VMEM(range_chirp.shape, BF16),
            pltpu.SMEM(block_shift.shape, jnp.int32),
            pltpu.SemaphoreType.DMA((chunks + len(args) - 1,)),
        ],
        compiler_params=params(),
        name="range_edges",
    )(*(in_hbm(x) for x in args))


def window_tiles(s_ref, start, left, right, part):
    half = CHUNK // 2
    low = low_lanes(CHUNK)
    picked = pl.ds(start, CHUNK)
    last = s_ref.shape[2] // LANES - 1
    inner = slice(4 * CHUNK + part * half, 4 * CHUNK + (part + 1) * half)

    def full(halo):
        ref, chunk = halo
        return [
            ref[chunk, (2 * part + i) * CHUNK : (2 * part + i + 1) * CHUNK, :] for i in range(2)
        ]

    packed = left[0][left[1], inner, :]
    halo = jnp.concatenate([packed, lane_roll(packed)], axis=0)
    first = jnp.where(low, halo, s_ref[part, picked, tile_of(0)])
    packed = right[0][right[1], inner, :]
    halo = jnp.concatenate([lane_roll(packed), packed], axis=0)
    final = jnp.where(low, s_ref[part, picked, tile_of(last)], halo)
    own = [s_ref[part, picked, tile_of(t)] for t in range(1, last)]
    return full(left) + [first] + own + [final] + full(right)


def compress_chunk(s_ref, start, left, right, w_ref, m_ref, out_ref, out_start, c_ref):
    rows = CHUNK
    taps = w_ref.shape[0] // (2 * LANES)
    tiles = [window_tiles(s_ref, start, left, right, part) for part in range(2)]
    for j in range(c_ref.shape[1] // LANES):
        window = jnp.concatenate(tiles[0][j : j + taps] + tiles[1][j : j + taps], axis=1)
        result = jnp.dot(window, w_ref[...], preferred_element_type=F32).astype(BF16)
        c_ref[0:rows, tile_of(j)] = result[:, :LANES]
        c_ref[rows:, tile_of(j)] = result[:, LANES:]
    for b in range(m_ref.shape[0]):
        window = c_ref[:, b * LANES : b * LANES + 2 * LANES]
        result = jnp.dot(window, m_ref[b], preferred_element_type=F32).astype(BF16)
        out_ref[0, out_start : out_start + rows, tile_of(b)] = result[:rows]
        out_ref[1, out_start : out_start + rows, tile_of(b)] = result[rows:]


def compress_kernel(which, s_ref, core_ref, far_ref, w_ref, *refs):
    near, away = near_away_rows(s_ref.shape[1])
    if which == "near":
        taps_ref, splat_ref, out_ref, m_ref, *c_refs = refs
        jobs = [(near, 0)]
    else:
        m_ref, out_ref, *c_refs = refs
        jobs = [(CHUNK * (i + 1), i) for i in range(out_ref.shape[1] // CHUNK)]
        if which == "away":
            jobs = [(away, 1)]

    def body(odd):
        if which == "near":
            migration_bands(taps_ref, splat_ref, m_ref)
        for i, (start, chunk) in enumerate(jobs):
            core, far = (core_ref, chunk), (far_ref, chunk if which == "mid" else 0)
            left, right = (core, far) if odd else (far, core)
            compress_chunk(
                s_ref, start, left, right, w_ref, m_ref, out_ref, i * CHUNK, c_refs[i]
            )

    by_parity("rg", body)


def compress(which, shifted, core, far, w, *bands):
    rows, cells = shifted.shape[1], shifted.shape[2] - LANES
    count = rows // CHUNK - 2 if which == "mid" else 1
    args = (shifted, core, far, w) + bands
    out = (jax.ShapeDtypeStruct((2, count * CHUNK, cells), BF16),)
    if which == "near":
        out += (jax.ShapeDtypeStruct((cells // LANES, 2 * LANES, LANES), BF16),)
    result = pl.pallas_call(
        functools.partial(compress_kernel, which),
        out_shape=out,
        in_specs=[pl.BlockSpec(memory_space=pltpu.VMEM)] * len(args),
        out_specs=(pl.BlockSpec(memory_space=pltpu.VMEM),) * len(out),
        scratch_shapes=[pltpu.VMEM((2 * CHUNK, cells + LANES), BF16)] * count,
        compiler_params=params(),
        name="compress_" + which,
    )(*args)
    return result if which == "near" else result[0]


def lines(ref, chunk):
    return lambda part, lanes: ref[part, chunk * CHUNK : (chunk + 1) * CHUNK, lanes]


def correlate_block(a_ref, b, pairs):
    taps = [a_ref[k, b] for k, _ in pairs]
    windows = [
        jnp.concatenate([window(0, tile_of(b)), window(1, tile_of(b))], axis=1)
        for _, window in pairs
    ]
    result = jnp.dot(
        jnp.concatenate(taps, axis=1),
        jnp.concatenate(windows, axis=0),
        preferred_element_type=F32,
    )
    top, bottom = result[:CHUNK], result[CHUNK:]
    return top[:, :LANES] + bottom[:, LANES:], top[:, LANES:] - bottom[:, :LANES]


def focus_outer_kernel(a_ref, near_ref, away_ref, part_ref, mid_part_ref):
    mids, steps, blocks = mid_part_ref.shape[0], a_ref.shape[0], a_ref.shape[1]

    def body(odd):
        first, final = (near_ref, away_ref) if odd else (away_ref, near_ref)
        order = {0: lines(first, 0), mids + 1: lines(final, 0)}
        jobs = [(part_ref.at[0], 0), (part_ref.at[1], mids + 1)]
        jobs += [(mid_part_ref.at[i], i + 1) for i in range(mids)]
        for out_ref, chunk in jobs:
            pairs = [
                (k, order[chunk + k - 1]) for k in range(steps) if chunk + k - 1 in order
            ]
            for b in range(blocks):
                out_ref[0, :, tile_of(b)], out_ref[1, :, tile_of(b)] = correlate_block(
                    a_ref, b, pairs
                )

    by_parity("az", body)


def focus_outer(a, near, away, mids):
    cells = near.shape[2]
    return pl.pallas_call(
        focus_outer_kernel,
        out_shape=(
            jax.ShapeDtypeStruct((2, 2, CHUNK, cells), F32),
            jax.ShapeDtypeStruct((mids, 2, CHUNK, cells), F32),
        ),
        in_specs=[pl.BlockSpec(memory_space=pltpu.VMEM)] * 3,
        out_specs=(pl.BlockSpec(memory_space=pltpu.VMEM),) * 2,
        compiler_params=params(),
        name="focus_outer",
    )(a, near, away)


def focus_mid_kernel(a_ref, mid_ref, part_ref, mid_part_ref, image_ref, end_ref, sum_ref, sems):
    mids, steps, blocks = mid_part_ref.shape[0], a_ref.shape[0], a_ref.shape[1]
    order = {i + 1: lines(mid_ref, i) for i in range(mids)}
    jobs = [(mid_part_ref.at[i], sum_ref.at[i], i + 1) for i in range(mids)]
    jobs += [(part_ref.at[0], end_ref.at[0], 0), (part_ref.at[1], end_ref.at[1], mids + 1)]
    copies = []
    for i, (before_ref, out_ref, chunk) in enumerate(jobs):
        pairs = [(k, order[chunk + k - 1]) for k in range(steps) if chunk + k - 1 in order]
        for b in range(blocks):
            real, imag = correlate_block(a_ref, b, pairs)
            out_ref[0, :, tile_of(b)] = before_ref[0, :, tile_of(b)] + real
            out_ref[1, :, tile_of(b)] = before_ref[1, :, tile_of(b)] + imag
        if i < mids:
            target = image_ref.at[:, pl.ds(chunk * CHUNK, CHUNK), :]
            copies.append(pltpu.make_async_copy(out_ref, target, sems.at[i]))
            copies[-1].start()
    for copy in copies:
        copy.wait()


def focus_mid(a, mid, part, mid_part):
    cells = mid.shape[2]
    mids = mid_part.shape[0]
    return pl.pallas_call(
        focus_mid_kernel,
        out_shape=(
            jax.ShapeDtypeStruct((2, (mids + 2) * CHUNK, cells), F32),
            jax.ShapeDtypeStruct(part.shape, F32),
        ),
        in_specs=[pl.BlockSpec(memory_space=pltpu.VMEM)] * 4,
        out_specs=(pl.BlockSpec(memory_space=pl.ANY), pl.BlockSpec(memory_space=pltpu.VMEM)),
        scratch_shapes=[pltpu.VMEM(mid_part.shape, F32), pltpu.SemaphoreType.DMA((mids,))],
        compiler_params=params(),
        name="focus_mid",
    )(a, mid, part, mid_part)


def add_halo(a_ref, end, part_ref, halo_ref, out_ref):
    for b in range(a_ref.shape[1]):
        real, imag = correlate_block(a_ref, b, [(2 * end, lines(halo_ref, 0))])
        out_ref[0, :, tile_of(b)] = part_ref[end, 0, :, tile_of(b)] + real
        out_ref[1, :, tile_of(b)] = part_ref[end, 1, :, tile_of(b)] + imag


def near_end_kernel(a_ref, part_ref, halo_ref, out_ref):
    by_parity("az", lambda odd: add_halo(a_ref, 1 - odd, part_ref, halo_ref, out_ref))


def near_end(a, part, halo):
    return pl.pallas_call(
        near_end_kernel,
        out_shape=jax.ShapeDtypeStruct(part.shape[1:], F32),
        in_specs=[pl.BlockSpec(memory_space=pltpu.VMEM)] * 3,
        out_specs=pl.BlockSpec(memory_space=pltpu.VMEM),
        compiler_params=params(),
        name="near_end",
    )(a, part, halo)


def ends_kernel(a_ref, part_ref, near_ref, halo_ref, _, image_ref, sum_ref, sems):
    rows = image_ref.shape[1]

    def body(odd):
        copies = []
        for i, (source, end) in enumerate(((near_ref, 1 - odd), (sum_ref, odd))):
            if i == 1:
                add_halo(a_ref, end, part_ref, halo_ref, sum_ref)
            target = image_ref.at[:, pl.ds(end * (rows - CHUNK), CHUNK), :]
            copies.append(pltpu.make_async_copy(source, target, sems.at[i]))
            copies[-1].start()
        for copy in copies:
            copy.wait()

    by_parity("az", body)


def ends(a, part, near, halo, image):
    return pl.pallas_call(
        ends_kernel,
        out_shape=jax.ShapeDtypeStruct(image.shape, F32),
        in_specs=[pl.BlockSpec(memory_space=pltpu.VMEM)] * 4
        + [pl.BlockSpec(memory_space=pl.ANY)],
        out_specs=pl.BlockSpec(memory_space=pl.ANY),
        scratch_shapes=[pltpu.VMEM(near.shape, F32), pltpu.SemaphoreType.DMA((2,))],
        input_output_aliases={4: 0},
        compiler_params=params(),
        name="ends",
    )(a, part, near, halo, image)


def per_device(raw_echo, range_chirp, migration_taps, block_shift, azimuth_chirp):
    shifted, far_near, far_away, far_mid, core_outer, core_mid, w, taps, splat, azimuth_chirp = range_edges(
        raw_echo, range_chirp, migration_taps, block_shift, azimuth_chirp
    )
    core_outer = swap(core_outer, "rg", 0)
    core_mid = swap(core_mid, "rg", 0)
    far_near = swap(far_near, "rg", 1)
    far_away = swap(far_away, "rg", 1)
    far_mid = swap(far_mid, "rg", 1)
    near, m = compress("near", shifted, core_outer, far_near, w, taps, splat)
    near_halo = swap(near, "az", 0)
    core_outer, core_mid, near = lax.optimization_barrier((core_outer, core_mid, near))
    away = compress("away", shifted, core_outer, far_away, w, m)
    away_halo = swap(away, "az", 1)
    away, azimuth_chirp = lax.optimization_barrier((away, azimuth_chirp))
    a = azimuth_weights(azimuth_chirp)
    part, mid_part = focus_outer(a, near, away, raw_echo.shape[1] // CHUNK - 2)
    far_mid, part = lax.optimization_barrier((far_mid, part))
    mid = compress("mid", shifted, core_mid, far_mid, w, m)
    image, part = focus_mid(a, mid, part, mid_part)
    return ends(a, part, near_end(a, part, near_halo), away_halo, image)


def solution(mesh):
    placed = (P(None, "az", "rg"), P(), P(None, "rg"), P("rg"), P("rg", None, None))
    return jax.shard_map(
        per_device, mesh=mesh, in_specs=placed, out_specs=P(None, "az", "rg"), check_vma=False
    )
```

```python
import functools

import jax
import jax.numpy as jnp
from jax import lax
from jax.experimental import pallas as pl
from jax.experimental.pallas import tpu as pltpu
from jax.sharding import PartitionSpec as P

MAXS = 60
LANES = 128
HALF = 64
CHUNK = 256
PAD = 16
VMEM_LIMIT = 20 * 1024 * 1024
F32 = jnp.float32
BF16 = jnp.bfloat16


def params():
    return pltpu.CompilerParams(vmem_limit_bytes=VMEM_LIMIT)


def whole(shape):
    return pl.BlockSpec(shape, lambda *_: (0,) * len(shape))


def in_hbm(x):
    return pltpu.with_memory_space_constraint(x, pltpu.HBM)


def lane_roll(x):
    return pltpu.roll(x, HALF, 1)


def low_lanes(rows):
    return lax.broadcasted_iota(jnp.int16, (rows, LANES), 1) < HALF


def swap_pairs(count, first):
    pairs = []
    for i in range(first, count - 1, 2):
        pairs += [(i, i + 1), (i + 1, i)]
    return pairs


def swap(x, axis, first):
    return lax.ppermute(x, axis, swap_pairs(lax.axis_size(axis), first))


def by_parity(axis, body):
    odd = lax.rem(lax.axis_index(axis), 2)
    pl.when(odd == 0)(lambda: body(0))
    pl.when(odd == 1)(lambda: body(1))


def shifted_rows(row, lead, width):
    taps = row.shape[1]
    padded = jnp.concatenate([row, jnp.zeros((1, width - taps), F32)], axis=1)
    return pltpu.roll(
        jnp.broadcast_to(padded, (LANES, width)), lead, 1, stride=1, stride_axis=0
    )


def range_toeplitz(range_ref, w_ref):
    depth = w_ref.shape[0] // 2
    real = shifted_rows(range_ref[0:1, :].astype(F32), 0, depth)
    imag = shifted_rows(range_ref[1:2, :].astype(F32), 0, depth)
    real_t, imag_t = real.T.astype(BF16), imag.T.astype(BF16)
    w_ref[0:depth, 0:LANES] = real_t
    w_ref[0:depth, LANES:] = -imag_t
    w_ref[depth:, 0:LANES] = imag_t
    w_ref[depth:, LANES:] = real_t


def migration_bands(taps_ref, shift_ref, m_ref):
    span = m_ref.shape[1]
    blocks = m_ref.shape[0]
    cells = taps_ref.shape[1]
    tap_count = taps_ref.shape[0]
    first = lax.axis_index("rg") * cells - HALF
    total = lax.axis_size("rg") * cells
    for b in range(blocks):
        source = lax.broadcasted_iota(jnp.int32, (span, LANES), 0)
        column = lax.broadcasted_iota(jnp.int32, (span, LANES), 1)
        tap = source - column - (HALF - tap_count // 2) - shift_ref[b][:1, :]
        place = source + first + b * LANES
        tap = jnp.where((place >= 0) & (place < total), tap, -1)
        matrix = jnp.zeros((span, LANES), F32)
        for k in range(tap_count):
            row = taps_ref[k : k + 1, b * LANES : (b + 1) * LANES].astype(F32)
            matrix = jnp.where(tap == k, row, matrix)
        m_ref[b] = matrix.astype(BF16)


def azimuth_weights_kernel(azimuth_ref, a_ref):
    steps, blocks, depth = a_ref.shape[0], a_ref.shape[1], a_ref.shape[3]
    gap = jnp.zeros((LANES, LANES), BF16)
    for b in range(blocks):
        for part in range(2):
            row = azimuth_ref[b, part : part + 1, :].astype(F32)
            rows = shifted_rows(row, 0, steps * depth - LANES).astype(BF16)
            upper = jnp.concatenate([rows, gap], axis=1)
            lower = jnp.concatenate([gap, rows], axis=1)
            base = part * CHUNK
            for k in range(steps):
                a_ref[k, b, base : base + LANES] = upper[:, k * depth : (k + 1) * depth]
                a_ref[k, b, base + LANES : base + CHUNK] = lower[:, k * depth : (k + 1) * depth]


def azimuth_weights(azimuth_chirp):
    blocks = azimuth_chirp.shape[0]
    steps = (azimuth_chirp.shape[2] + CHUNK) // CHUNK
    return pl.pallas_call(
        azimuth_weights_kernel,
        out_shape=jax.ShapeDtypeStruct((steps, blocks, 2 * CHUNK, CHUNK), BF16),
        in_specs=[pl.BlockSpec(memory_space=pltpu.VMEM)],
        out_specs=pl.BlockSpec(memory_space=pltpu.VMEM),
        compiler_params=params(),
        name="azimuth_weights",
    )(azimuth_chirp)


def tile_of(t):
    return slice(t * LANES, (t + 1) * LANES)


def edge_chunk(x_ref, s_ref, start, targets):
    picked = pl.ds(start, CHUNK)
    half = CHUNK // 2
    low, low_half = low_lanes(CHUNK), low_lanes(half)
    count = x_ref.shape[2] // LANES
    for part in range(2):
        cells = [x_ref[part, picked, tile_of(t)] for t in range(count)]
        rolled = [lane_roll(c) for c in cells]
        tiles = [rolled[0]]
        tiles += [jnp.where(low, rolled[t], rolled[t + 1]) for t in range(count - 1)]
        tiles += [rolled[-1]]
        for t, tile in enumerate(tiles):
            s_ref[part, picked, tile_of(t)] = tile
        for out_ref, chunk, side in targets:
            inner = (1, 2) if side == 0 else (count - 2, count - 1)
            for i, t in enumerate(inner):
                at = (2 * part + i) * CHUNK
                out_ref[chunk, at : at + CHUNK, :] = tiles[t]
            at = 4 * CHUNK + part * half
            if side == 0:
                packed = jnp.where(low_half, cells[0][:half], rolled[0][half:])
            else:
                packed = jnp.where(low_half, rolled[-1][:half], cells[-1][half:])
            out_ref[chunk, at : at + half, :] = packed


def near_away_rows(rows):
    odd = lax.rem(lax.axis_index("az"), 2)
    last = rows - CHUNK
    near = pl.multiple_of((1 - odd) * last, CHUNK)
    away = pl.multiple_of(odd * last, CHUNK)
    return near, away


def edges_kernel(
    x_hbm, range_hbm, taps_hbm, shift_hbm, azimuth_hbm,
    s_ref, far_near_ref, far_away_ref, far_mid_ref, core_outer_ref, core_mid_ref,
    w_ref, taps_ref, splat_ref, azimuth_ref, x_ref, range_ref, shift_ref, sems,
):
    rows = x_ref.shape[1]
    near, away = near_away_rows(rows)
    starts = [near, away] + list(range(CHUNK, rows - CHUNK, CHUNK))
    moves = []
    for start in starts:
        picked = pl.ds(start, CHUNK)
        moves.append((x_hbm.at[:, picked, :], x_ref.at[:, picked, :]))
    moves += [
        (range_hbm, range_ref),
        (shift_hbm, shift_ref),
        (taps_hbm, taps_ref),
        (azimuth_hbm, azimuth_ref),
    ]
    copies = [
        pltpu.make_async_copy(source, target, sems.at[i])
        for i, (source, target) in enumerate(moves)
    ]
    for copy in copies:
        copy.start()
    for copy in copies[len(starts) :]:
        copy.wait()
    for ref in (core_outer_ref, core_mid_ref):
        extra = ref.shape[1] - 5 * CHUNK
        ref[:, 5 * CHUNK :, :] = jnp.zeros((ref.shape[0], extra, LANES), BF16)
    range_toeplitz(range_ref, w_ref)
    for b in range(splat_ref.shape[0]):
        splat_ref[b] = jnp.full(splat_ref.shape[1:], shift_ref[b], jnp.int32)

    def body(odd):
        for i, start in enumerate(starts):
            copies[i].wait()
            far = [(far_near_ref, 0), (far_away_ref, 0)][i] if i < 2 else (far_mid_ref, i - 2)
            core = (core_outer_ref, i) if i < 2 else (core_mid_ref, i - 2)
            edge_chunk(x_ref, s_ref, start, [core + (1 - odd,), far + (odd,)])

    by_parity("rg", body)


def range_edges(raw, range_chirp, migration_taps, block_shift, azimuth_chirp):
    chunks = raw.shape[1] // CHUNK
    blocks = block_shift.shape[0]
    depth = range_chirp.shape[1] + LANES
    args = (raw, range_chirp, migration_taps, block_shift, azimuth_chirp)
    return pl.pallas_call(
        edges_kernel,
        out_shape=(jax.ShapeDtypeStruct(raw.shape[:2] + (raw.shape[2] + LANES,), BF16),)
        + tuple(
            jax.ShapeDtypeStruct((n, 5 * CHUNK + extra, LANES), BF16)
            for n, extra in ((1, 0), (1, 0), (chunks - 2, 0), (2, 2 * PAD), (chunks - 2, PAD))
        )
        + (
            jax.ShapeDtypeStruct((2 * depth, 2 * LANES), BF16),
            jax.ShapeDtypeStruct(migration_taps.shape, BF16),
            jax.ShapeDtypeStruct((blocks, 8, LANES), jnp.int32),
            jax.ShapeDtypeStruct(azimuth_chirp.shape, BF16),
        ),
        in_specs=[pl.BlockSpec(memory_space=pltpu.HBM)] * len(args),
        out_specs=(pl.BlockSpec(memory_space=pltpu.VMEM),) * 10,
        scratch_shapes=[
            pltpu.VMEM(raw.shape, BF16),
            pltpu.VMEM(range_chirp.shape, BF16),
            pltpu.SMEM(block_shift.shape, jnp.int32),
            pltpu.SemaphoreType.DMA((chunks + len(args) - 1,)),
        ],
        compiler_params=params(),
        name="range_edges",
    )(*(in_hbm(x) for x in args))


def window_tiles(s_ref, start, left, right, part):
    half = CHUNK // 2
    low = low_lanes(CHUNK)
    picked = pl.ds(start, CHUNK)
    last = s_ref.shape[2] // LANES - 1
    inner = slice(4 * CHUNK + part * half, 4 * CHUNK + (part + 1) * half)

    def full(halo):
        ref, chunk = halo
        return [
            ref[chunk, (2 * part + i) * CHUNK : (2 * part + i + 1) * CHUNK, :] for i in range(2)
        ]

    packed = left[0][left[1], inner, :]
    halo = jnp.concatenate([packed, lane_roll(packed)], axis=0)
    first = jnp.where(low, halo, s_ref[part, picked, tile_of(0)])
    packed = right[0][right[1], inner, :]
    halo = jnp.concatenate([lane_roll(packed), packed], axis=0)
    final = jnp.where(low, s_ref[part, picked, tile_of(last)], halo)
    own = [s_ref[part, picked, tile_of(t)] for t in range(1, last)]
    return full(left) + [first] + own + [final] + full(right)


def compress_chunk(s_ref, start, left, right, w_ref, m_ref, out_ref, out_start, c_ref):
    rows = CHUNK
    taps = w_ref.shape[0] // (2 * LANES)
    tiles = [window_tiles(s_ref, start, left, right, part) for part in range(2)]
    for j in range(c_ref.shape[1] // LANES):
        window = jnp.concatenate(tiles[0][j : j + taps] + tiles[1][j : j + taps], axis=1)
        result = jnp.dot(window, w_ref[...], preferred_element_type=F32).astype(BF16)
        c_ref[0:rows, tile_of(j)] = result[:, :LANES]
        c_ref[rows:, tile_of(j)] = result[:, LANES:]
    for b in range(m_ref.shape[0]):
        window = c_ref[:, b * LANES : b * LANES + 2 * LANES]
        result = jnp.dot(window, m_ref[b], preferred_element_type=F32).astype(BF16)
        out_ref[0, out_start : out_start + rows, tile_of(b)] = result[:rows]
        out_ref[1, out_start : out_start + rows, tile_of(b)] = result[rows:]


def compress_kernel(which, s_ref, core_ref, far_ref, w_ref, *refs):
    near, away = near_away_rows(s_ref.shape[1])
    if which == "near":
        taps_ref, splat_ref, out_ref, m_ref, *c_refs = refs
        jobs = [(near, 0)]
    else:
        m_ref, out_ref, *c_refs = refs
        jobs = [(CHUNK * (i + 1), i) for i in range(out_ref.shape[1] // CHUNK)]
        if which == "away":
            jobs = [(away, 1)]

    def body(odd):
        if which == "near":
            migration_bands(taps_ref, splat_ref, m_ref)
        for i, (start, chunk) in enumerate(jobs):
            core, far = (core_ref, chunk), (far_ref, chunk if which == "mid" else 0)
            left, right = (core, far) if odd else (far, core)
            compress_chunk(
                s_ref, start, left, right, w_ref, m_ref, out_ref, i * CHUNK, c_refs[i]
            )

    by_parity("rg", body)


def compress(which, shifted, core, far, w, *bands):
    rows, cells = shifted.shape[1], shifted.shape[2] - LANES
    count = rows // CHUNK - 2 if which == "mid" else 1
    args = (shifted, core, far, w) + bands
    out = (jax.ShapeDtypeStruct((2, count * CHUNK, cells), BF16),)
    if which == "near":
        out += (jax.ShapeDtypeStruct((cells // LANES, 2 * LANES, LANES), BF16),)
    result = pl.pallas_call(
        functools.partial(compress_kernel, which),
        out_shape=out,
        in_specs=[pl.BlockSpec(memory_space=pltpu.VMEM)] * len(args),
        out_specs=(pl.BlockSpec(memory_space=pltpu.VMEM),) * len(out),
        scratch_shapes=[pltpu.VMEM((2 * CHUNK, cells + LANES), BF16)] * count,
        compiler_params=params(),
        name="compress_" + which,
    )(*args)
    return result if which == "near" else result[0]


def lines(ref, chunk):
    return lambda part, lanes: ref[part, chunk * CHUNK : (chunk + 1) * CHUNK, lanes]


def correlate_block(a_ref, b, pairs):
    taps = [a_ref[k, b] for k, _ in pairs]
    windows = [
        jnp.concatenate([window(0, tile_of(b)), window(1, tile_of(b))], axis=1)
        for _, window in pairs
    ]
    result = jnp.dot(
        jnp.concatenate(taps, axis=1),
        jnp.concatenate(windows, axis=0),
        preferred_element_type=F32,
    )
    top, bottom = result[:CHUNK], result[CHUNK:]
    return top[:, :LANES] + bottom[:, LANES:], top[:, LANES:] - bottom[:, :LANES]


def focus_outer_kernel(a_ref, near_ref, away_ref, part_ref, mid_part_ref):
    mids, steps, blocks = mid_part_ref.shape[0], a_ref.shape[0], a_ref.shape[1]

    def body(odd):
        first, final = (near_ref, away_ref) if odd else (away_ref, near_ref)
        order = {0: lines(first, 0), mids + 1: lines(final, 0)}
        jobs = [(part_ref.at[0], 0), (part_ref.at[1], mids + 1)]
        jobs += [(mid_part_ref.at[i], i + 1) for i in range(mids)]
        for out_ref, chunk in jobs:
            pairs = [
                (k, order[chunk + k - 1]) for k in range(steps) if chunk + k - 1 in order
            ]
            for b in range(blocks):
                out_ref[0, :, tile_of(b)], out_ref[1, :, tile_of(b)] = correlate_block(
                    a_ref, b, pairs
                )

    by_parity("az", body)


def focus_outer(a, near, away, mids):
    cells = near.shape[2]
    return pl.pallas_call(
        focus_outer_kernel,
        out_shape=(
            jax.ShapeDtypeStruct((2, 2, CHUNK, cells), F32),
            jax.ShapeDtypeStruct((mids, 2, CHUNK, cells), F32),
        ),
        in_specs=[pl.BlockSpec(memory_space=pltpu.VMEM)] * 3,
        out_specs=(pl.BlockSpec(memory_space=pltpu.VMEM),) * 2,
        compiler_params=params(),
        name="focus_outer",
    )(a, near, away)


def focus_mid_kernel(a_ref, mid_ref, part_ref, mid_part_ref, image_ref, end_ref, sum_ref, sems):
    mids, steps, blocks = mid_part_ref.shape[0], a_ref.shape[0], a_ref.shape[1]
    order = {i + 1: lines(mid_ref, i) for i in range(mids)}
    jobs = [(mid_part_ref.at[i], sum_ref.at[i], i + 1) for i in range(mids)]
    jobs += [(part_ref.at[0], end_ref.at[0], 0), (part_ref.at[1], end_ref.at[1], mids + 1)]
    copies = []
    for i, (before_ref, out_ref, chunk) in enumerate(jobs):
        pairs = [(k, order[chunk + k - 1]) for k in range(steps) if chunk + k - 1 in order]
        for b in range(blocks):
            real, imag = correlate_block(a_ref, b, pairs)
            out_ref[0, :, tile_of(b)] = before_ref[0, :, tile_of(b)] + real
            out_ref[1, :, tile_of(b)] = before_ref[1, :, tile_of(b)] + imag
        if i < mids:
            target = image_ref.at[:, pl.ds(chunk * CHUNK, CHUNK), :]
            copies.append(pltpu.make_async_copy(out_ref, target, sems.at[i]))
            copies[-1].start()
    for copy in copies:
        copy.wait()


def focus_mid(a, mid, part, mid_part):
    cells = mid.shape[2]
    mids = mid_part.shape[0]
    return pl.pallas_call(
        focus_mid_kernel,
        out_shape=(
            jax.ShapeDtypeStruct((2, (mids + 2) * CHUNK, cells), F32),
            jax.ShapeDtypeStruct(part.shape, F32),
        ),
        in_specs=[pl.BlockSpec(memory_space=pltpu.VMEM)] * 4,
        out_specs=(pl.BlockSpec(memory_space=pl.ANY), pl.BlockSpec(memory_space=pltpu.VMEM)),
        scratch_shapes=[pltpu.VMEM(mid_part.shape, F32), pltpu.SemaphoreType.DMA((mids,))],
        compiler_params=params(),
        name="focus_mid",
    )(a, mid, part, mid_part)


def add_halo(a_ref, end, part_ref, halo_ref, out_ref):
    for b in range(a_ref.shape[1]):
        real, imag = correlate_block(a_ref, b, [(2 * end, lines(halo_ref, 0))])
        out_ref[0, :, tile_of(b)] = part_ref[end, 0, :, tile_of(b)] + real
        out_ref[1, :, tile_of(b)] = part_ref[end, 1, :, tile_of(b)] + imag


def near_end_kernel(a_ref, part_ref, halo_ref, out_ref):
    by_parity("az", lambda odd: add_halo(a_ref, 1 - odd, part_ref, halo_ref, out_ref))


def near_end(a, part, halo):
    return pl.pallas_call(
        near_end_kernel,
        out_shape=jax.ShapeDtypeStruct(part.shape[1:], F32),
        in_specs=[pl.BlockSpec(memory_space=pltpu.VMEM)] * 3,
        out_specs=pl.BlockSpec(memory_space=pltpu.VMEM),
        compiler_params=params(),
        name="near_end",
    )(a, part, halo)


def ends_kernel(a_ref, part_ref, near_ref, halo_ref, _, image_ref, sum_ref, sems):
    rows = image_ref.shape[1]
    half = CHUNK // 2

    def body(odd):
        near_first, away_first = (1 - odd) * (rows - CHUNK), odd * (rows - CHUNK)
        copies = [
            pltpu.make_async_copy(
                near_ref, image_ref.at[:, pl.ds(near_first, CHUNK), :], sems.at[2]
            )
        ]
        copies[0].start()
        window = lines(halo_ref, 0)
        for h in range(2):
            picked = slice(h * half, (h + 1) * half)
            for b in range(a_ref.shape[1]):
                taps = jnp.concatenate(
                    [a_ref[2 * odd, b, base + h * half : base + (h + 1) * half] for base in (0, CHUNK)],
                    axis=0,
                )
                both = jnp.concatenate([window(0, tile_of(b)), window(1, tile_of(b))], axis=1)
                result = jnp.dot(taps, both, preferred_element_type=F32)
                top, bottom = result[:half], result[half:]
                real = top[:, :LANES] + bottom[:, LANES:]
                imag = top[:, LANES:] - bottom[:, :LANES]
                sum_ref[0, picked, tile_of(b)] = part_ref[odd, 0, picked, tile_of(b)] + real
                sum_ref[1, picked, tile_of(b)] = part_ref[odd, 1, picked, tile_of(b)] + imag
            target = image_ref.at[:, pl.ds(away_first + h * half, half), :]
            copies.append(pltpu.make_async_copy(sum_ref.at[:, picked, :], target, sems.at[h]))
            copies[-1].start()
        for copy in copies:
            copy.wait()

    by_parity("az", body)


def ends(a, part, near, halo, image):
    return pl.pallas_call(
        ends_kernel,
        out_shape=jax.ShapeDtypeStruct(image.shape, F32),
        in_specs=[pl.BlockSpec(memory_space=pltpu.VMEM)] * 4
        + [pl.BlockSpec(memory_space=pl.ANY)],
        out_specs=pl.BlockSpec(memory_space=pl.ANY),
        scratch_shapes=[pltpu.VMEM(near.shape, F32), pltpu.SemaphoreType.DMA((3,))],
        input_output_aliases={4: 0},
        compiler_params=params(),
        name="ends",
    )(a, part, near, halo, image)


def per_device(raw_echo, range_chirp, migration_taps, block_shift, azimuth_chirp):
    shifted, far_near, far_away, far_mid, core_outer, core_mid, w, taps, splat, azimuth_chirp = range_edges(
        raw_echo, range_chirp, migration_taps, block_shift, azimuth_chirp
    )
    core_outer = swap(core_outer, "rg", 0)
    core_mid = swap(core_mid, "rg", 0)
    far_near = swap(far_near, "rg", 1)
    far_away = swap(far_away, "rg", 1)
    far_mid = swap(far_mid, "rg", 1)
    near, m = compress("near", shifted, core_outer, far_near, w, taps, splat)
    near_halo = swap(near, "az", 0)
    core_outer, core_mid, near = lax.optimization_barrier((core_outer, core_mid, near))
    away = compress("away", shifted, core_outer, far_away, w, m)
    away_halo = swap(away, "az", 1)
    away, azimuth_chirp = lax.optimization_barrier((away, azimuth_chirp))
    a = azimuth_weights(azimuth_chirp)
    part, mid_part = focus_outer(a, near, away, raw_echo.shape[1] // CHUNK - 2)
    far_mid, part = lax.optimization_barrier((far_mid, part))
    mid = compress("mid", shifted, core_mid, far_mid, w, m)
    image, part = focus_mid(a, mid, part, mid_part)
    return ends(a, part, near_end(a, part, near_halo), away_halo, image)


def solution(mesh):
    placed = (P(None, "az", "rg"), P(), P(None, "rg"), P("rg"), P("rg", None, None))
    return jax.shard_map(
        per_device, mesh=mesh, in_specs=placed, out_specs=P(None, "az", "rg"), check_vma=False
    )
```

```python
import functools

import jax
import jax.numpy as jnp
from jax import lax
from jax.experimental import pallas as pl
from jax.experimental.pallas import tpu as pltpu
from jax.sharding import PartitionSpec as P

MAXS = 60
LANES = 128
HALF = 64
CHUNK = 256
PAD = 16
VMEM_LIMIT = 20 * 1024 * 1024
F32 = jnp.float32
BF16 = jnp.bfloat16


def params():
    return pltpu.CompilerParams(vmem_limit_bytes=VMEM_LIMIT)


def whole(shape):
    return pl.BlockSpec(shape, lambda *_: (0,) * len(shape))


def in_hbm(x):
    return pltpu.with_memory_space_constraint(x, pltpu.HBM)


def lane_roll(x):
    return pltpu.roll(x, HALF, 1)


def low_lanes(rows):
    return lax.broadcasted_iota(jnp.int16, (rows, LANES), 1) < HALF


def swap_pairs(count, first):
    pairs = []
    for i in range(first, count - 1, 2):
        pairs += [(i, i + 1), (i + 1, i)]
    return pairs


def swap(x, axis, first):
    return lax.ppermute(x, axis, swap_pairs(lax.axis_size(axis), first))


def by_parity(axis, body):
    odd = lax.rem(lax.axis_index(axis), 2)
    pl.when(odd == 0)(lambda: body(0))
    pl.when(odd == 1)(lambda: body(1))


def shifted_rows(row, lead, width):
    taps = row.shape[1]
    padded = jnp.concatenate([row, jnp.zeros((1, width - taps), F32)], axis=1)
    return pltpu.roll(
        jnp.broadcast_to(padded, (LANES, width)), lead, 1, stride=1, stride_axis=0
    )


def range_toeplitz(range_ref, w_ref):
    depth = w_ref.shape[0] // 2
    real = shifted_rows(range_ref[0:1, :].astype(F32), 0, depth)
    imag = shifted_rows(range_ref[1:2, :].astype(F32), 0, depth)
    real_t, imag_t = real.T.astype(BF16), imag.T.astype(BF16)
    w_ref[0:depth, 0:LANES] = real_t
    w_ref[0:depth, LANES:] = -imag_t
    w_ref[depth:, 0:LANES] = imag_t
    w_ref[depth:, LANES:] = real_t


def migration_bands(taps_ref, shift_ref, m_ref):
    span = m_ref.shape[1]
    blocks = m_ref.shape[0]
    cells = taps_ref.shape[1]
    tap_count = taps_ref.shape[0]
    first = lax.axis_index("rg") * cells - HALF
    total = lax.axis_size("rg") * cells
    for b in range(blocks):
        source = lax.broadcasted_iota(jnp.int32, (span, LANES), 0)
        column = lax.broadcasted_iota(jnp.int32, (span, LANES), 1)
        tap = source - column - (HALF - tap_count // 2) - shift_ref[b][:1, :]
        place = source + first + b * LANES
        tap = jnp.where((place >= 0) & (place < total), tap, -1)
        matrix = jnp.zeros((span, LANES), F32)
        for k in range(tap_count):
            row = taps_ref[k : k + 1, b * LANES : (b + 1) * LANES].astype(F32)
            matrix = jnp.where(tap == k, row, matrix)
        m_ref[b] = matrix.astype(BF16)


def azimuth_weights_kernel(azimuth_ref, a_ref):
    steps, blocks, depth = a_ref.shape[0], a_ref.shape[1], a_ref.shape[3]
    gap = jnp.zeros((LANES, LANES), BF16)
    for b in range(blocks):
        for part in range(2):
            row = azimuth_ref[b, part : part + 1, :].astype(F32)
            rows = shifted_rows(row, 0, steps * depth - LANES).astype(BF16)
            upper = jnp.concatenate([rows, gap], axis=1)
            lower = jnp.concatenate([gap, rows], axis=1)
            base = part * CHUNK
            for k in range(steps):
                a_ref[k, b, base : base + LANES] = upper[:, k * depth : (k + 1) * depth]
                a_ref[k, b, base + LANES : base + CHUNK] = lower[:, k * depth : (k + 1) * depth]


def azimuth_weights(azimuth_chirp):
    blocks = azimuth_chirp.shape[0]
    steps = (azimuth_chirp.shape[2] + CHUNK) // CHUNK
    return pl.pallas_call(
        azimuth_weights_kernel,
        out_shape=jax.ShapeDtypeStruct((steps, blocks, 2 * CHUNK, CHUNK), BF16),
        in_specs=[pl.BlockSpec(memory_space=pltpu.VMEM)],
        out_specs=pl.BlockSpec(memory_space=pltpu.VMEM),
        compiler_params=params(),
        name="azimuth_weights",
    )(azimuth_chirp)


def tile_of(t):
    return slice(t * LANES, (t + 1) * LANES)


def write_edge(x_ref, start, out_ref, chunk, side):
    picked = pl.ds(start, CHUNK)
    half = CHUNK // 2
    low = low_lanes(half)
    last = x_ref.shape[2] // LANES - 1
    for part in range(2):
        for i, t in enumerate((0, 1) if side == 0 else (last - 1, last)):
            at = (2 * part + i) * CHUNK
            out_ref[chunk, at : at + CHUNK, :] = x_ref[part, picked, tile_of(t)]
        cells = x_ref[part, picked, tile_of(2 if side == 0 else last - 2)]
        top, bottom = cells[:half], cells[half:]
        at = 4 * CHUNK + part * half
        if side == 0:
            out_ref[chunk, at : at + half, :] = jnp.where(low, top, lane_roll(bottom))
        else:
            out_ref[chunk, at : at + half, :] = jnp.where(low, lane_roll(top), bottom)


def near_away_rows(rows):
    odd = lax.rem(lax.axis_index("az"), 2)
    last = rows - CHUNK
    near = pl.multiple_of((1 - odd) * last, CHUNK)
    away = pl.multiple_of(odd * last, CHUNK)
    return near, away


def edges_kernel(
    x_hbm, range_hbm, taps_hbm, shift_hbm, azimuth_hbm,
    x_ref, far_near_ref, far_away_ref, far_mid_ref, core_outer_ref, core_mid_ref,
    w_ref, taps_ref, splat_ref, azimuth_ref, range_ref, shift_ref, sems,
):
    rows = x_ref.shape[1]
    near, away = near_away_rows(rows)
    starts = [near, away] + list(range(CHUNK, rows - CHUNK, CHUNK))
    moves = [
        (range_hbm, range_ref),
        (taps_hbm, taps_ref),
        (shift_hbm, shift_ref),
        (azimuth_hbm, azimuth_ref),
    ]
    small = len(moves)
    for start in starts:
        picked = pl.ds(start, CHUNK)
        moves.append((x_hbm.at[:, picked, :], x_ref.at[:, picked, :]))
    copies = [
        pltpu.make_async_copy(source, target, sems.at[i])
        for i, (source, target) in enumerate(moves)
    ]
    for copy in copies:
        copy.start()
    for copy in copies[:small]:
        copy.wait()
    for ref in (core_outer_ref, core_mid_ref):
        extra = ref.shape[1] - 5 * CHUNK
        ref[:, 5 * CHUNK :, :] = jnp.zeros((ref.shape[0], extra, LANES), BF16)
    range_toeplitz(range_ref, w_ref)
    for b in range(splat_ref.shape[0]):
        splat_ref[b] = jnp.full(splat_ref.shape[1:], shift_ref[b], jnp.int32)

    def body(odd):
        for i, start in enumerate(starts):
            copies[small + i].wait()
            far = [(far_near_ref, 0), (far_away_ref, 0)][i] if i < 2 else (far_mid_ref, i - 2)
            core = (core_outer_ref, i) if i < 2 else (core_mid_ref, i - 2)
            write_edge(x_ref, start, *core, 1 - odd)
            write_edge(x_ref, start, *far, odd)

    by_parity("rg", body)


def range_edges(raw, range_chirp, migration_taps, block_shift, azimuth_chirp):
    chunks = raw.shape[1] // CHUNK
    blocks = block_shift.shape[0]
    depth = range_chirp.shape[1] + LANES
    args = (raw, range_chirp, migration_taps, block_shift, azimuth_chirp)
    return pl.pallas_call(
        edges_kernel,
        out_shape=(jax.ShapeDtypeStruct(raw.shape, BF16),)
        + tuple(
            jax.ShapeDtypeStruct((n, 5 * CHUNK + extra, LANES), BF16)
            for n, extra in ((1, 0), (1, 0), (chunks - 2, 0), (2, 2 * PAD), (chunks - 2, PAD))
        )
        + (
            jax.ShapeDtypeStruct((2 * depth, 2 * LANES), BF16),
            jax.ShapeDtypeStruct(migration_taps.shape, BF16),
            jax.ShapeDtypeStruct((blocks, 8, LANES), jnp.int32),
            jax.ShapeDtypeStruct(azimuth_chirp.shape, BF16),
        ),
        in_specs=[pl.BlockSpec(memory_space=pltpu.HBM)] * len(args),
        out_specs=(pl.BlockSpec(memory_space=pltpu.VMEM),) * 10,
        scratch_shapes=[
            pltpu.VMEM(range_chirp.shape, BF16),
            pltpu.SMEM(block_shift.shape, jnp.int32),
            pltpu.SemaphoreType.DMA((chunks + len(args) - 1,)),
        ],
        compiler_params=params(),
        name="range_edges",
    )(*(in_hbm(x) for x in args))


def window_tiles(x_ref, start, left, right, part):
    half = CHUNK // 2
    low = low_lanes(CHUNK)
    picked = pl.ds(start, CHUNK)

    def halo(edge):
        ref, chunk = edge
        at = 4 * CHUNK + part * half
        tiles = [ref[chunk, (2 * part + i) * CHUNK : (2 * part + i + 1) * CHUNK, :] for i in (0, 1)]
        return tiles, ref[chunk, at : at + half, :]

    before, first = halo(left)
    after, final = halo(right)
    own = [x_ref[part, picked, tile_of(t)] for t in range(x_ref.shape[2] // LANES)]
    rolled = [lane_roll(t) for t in before + own + after]
    rolled = (
        [jnp.concatenate([first, lane_roll(first)], axis=0)]
        + rolled
        + [jnp.concatenate([lane_roll(final), final], axis=0)]
    )
    return [jnp.where(low, rolled[i], rolled[i + 1]) for i in range(len(rolled) - 1)]


def compress_chunk(s_ref, start, left, right, w_ref, m_ref, out_ref, out_start, c_ref):
    rows = CHUNK
    taps = w_ref.shape[0] // (2 * LANES)
    tiles = [window_tiles(s_ref, start, left, right, part) for part in range(2)]
    for j in range(c_ref.shape[1] // LANES):
        window = jnp.concatenate(tiles[0][j : j + taps] + tiles[1][j : j + taps], axis=1)
        result = jnp.dot(window, w_ref[...], preferred_element_type=F32).astype(BF16)
        c_ref[0:rows, tile_of(j)] = result[:, :LANES]
        c_ref[rows:, tile_of(j)] = result[:, LANES:]
    for b in range(m_ref.shape[0]):
        window = c_ref[:, b * LANES : b * LANES + 2 * LANES]
        result = jnp.dot(window, m_ref[b], preferred_element_type=F32).astype(BF16)
        out_ref[0, out_start : out_start + rows, tile_of(b)] = result[:rows]
        out_ref[1, out_start : out_start + rows, tile_of(b)] = result[rows:]


def compress_kernel(which, s_ref, core_ref, far_ref, w_ref, *refs):
    near, away = near_away_rows(s_ref.shape[1])
    if which == "near":
        taps_ref, splat_ref, out_ref, m_ref, *c_refs = refs
        jobs = [(near, 0)]
    else:
        m_ref, out_ref, *c_refs = refs
        jobs = [(CHUNK * (i + 1), i) for i in range(out_ref.shape[1] // CHUNK)]
        if which == "away":
            jobs = [(away, 1)]

    def body(odd):
        if which == "near":
            migration_bands(taps_ref, splat_ref, m_ref)
        for i, (start, chunk) in enumerate(jobs):
            core, far = (core_ref, chunk), (far_ref, chunk if which == "mid" else 0)
            left, right = (core, far) if odd else (far, core)
            compress_chunk(
                s_ref, start, left, right, w_ref, m_ref, out_ref, i * CHUNK, c_refs[i]
            )

    by_parity("rg", body)


def compress(which, echo, core, far, w, *bands):
    rows, cells = echo.shape[1], echo.shape[2]
    count = rows // CHUNK - 2 if which == "mid" else 1
    args = (echo, core, far, w) + bands
    out = (jax.ShapeDtypeStruct((2, count * CHUNK, cells), BF16),)
    if which == "near":
        out += (jax.ShapeDtypeStruct((cells // LANES, 2 * LANES, LANES), BF16),)
    result = pl.pallas_call(
        functools.partial(compress_kernel, which),
        out_shape=out,
        in_specs=[pl.BlockSpec(memory_space=pltpu.VMEM)] * len(args),
        out_specs=(pl.BlockSpec(memory_space=pltpu.VMEM),) * len(out),
        scratch_shapes=[pltpu.VMEM((2 * CHUNK, cells + LANES), BF16)] * count,
        compiler_params=params(),
        name="compress_" + which,
    )(*args)
    return result if which == "near" else result[0]


def lines(ref, chunk):
    return lambda part, lanes: ref[part, chunk * CHUNK : (chunk + 1) * CHUNK, lanes]


def correlate_block(a_ref, b, pairs):
    taps = [a_ref[k, b] for k, _ in pairs]
    windows = [
        jnp.concatenate([window(0, tile_of(b)), window(1, tile_of(b))], axis=1)
        for _, window in pairs
    ]
    result = jnp.dot(
        jnp.concatenate(taps, axis=1),
        jnp.concatenate(windows, axis=0),
        preferred_element_type=F32,
    )
    top, bottom = result[:CHUNK], result[CHUNK:]
    return top[:, :LANES] + bottom[:, LANES:], top[:, LANES:] - bottom[:, :LANES]


def focus_outer_kernel(a_ref, near_ref, away_ref, part_ref, mid_part_ref):
    mids, steps, blocks = mid_part_ref.shape[0], a_ref.shape[0], a_ref.shape[1]

    def body(odd):
        first, final = (near_ref, away_ref) if odd else (away_ref, near_ref)
        order = {0: lines(first, 0), mids + 1: lines(final, 0)}
        jobs = [(part_ref.at[0], 0), (part_ref.at[1], mids + 1)]
        jobs += [(mid_part_ref.at[i], i + 1) for i in range(mids)]
        for out_ref, chunk in jobs:
            pairs = [
                (k, order[chunk + k - 1]) for k in range(steps) if chunk + k - 1 in order
            ]
            for b in range(blocks):
                out_ref[0, :, tile_of(b)], out_ref[1, :, tile_of(b)] = correlate_block(
                    a_ref, b, pairs
                )

    by_parity("az", body)


def focus_outer(a, near, away, mids):
    cells = near.shape[2]
    return pl.pallas_call(
        focus_outer_kernel,
        out_shape=(
            jax.ShapeDtypeStruct((2, 2, CHUNK, cells), F32),
            jax.ShapeDtypeStruct((mids, 2, CHUNK, cells), F32),
        ),
        in_specs=[pl.BlockSpec(memory_space=pltpu.VMEM)] * 3,
        out_specs=(pl.BlockSpec(memory_space=pltpu.VMEM),) * 2,
        compiler_params=params(),
        name="focus_outer",
    )(a, near, away)


def focus_mid_kernel(a_ref, mid_ref, part_ref, mid_part_ref, image_ref, end_ref, sum_ref, sems):
    mids, steps, blocks = mid_part_ref.shape[0], a_ref.shape[0], a_ref.shape[1]
    order = {i + 1: lines(mid_ref, i) for i in range(mids)}
    jobs = [(mid_part_ref.at[i], sum_ref.at[i], i + 1) for i in range(mids)]
    jobs += [(part_ref.at[0], end_ref.at[0], 0), (part_ref.at[1], end_ref.at[1], mids + 1)]
    copies = []
    for i, (before_ref, out_ref, chunk) in enumerate(jobs):
        pairs = [(k, order[chunk + k - 1]) for k in range(steps) if chunk + k - 1 in order]
        for b in range(blocks):
            real, imag = correlate_block(a_ref, b, pairs)
            out_ref[0, :, tile_of(b)] = before_ref[0, :, tile_of(b)] + real
            out_ref[1, :, tile_of(b)] = before_ref[1, :, tile_of(b)] + imag
        if i < mids:
            target = image_ref.at[:, pl.ds(chunk * CHUNK, CHUNK), :]
            copies.append(pltpu.make_async_copy(out_ref, target, sems.at[i]))
            copies[-1].start()
    for copy in copies:
        copy.wait()


def focus_mid(a, mid, part, mid_part):
    cells = mid.shape[2]
    mids = mid_part.shape[0]
    return pl.pallas_call(
        focus_mid_kernel,
        out_shape=(
            jax.ShapeDtypeStruct((2, (mids + 2) * CHUNK, cells), F32),
            jax.ShapeDtypeStruct(part.shape, F32),
        ),
        in_specs=[pl.BlockSpec(memory_space=pltpu.VMEM)] * 4,
        out_specs=(pl.BlockSpec(memory_space=pl.ANY), pl.BlockSpec(memory_space=pltpu.VMEM)),
        scratch_shapes=[pltpu.VMEM(mid_part.shape, F32), pltpu.SemaphoreType.DMA((mids,))],
        compiler_params=params(),
        name="focus_mid",
    )(a, mid, part, mid_part)


def add_halo(a_ref, end, part_ref, halo_ref, out_ref):
    for b in range(a_ref.shape[1]):
        real, imag = correlate_block(a_ref, b, [(2 * end, lines(halo_ref, 0))])
        out_ref[0, :, tile_of(b)] = part_ref[end, 0, :, tile_of(b)] + real
        out_ref[1, :, tile_of(b)] = part_ref[end, 1, :, tile_of(b)] + imag


def near_end_kernel(a_ref, part_ref, halo_ref, out_ref):
    by_parity("az", lambda odd: add_halo(a_ref, 1 - odd, part_ref, halo_ref, out_ref))


def near_end(a, part, halo):
    return pl.pallas_call(
        near_end_kernel,
        out_shape=jax.ShapeDtypeStruct(part.shape[1:], F32),
        in_specs=[pl.BlockSpec(memory_space=pltpu.VMEM)] * 3,
        out_specs=pl.BlockSpec(memory_space=pltpu.VMEM),
        compiler_params=params(),
        name="near_end",
    )(a, part, halo)


def ends_kernel(a_ref, part_ref, near_ref, halo_ref, _, image_ref, sum_ref, sems):
    rows = image_ref.shape[1]

    def body(odd):
        copies = []
        for i, (source, end) in enumerate(((near_ref, 1 - odd), (sum_ref, odd))):
            if i == 1:
                add_halo(a_ref, end, part_ref, halo_ref, sum_ref)
            target = image_ref.at[:, pl.ds(end * (rows - CHUNK), CHUNK), :]
            copies.append(pltpu.make_async_copy(source, target, sems.at[i]))
            copies[-1].start()
        for copy in copies:
            copy.wait()

    by_parity("az", body)


def ends(a, part, near, halo, image):
    return pl.pallas_call(
        ends_kernel,
        out_shape=jax.ShapeDtypeStruct(image.shape, F32),
        in_specs=[pl.BlockSpec(memory_space=pltpu.VMEM)] * 4
        + [pl.BlockSpec(memory_space=pl.ANY)],
        out_specs=pl.BlockSpec(memory_space=pl.ANY),
        scratch_shapes=[pltpu.VMEM(near.shape, F32), pltpu.SemaphoreType.DMA((2,))],
        input_output_aliases={4: 0},
        compiler_params=params(),
        name="ends",
    )(a, part, near, halo, image)


def per_device(raw_echo, range_chirp, migration_taps, block_shift, azimuth_chirp):
    echo, far_near, far_away, far_mid, core_outer, core_mid, w, taps, splat, azimuth_chirp = range_edges(
        raw_echo, range_chirp, migration_taps, block_shift, azimuth_chirp
    )
    core_outer = swap(core_outer, "rg", 0)
    core_mid = swap(core_mid, "rg", 0)
    far_near = swap(far_near, "rg", 1)
    far_away = swap(far_away, "rg", 1)
    far_mid = swap(far_mid, "rg", 1)
    near, m = compress("near", echo, core_outer, far_near, w, taps, splat)
    near_halo = swap(near, "az", 0)
    core_outer, core_mid, near = lax.optimization_barrier((core_outer, core_mid, near))
    away = compress("away", echo, core_outer, far_away, w, m)
    away_halo = swap(away, "az", 1)
    away, azimuth_chirp = lax.optimization_barrier((away, azimuth_chirp))
    a = azimuth_weights(azimuth_chirp)
    part, mid_part = focus_outer(a, near, away, raw_echo.shape[1] // CHUNK - 2)
    far_mid, part = lax.optimization_barrier((far_mid, part))
    mid = compress("mid", echo, core_mid, far_mid, w, m)
    image, part = focus_mid(a, mid, part, mid_part)
    return ends(a, part, near_end(a, part, near_halo), away_halo, image)


def solution(mesh):
    placed = (P(None, "az", "rg"), P(), P(None, "rg"), P("rg"), P("rg", None, None))
    return jax.shard_map(
        per_device, mesh=mesh, in_specs=placed, out_specs=P(None, "az", "rg"), check_vma=False
    )
```

```python
import functools

import jax
import jax.numpy as jnp
from jax import lax
from jax.experimental import pallas as pl
from jax.experimental.pallas import tpu as pltpu
from jax.sharding import PartitionSpec as P

MAXS = 60
LANES = 128
HALF = 64
CHUNK = 256
PAD = 16
VMEM_LIMIT = 20 * 1024 * 1024
F32 = jnp.float32
BF16 = jnp.bfloat16


def params():
    return pltpu.CompilerParams(vmem_limit_bytes=VMEM_LIMIT)


def whole(shape):
    return pl.BlockSpec(shape, lambda *_: (0,) * len(shape))


def in_hbm(x):
    return pltpu.with_memory_space_constraint(x, pltpu.HBM)


def lane_roll(x):
    return pltpu.roll(x, HALF, 1)


def low_lanes(rows):
    return lax.broadcasted_iota(jnp.int16, (rows, LANES), 1) < HALF


def swap_pairs(count, first):
    pairs = []
    for i in range(first, count - 1, 2):
        pairs += [(i, i + 1), (i + 1, i)]
    return pairs


def swap(x, axis, first):
    return lax.ppermute(x, axis, swap_pairs(lax.axis_size(axis), first))


def by_parity(axis, body):
    odd = lax.rem(lax.axis_index(axis), 2)
    pl.when(odd == 0)(lambda: body(0))
    pl.when(odd == 1)(lambda: body(1))


def shifted_rows(row, lead, width):
    taps = row.shape[1]
    padded = jnp.concatenate([row, jnp.zeros((1, width - taps), F32)], axis=1)
    return pltpu.roll(
        jnp.broadcast_to(padded, (LANES, width)), lead, 1, stride=1, stride_axis=0
    )


def range_toeplitz(range_ref, w_ref):
    depth = w_ref.shape[0] // 2
    real = shifted_rows(range_ref[0:1, :].astype(F32), 0, depth)
    imag = shifted_rows(range_ref[1:2, :].astype(F32), 0, depth)
    real_t, imag_t = real.T.astype(BF16), imag.T.astype(BF16)
    w_ref[0:depth, 0:LANES] = real_t
    w_ref[0:depth, LANES:] = -imag_t
    w_ref[depth:, 0:LANES] = imag_t
    w_ref[depth:, LANES:] = real_t


def migration_bands(taps_ref, shift_ref, m_ref):
    span = m_ref.shape[1]
    blocks = m_ref.shape[0]
    cells = taps_ref.shape[1]
    tap_count = taps_ref.shape[0]
    first = lax.axis_index("rg") * cells - HALF
    total = lax.axis_size("rg") * cells
    for b in range(blocks):
        source = lax.broadcasted_iota(jnp.int32, (span, LANES), 0)
        column = lax.broadcasted_iota(jnp.int32, (span, LANES), 1)
        tap = source - column - (HALF - tap_count // 2) - shift_ref[b][:1, :]
        place = source + first + b * LANES
        tap = jnp.where((place >= 0) & (place < total), tap, -1)
        matrix = jnp.zeros((span, LANES), F32)
        for k in range(tap_count):
            row = taps_ref[k : k + 1, b * LANES : (b + 1) * LANES].astype(F32)
            matrix = jnp.where(tap == k, row, matrix)
        m_ref[b] = matrix.astype(BF16)


def azimuth_weights_kernel(azimuth_ref, a_ref):
    steps, blocks, depth = a_ref.shape[0], a_ref.shape[1], a_ref.shape[3]
    gap = jnp.zeros((LANES, LANES), BF16)
    for b in range(blocks):
        for part in range(2):
            row = azimuth_ref[b, part : part + 1, :].astype(F32)
            rows = shifted_rows(row, 0, steps * depth - LANES).astype(BF16)
            upper = jnp.concatenate([rows, gap], axis=1)
            lower = jnp.concatenate([gap, rows], axis=1)
            base = part * CHUNK
            for k in range(steps):
                a_ref[k, b, base : base + LANES] = upper[:, k * depth : (k + 1) * depth]
                a_ref[k, b, base + LANES : base + CHUNK] = lower[:, k * depth : (k + 1) * depth]


def azimuth_weights(azimuth_chirp):
    blocks = azimuth_chirp.shape[0]
    steps = (azimuth_chirp.shape[2] + CHUNK) // CHUNK
    return pl.pallas_call(
        azimuth_weights_kernel,
        out_shape=jax.ShapeDtypeStruct((steps, blocks, 2 * CHUNK, CHUNK), BF16),
        in_specs=[pl.BlockSpec(memory_space=pltpu.VMEM)],
        out_specs=pl.BlockSpec(memory_space=pltpu.VMEM),
        compiler_params=params(),
        name="azimuth_weights",
    )(azimuth_chirp)


def tile_of(t):
    return slice(t * LANES, (t + 1) * LANES)


def write_edge(x_ref, start, out_ref, chunk, side):
    picked = pl.ds(start, CHUNK)
    half = CHUNK // 2
    low = low_lanes(half)
    last = x_ref.shape[2] // LANES - 1
    for part in range(2):
        for i, t in enumerate((0, 1) if side == 0 else (last - 1, last)):
            at = (2 * part + i) * CHUNK
            out_ref[chunk, at : at + CHUNK, :] = x_ref[part, picked, tile_of(t)]
        cells = x_ref[part, picked, tile_of(2 if side == 0 else last - 2)]
        top, bottom = cells[:half], cells[half:]
        at = 4 * CHUNK + part * half
        if side == 0:
            out_ref[chunk, at : at + half, :] = jnp.where(low, top, lane_roll(bottom))
        else:
            out_ref[chunk, at : at + half, :] = jnp.where(low, lane_roll(top), bottom)


def near_away_rows(rows):
    odd = lax.rem(lax.axis_index("az"), 2)
    last = rows - CHUNK
    near = pl.multiple_of((1 - odd) * last, CHUNK)
    away = pl.multiple_of(odd * last, CHUNK)
    return near, away


def edges_kernel(
    x_hbm, range_hbm, taps_hbm, shift_hbm, azimuth_hbm,
    x_ref, far_near_ref, far_away_ref, far_mid_ref, core_outer_ref, core_mid_ref,
    w_ref, taps_ref, splat_ref, azimuth_ref, range_ref, shift_ref, sems,
):
    rows = x_ref.shape[1]
    near, away = near_away_rows(rows)
    starts = [near, away] + list(range(CHUNK, rows - CHUNK, CHUNK))
    moves = [
        (range_hbm, range_ref),
        (taps_hbm, taps_ref),
        (shift_hbm, shift_ref),
        (azimuth_hbm, azimuth_ref),
    ]
    for start in starts:
        picked = pl.ds(start, CHUNK)
        moves.append((x_hbm.at[:, picked, :], x_ref.at[:, picked, :]))
    copies = [
        pltpu.make_async_copy(source, target, sems.at[i])
        for i, (source, target) in enumerate(moves)
    ]
    for copy in copies:
        copy.start()
    for copy in copies:
        copy.wait()

    def body(odd):
        for ref in (core_outer_ref, core_mid_ref):
            extra = ref.shape[1] - 5 * CHUNK
            ref[:, 5 * CHUNK :, :] = jnp.zeros((ref.shape[0], extra, LANES), BF16)
        for b in range(splat_ref.shape[0]):
            splat_ref[b] = jnp.full(splat_ref.shape[1:], shift_ref[b], jnp.int32)
        range_toeplitz(range_ref, w_ref)
        for i, start in enumerate(starts):
            far = [(far_near_ref, 0), (far_away_ref, 0)][i] if i < 2 else (far_mid_ref, i - 2)
            core = (core_outer_ref, i) if i < 2 else (core_mid_ref, i - 2)
            write_edge(x_ref, start, *core, 1 - odd)
            write_edge(x_ref, start, *far, odd)

    by_parity("rg", body)


def range_edges(raw, range_chirp, migration_taps, block_shift, azimuth_chirp):
    chunks = raw.shape[1] // CHUNK
    blocks = block_shift.shape[0]
    depth = range_chirp.shape[1] + LANES
    args = (raw, range_chirp, migration_taps, block_shift, azimuth_chirp)
    return pl.pallas_call(
        edges_kernel,
        out_shape=(jax.ShapeDtypeStruct(raw.shape, BF16),)
        + tuple(
            jax.ShapeDtypeStruct((n, 5 * CHUNK + extra, LANES), BF16)
            for n, extra in ((1, 0), (1, 0), (chunks - 2, 0), (2, 2 * PAD), (chunks - 2, PAD))
        )
        + (
            jax.ShapeDtypeStruct((2 * depth, 2 * LANES), BF16),
            jax.ShapeDtypeStruct(migration_taps.shape, BF16),
            jax.ShapeDtypeStruct((blocks, 8, LANES), jnp.int32),
            jax.ShapeDtypeStruct(azimuth_chirp.shape, BF16),
        ),
        in_specs=[pl.BlockSpec(memory_space=pltpu.HBM)] * len(args),
        out_specs=(pl.BlockSpec(memory_space=pltpu.VMEM),) * 10,
        scratch_shapes=[
            pltpu.VMEM(range_chirp.shape, BF16),
            pltpu.SMEM(block_shift.shape, jnp.int32),
            pltpu.SemaphoreType.DMA((chunks + len(args) - 1,)),
        ],
        compiler_params=params(),
        name="range_edges",
    )(*(in_hbm(x) for x in args))


def window_tiles(x_ref, start, left, right, part):
    half = CHUNK // 2
    low = low_lanes(CHUNK)
    picked = pl.ds(start, CHUNK)

    def halo(edge):
        ref, chunk = edge
        at = 4 * CHUNK + part * half
        tiles = [ref[chunk, (2 * part + i) * CHUNK : (2 * part + i + 1) * CHUNK, :] for i in (0, 1)]
        return tiles, ref[chunk, at : at + half, :]

    before, first = halo(left)
    after, final = halo(right)
    own = [x_ref[part, picked, tile_of(t)] for t in range(x_ref.shape[2] // LANES)]
    rolled = [lane_roll(t) for t in before + own + after]
    rolled = (
        [jnp.concatenate([first, lane_roll(first)], axis=0)]
        + rolled
        + [jnp.concatenate([lane_roll(final), final], axis=0)]
    )
    return [jnp.where(low, rolled[i], rolled[i + 1]) for i in range(len(rolled) - 1)]


def compress_chunk(s_ref, start, left, right, w_ref, m_ref, out_ref, out_start, c_ref):
    rows = CHUNK
    taps = w_ref.shape[0] // (2 * LANES)
    tiles = [window_tiles(s_ref, start, left, right, part) for part in range(2)]
    for j in range(c_ref.shape[1] // LANES):
        window = jnp.concatenate(tiles[0][j : j + taps] + tiles[1][j : j + taps], axis=1)
        result = jnp.dot(window, w_ref[...], preferred_element_type=F32).astype(BF16)
        c_ref[0:rows, tile_of(j)] = result[:, :LANES]
        c_ref[rows:, tile_of(j)] = result[:, LANES:]
    for b in range(m_ref.shape[0]):
        window = c_ref[:, b * LANES : b * LANES + 2 * LANES]
        result = jnp.dot(window, m_ref[b], preferred_element_type=F32).astype(BF16)
        out_ref[0, out_start : out_start + rows, tile_of(b)] = result[:rows]
        out_ref[1, out_start : out_start + rows, tile_of(b)] = result[rows:]


def compress_kernel(which, s_ref, core_ref, far_ref, w_ref, *refs):
    near, away = near_away_rows(s_ref.shape[1])
    if which == "near":
        taps_ref, splat_ref, out_ref, m_ref, *c_refs = refs
        jobs = [(near, 0)]
    else:
        m_ref, out_ref, *c_refs = refs
        jobs = [(CHUNK * (i + 1), i) for i in range(out_ref.shape[1] // CHUNK)]
        if which == "away":
            jobs = [(away, 1)]

    def body(odd):
        if which == "near":
            migration_bands(taps_ref, splat_ref, m_ref)
        for i, (start, chunk) in enumerate(jobs):
            core, far = (core_ref, chunk), (far_ref, chunk if which == "mid" else 0)
            left, right = (core, far) if odd else (far, core)
            compress_chunk(
                s_ref, start, left, right, w_ref, m_ref, out_ref, i * CHUNK, c_refs[i]
            )

    by_parity("rg", body)


def compress(which, echo, core, far, w, *bands):
    rows, cells = echo.shape[1], echo.shape[2]
    count = rows // CHUNK - 2 if which == "mid" else 1
    args = (echo, core, far, w) + bands
    out = (jax.ShapeDtypeStruct((2, count * CHUNK, cells), BF16),)
    if which == "near":
        out += (jax.ShapeDtypeStruct((cells // LANES, 2 * LANES, LANES), BF16),)
    result = pl.pallas_call(
        functools.partial(compress_kernel, which),
        out_shape=out,
        in_specs=[pl.BlockSpec(memory_space=pltpu.VMEM)] * len(args),
        out_specs=(pl.BlockSpec(memory_space=pltpu.VMEM),) * len(out),
        scratch_shapes=[pltpu.VMEM((2 * CHUNK, cells + LANES), BF16)] * count,
        compiler_params=params(),
        name="compress_" + which,
    )(*args)
    return result if which == "near" else result[0]


def lines(ref, chunk):
    return lambda part, lanes: ref[part, chunk * CHUNK : (chunk + 1) * CHUNK, lanes]


def correlate_block(a_ref, b, pairs):
    taps = [a_ref[k, b] for k, _ in pairs]
    windows = [
        jnp.concatenate([window(0, tile_of(b)), window(1, tile_of(b))], axis=1)
        for _, window in pairs
    ]
    result = jnp.dot(
        jnp.concatenate(taps, axis=1),
        jnp.concatenate(windows, axis=0),
        preferred_element_type=F32,
    )
    top, bottom = result[:CHUNK], result[CHUNK:]
    return top[:, :LANES] + bottom[:, LANES:], top[:, LANES:] - bottom[:, :LANES]


def focus_outer_kernel(a_ref, near_ref, away_ref, part_ref, mid_part_ref):
    mids, steps, blocks = mid_part_ref.shape[0], a_ref.shape[0], a_ref.shape[1]

    def body(odd):
        first, final = (near_ref, away_ref) if odd else (away_ref, near_ref)
        order = {0: lines(first, 0), mids + 1: lines(final, 0)}
        jobs = [(part_ref.at[0], 0), (part_ref.at[1], mids + 1)]
        jobs += [(mid_part_ref.at[i], i + 1) for i in range(mids)]
        for out_ref, chunk in jobs:
            pairs = [
                (k, order[chunk + k - 1]) for k in range(steps) if chunk + k - 1 in order
            ]
            for b in range(blocks):
                out_ref[0, :, tile_of(b)], out_ref[1, :, tile_of(b)] = correlate_block(
                    a_ref, b, pairs
                )

    by_parity("az", body)


def focus_outer(a, near, away, mids):
    cells = near.shape[2]
    return pl.pallas_call(
        focus_outer_kernel,
        out_shape=(
            jax.ShapeDtypeStruct((2, 2, CHUNK, cells), F32),
            jax.ShapeDtypeStruct((mids, 2, CHUNK, cells), F32),
        ),
        in_specs=[pl.BlockSpec(memory_space=pltpu.VMEM)] * 3,
        out_specs=(pl.BlockSpec(memory_space=pltpu.VMEM),) * 2,
        compiler_params=params(),
        name="focus_outer",
    )(a, near, away)


def focus_mid_kernel(a_ref, mid_ref, part_ref, mid_part_ref, image_ref, end_ref, sum_ref, sems):
    mids, steps, blocks = mid_part_ref.shape[0], a_ref.shape[0], a_ref.shape[1]
    order = {i + 1: lines(mid_ref, i) for i in range(mids)}
    jobs = [(mid_part_ref.at[i], sum_ref.at[i], i + 1) for i in range(mids)]
    jobs += [(part_ref.at[0], end_ref.at[0], 0), (part_ref.at[1], end_ref.at[1], mids + 1)]
    copies = []
    for i, (before_ref, out_ref, chunk) in enumerate(jobs):
        pairs = [(k, order[chunk + k - 1]) for k in range(steps) if chunk + k - 1 in order]
        for b in range(blocks):
            real, imag = correlate_block(a_ref, b, pairs)
            out_ref[0, :, tile_of(b)] = before_ref[0, :, tile_of(b)] + real
            out_ref[1, :, tile_of(b)] = before_ref[1, :, tile_of(b)] + imag
        if i < mids:
            target = image_ref.at[:, pl.ds(chunk * CHUNK, CHUNK), :]
            copies.append(pltpu.make_async_copy(out_ref, target, sems.at[i]))
            copies[-1].start()
    for copy in copies:
        copy.wait()


def focus_mid(a, mid, part, mid_part):
    cells = mid.shape[2]
    mids = mid_part.shape[0]
    return pl.pallas_call(
        focus_mid_kernel,
        out_shape=(
            jax.ShapeDtypeStruct((2, (mids + 2) * CHUNK, cells), F32),
            jax.ShapeDtypeStruct(part.shape, F32),
        ),
        in_specs=[pl.BlockSpec(memory_space=pltpu.VMEM)] * 4,
        out_specs=(pl.BlockSpec(memory_space=pl.ANY), pl.BlockSpec(memory_space=pltpu.VMEM)),
        scratch_shapes=[pltpu.VMEM(mid_part.shape, F32), pltpu.SemaphoreType.DMA((mids,))],
        compiler_params=params(),
        name="focus_mid",
    )(a, mid, part, mid_part)


def add_halo(a_ref, end, part_ref, halo_ref, out_ref):
    for b in range(a_ref.shape[1]):
        real, imag = correlate_block(a_ref, b, [(2 * end, lines(halo_ref, 0))])
        out_ref[0, :, tile_of(b)] = part_ref[end, 0, :, tile_of(b)] + real
        out_ref[1, :, tile_of(b)] = part_ref[end, 1, :, tile_of(b)] + imag


def near_end_kernel(a_ref, part_ref, halo_ref, out_ref):
    by_parity("az", lambda odd: add_halo(a_ref, 1 - odd, part_ref, halo_ref, out_ref))


def near_end(a, part, halo):
    return pl.pallas_call(
        near_end_kernel,
        out_shape=jax.ShapeDtypeStruct(part.shape[1:], F32),
        in_specs=[pl.BlockSpec(memory_space=pltpu.VMEM)] * 3,
        out_specs=pl.BlockSpec(memory_space=pltpu.VMEM),
        compiler_params=params(),
        name="near_end",
    )(a, part, halo)


def ends_kernel(a_ref, part_ref, near_ref, halo_ref, _, image_ref, sum_ref, sems):
    rows = image_ref.shape[1]

    def body(odd):
        copies = []
        for i, (source, end) in enumerate(((near_ref, 1 - odd), (sum_ref, odd))):
            if i == 1:
                add_halo(a_ref, end, part_ref, halo_ref, sum_ref)
            target = image_ref.at[:, pl.ds(end * (rows - CHUNK), CHUNK), :]
            copies.append(pltpu.make_async_copy(source, target, sems.at[i]))
            copies[-1].start()
        for copy in copies:
            copy.wait()

    by_parity("az", body)


def ends(a, part, near, halo, image):
    return pl.pallas_call(
        ends_kernel,
        out_shape=jax.ShapeDtypeStruct(image.shape, F32),
        in_specs=[pl.BlockSpec(memory_space=pltpu.VMEM)] * 4
        + [pl.BlockSpec(memory_space=pl.ANY)],
        out_specs=pl.BlockSpec(memory_space=pl.ANY),
        scratch_shapes=[pltpu.VMEM(near.shape, F32), pltpu.SemaphoreType.DMA((2,))],
        input_output_aliases={4: 0},
        compiler_params=params(),
        name="ends",
    )(a, part, near, halo, image)


def per_device(raw_echo, range_chirp, migration_taps, block_shift, azimuth_chirp):
    echo, far_near, far_away, far_mid, core_outer, core_mid, w, taps, splat, azimuth_chirp = range_edges(
        raw_echo, range_chirp, migration_taps, block_shift, azimuth_chirp
    )
    core_outer = swap(core_outer, "rg", 0)
    core_mid = swap(core_mid, "rg", 0)
    far_near = swap(far_near, "rg", 1)
    far_away = swap(far_away, "rg", 1)
    far_mid = swap(far_mid, "rg", 1)
    near, m = compress("near", echo, core_outer, far_near, w, taps, splat)
    near_halo = swap(near, "az", 0)
    core_outer, core_mid, near = lax.optimization_barrier((core_outer, core_mid, near))
    away = compress("away", echo, core_outer, far_away, w, m)
    away_halo = swap(away, "az", 1)
    away, azimuth_chirp = lax.optimization_barrier((away, azimuth_chirp))
    a = azimuth_weights(azimuth_chirp)
    part, mid_part = focus_outer(a, near, away, raw_echo.shape[1] // CHUNK - 2)
    far_mid, part = lax.optimization_barrier((far_mid, part))
    mid = compress("mid", echo, core_mid, far_mid, w, m)
    image, part = focus_mid(a, mid, part, mid_part)
    return ends(a, part, near_end(a, part, near_halo), away_halo, image)


def solution(mesh):
    placed = (P(None, "az", "rg"), P(), P(None, "rg"), P("rg"), P("rg", None, None))
    return jax.shard_map(
        per_device, mesh=mesh, in_specs=placed, out_specs=P(None, "az", "rg"), check_vma=False
    )
```

```python
import functools

import jax
import jax.numpy as jnp
from jax import lax
from jax.experimental import pallas as pl
from jax.experimental.pallas import tpu as pltpu
from jax.sharding import PartitionSpec as P

MAXS = 60
LANES = 128
HALF = 64
CHUNK = 256
PAD = 16
VMEM_LIMIT = 20 * 1024 * 1024
F32 = jnp.float32
BF16 = jnp.bfloat16


def params():
    return pltpu.CompilerParams(vmem_limit_bytes=VMEM_LIMIT)


def whole(shape):
    return pl.BlockSpec(shape, lambda *_: (0,) * len(shape))


def in_hbm(x):
    return pltpu.with_memory_space_constraint(x, pltpu.HBM)


def lane_roll(x):
    return pltpu.roll(x, HALF, 1)


def low_lanes(rows):
    return lax.broadcasted_iota(jnp.int16, (rows, LANES), 1) < HALF


def swap_pairs(count, first):
    pairs = []
    for i in range(first, count - 1, 2):
        pairs += [(i, i + 1), (i + 1, i)]
    return pairs


def swap(x, axis, first):
    return lax.ppermute(x, axis, swap_pairs(lax.axis_size(axis), first))


def by_parity(axis, body):
    odd = lax.rem(lax.axis_index(axis), 2)
    pl.when(odd == 0)(lambda: body(0))
    pl.when(odd == 1)(lambda: body(1))


def shifted_rows(row, lead, width):
    taps = row.shape[1]
    padded = jnp.concatenate([row, jnp.zeros((1, width - taps), F32)], axis=1)
    return pltpu.roll(
        jnp.broadcast_to(padded, (LANES, width)), lead, 1, stride=1, stride_axis=0
    )


def range_toeplitz(range_ref, w_ref):
    depth = w_ref.shape[0] // 2
    real = shifted_rows(range_ref[0:1, :].astype(F32), 0, depth)
    imag = shifted_rows(range_ref[1:2, :].astype(F32), 0, depth)
    real_t, imag_t = real.T.astype(BF16), imag.T.astype(BF16)
    w_ref[0:depth, 0:LANES] = real_t
    w_ref[0:depth, LANES:] = -imag_t
    w_ref[depth:, 0:LANES] = imag_t
    w_ref[depth:, LANES:] = real_t


def migration_bands(taps_ref, shift_ref, m_ref):
    span = m_ref.shape[1]
    blocks = m_ref.shape[0]
    cells = taps_ref.shape[1]
    tap_count = taps_ref.shape[0]
    first = lax.axis_index("rg") * cells - HALF
    total = lax.axis_size("rg") * cells
    for b in range(blocks):
        source = lax.broadcasted_iota(jnp.int32, (span, LANES), 0)
        column = lax.broadcasted_iota(jnp.int32, (span, LANES), 1)
        tap = source - column - (HALF - tap_count // 2) - shift_ref[b][:1, :]
        place = source + first + b * LANES
        tap = jnp.where((place >= 0) & (place < total), tap, -1)
        matrix = jnp.zeros((span, LANES), F32)
        for k in range(tap_count):
            row = taps_ref[k : k + 1, b * LANES : (b + 1) * LANES].astype(F32)
            matrix = jnp.where(tap == k, row, matrix)
        m_ref[b] = matrix.astype(BF16)


def azimuth_weights_kernel(azimuth_ref, a_ref):
    steps, blocks, depth = a_ref.shape[0], a_ref.shape[1], a_ref.shape[3]
    gap = jnp.zeros((LANES, LANES), BF16)
    for b in range(blocks):
        for part in range(2):
            row = azimuth_ref[b, part : part + 1, :].astype(F32)
            rows = shifted_rows(row, 0, steps * depth - LANES).astype(BF16)
            upper = jnp.concatenate([rows, gap], axis=1)
            lower = jnp.concatenate([gap, rows], axis=1)
            base = part * CHUNK
            for k in range(steps):
                a_ref[k, b, base : base + LANES] = upper[:, k * depth : (k + 1) * depth]
                a_ref[k, b, base + LANES : base + CHUNK] = lower[:, k * depth : (k + 1) * depth]


def azimuth_weights(azimuth_chirp):
    blocks = azimuth_chirp.shape[0]
    steps = (azimuth_chirp.shape[2] + CHUNK) // CHUNK
    return pl.pallas_call(
        azimuth_weights_kernel,
        out_shape=jax.ShapeDtypeStruct((steps, blocks, 2 * CHUNK, CHUNK), BF16),
        in_specs=[pl.BlockSpec(memory_space=pltpu.VMEM)],
        out_specs=pl.BlockSpec(memory_space=pltpu.VMEM),
        compiler_params=params(),
        name="azimuth_weights",
    )(azimuth_chirp)


def tile_of(t):
    return slice(t * LANES, (t + 1) * LANES)


def edge_chunk(x_ref, s_ref, start, targets):
    picked = pl.ds(start, CHUNK)
    half = CHUNK // 2
    low, low_half = low_lanes(CHUNK), low_lanes(half)
    count = x_ref.shape[2] // LANES
    for part in range(2):
        cells = [x_ref[part, picked, tile_of(t)] for t in range(count)]
        rolled = [lane_roll(c) for c in cells]
        tiles = [rolled[0]]
        tiles += [jnp.where(low, rolled[t], rolled[t + 1]) for t in range(count - 1)]
        tiles += [rolled[-1]]
        for t, tile in enumerate(tiles):
            s_ref[part, picked, tile_of(t)] = tile
        for out_ref, chunk, side in targets:
            inner = (1, 2) if side == 0 else (count - 2, count - 1)
            for i, t in enumerate(inner):
                at = (2 * part + i) * CHUNK
                out_ref[chunk, at : at + CHUNK, :] = tiles[t]
            at = 4 * CHUNK + part * half
            if side == 0:
                packed = jnp.where(low_half, cells[0][:half], rolled[0][half:])
            else:
                packed = jnp.where(low_half, rolled[-1][:half], cells[-1][half:])
            out_ref[chunk, at : at + half, :] = packed


def near_away_rows(rows):
    odd = lax.rem(lax.axis_index("az"), 2)
    last = rows - CHUNK
    near = pl.multiple_of((1 - odd) * last, CHUNK)
    away = pl.multiple_of(odd * last, CHUNK)
    return near, away


def edges_kernel(
    x_hbm, range_hbm, taps_hbm, shift_hbm, azimuth_hbm,
    s_ref, far_near_ref, far_away_ref, far_mid_ref, core_outer_ref, core_mid_ref,
    w_ref, taps_ref, splat_ref, azimuth_ref, x_ref, range_ref, shift_ref, sems,
):
    rows = x_ref.shape[1]
    near, away = near_away_rows(rows)
    starts = [near, away] + list(range(CHUNK, rows - CHUNK, CHUNK))
    moves = [
        (range_hbm, range_ref),
        (taps_hbm, taps_ref),
        (shift_hbm, shift_ref),
        (azimuth_hbm, azimuth_ref),
    ]
    small = len(moves)
    for start in starts:
        picked = pl.ds(start, CHUNK)
        moves.append((x_hbm.at[:, picked, :], x_ref.at[:, picked, :]))
    copies = [
        pltpu.make_async_copy(source, target, sems.at[i])
        for i, (source, target) in enumerate(moves)
    ]
    for copy in copies:
        copy.start()
    for copy in copies[:small]:
        copy.wait()
    for ref in (core_outer_ref, core_mid_ref):
        extra = ref.shape[1] - 5 * CHUNK
        ref[:, 5 * CHUNK :, :] = jnp.zeros((ref.shape[0], extra, LANES), BF16)
    range_toeplitz(range_ref, w_ref)
    for b in range(splat_ref.shape[0]):
        splat_ref[b] = jnp.full(splat_ref.shape[1:], shift_ref[b], jnp.int32)

    def body(odd):
        for i, start in enumerate(starts):
            copies[small + i].wait()
            far = [(far_near_ref, 0), (far_away_ref, 0)][i] if i < 2 else (far_mid_ref, i - 2)
            core = (core_outer_ref, i) if i < 2 else (core_mid_ref, i - 2)
            edge_chunk(x_ref, s_ref, start, [core + (1 - odd,), far + (odd,)])

    by_parity("rg", body)


def range_edges(raw, range_chirp, migration_taps, block_shift, azimuth_chirp):
    chunks = raw.shape[1] // CHUNK
    blocks = block_shift.shape[0]
    depth = range_chirp.shape[1] + LANES
    args = (raw, range_chirp, migration_taps, block_shift, azimuth_chirp)
    return pl.pallas_call(
        edges_kernel,
        out_shape=(jax.ShapeDtypeStruct(raw.shape[:2] + (raw.shape[2] + LANES,), BF16),)
        + tuple(
            jax.ShapeDtypeStruct((n, 5 * CHUNK + extra, LANES), BF16)
            for n, extra in ((1, 0), (1, 0), (chunks - 2, 0), (2, 2 * PAD), (chunks - 2, PAD))
        )
        + (
            jax.ShapeDtypeStruct((2 * depth, 2 * LANES), BF16),
            jax.ShapeDtypeStruct(migration_taps.shape, BF16),
            jax.ShapeDtypeStruct((blocks, 8, LANES), jnp.int32),
            jax.ShapeDtypeStruct(azimuth_chirp.shape, BF16),
        ),
        in_specs=[pl.BlockSpec(memory_space=pltpu.HBM)] * len(args),
        out_specs=(pl.BlockSpec(memory_space=pltpu.VMEM),) * 10,
        scratch_shapes=[
            pltpu.VMEM(raw.shape, BF16),
            pltpu.VMEM(range_chirp.shape, BF16),
            pltpu.SMEM(block_shift.shape, jnp.int32),
            pltpu.SemaphoreType.DMA((chunks + len(args) - 1,)),
        ],
        compiler_params=params(),
        name="range_edges",
    )(*(in_hbm(x) for x in args))


def window_tiles(s_ref, start, left, right, part):
    half = CHUNK // 2
    low = low_lanes(CHUNK)
    picked = pl.ds(start, CHUNK)
    last = s_ref.shape[2] // LANES - 1
    inner = slice(4 * CHUNK + part * half, 4 * CHUNK + (part + 1) * half)

    def full(halo):
        ref, chunk = halo
        return [
            ref[chunk, (2 * part + i) * CHUNK : (2 * part + i + 1) * CHUNK, :] for i in range(2)
        ]

    packed = left[0][left[1], inner, :]
    halo = jnp.concatenate([packed, lane_roll(packed)], axis=0)
    first = jnp.where(low, halo, s_ref[part, picked, tile_of(0)])
    packed = right[0][right[1], inner, :]
    halo = jnp.concatenate([lane_roll(packed), packed], axis=0)
    final = jnp.where(low, s_ref[part, picked, tile_of(last)], halo)
    own = [s_ref[part, picked, tile_of(t)] for t in range(1, last)]
    return full(left) + [first] + own + [final] + full(right)


def compress_chunk(s_ref, start, left, right, w_ref, m_ref, out_ref, out_start, c_ref):
    rows = CHUNK
    taps = w_ref.shape[0] // (2 * LANES)
    tiles = [window_tiles(s_ref, start, left, right, part) for part in range(2)]
    for j in range(c_ref.shape[1] // LANES):
        window = jnp.concatenate(tiles[0][j : j + taps] + tiles[1][j : j + taps], axis=1)
        result = jnp.dot(window, w_ref[...], preferred_element_type=F32).astype(BF16)
        c_ref[0:rows, tile_of(j)] = result[:, :LANES]
        c_ref[rows:, tile_of(j)] = result[:, LANES:]
    for b in range(m_ref.shape[0]):
        window = c_ref[:, b * LANES : b * LANES + 2 * LANES]
        result = jnp.dot(window, m_ref[b], preferred_element_type=F32).astype(BF16)
        out_ref[0, out_start : out_start + rows, tile_of(b)] = result[:rows]
        out_ref[1, out_start : out_start + rows, tile_of(b)] = result[rows:]


def compress_kernel(which, s_ref, core_ref, far_ref, w_ref, *refs):
    near, away = near_away_rows(s_ref.shape[1])
    if which == "near":
        taps_ref, splat_ref, out_ref, m_ref, *c_refs = refs
        jobs = [(near, 0)]
    else:
        m_ref, out_ref, *c_refs = refs
        jobs = [(CHUNK * (i + 1), i) for i in range(out_ref.shape[1] // CHUNK)]
        if which == "away":
            jobs = [(away, 1)]

    def body(odd):
        if which == "near":
            migration_bands(taps_ref, splat_ref, m_ref)
        for i, (start, chunk) in enumerate(jobs):
            core, far = (core_ref, chunk), (far_ref, chunk if which == "mid" else 0)
            left, right = (core, far) if odd else (far, core)
            compress_chunk(
                s_ref, start, left, right, w_ref, m_ref, out_ref, i * CHUNK, c_refs[i]
            )

    by_parity("rg", body)


def compress(which, shifted, core, far, w, *bands):
    rows, cells = shifted.shape[1], shifted.shape[2] - LANES
    count = rows // CHUNK - 2 if which == "mid" else 1
    args = (shifted, core, far, w) + bands
    out = (jax.ShapeDtypeStruct((2, count * CHUNK, cells), BF16),)
    if which == "near":
        out += (jax.ShapeDtypeStruct((cells // LANES, 2 * LANES, LANES), BF16),)
    result = pl.pallas_call(
        functools.partial(compress_kernel, which),
        out_shape=out,
        in_specs=[pl.BlockSpec(memory_space=pltpu.VMEM)] * len(args),
        out_specs=(pl.BlockSpec(memory_space=pltpu.VMEM),) * len(out),
        scratch_shapes=[pltpu.VMEM((2 * CHUNK, cells + LANES), BF16)] * count,
        compiler_params=params(),
        name="compress_" + which,
    )(*args)
    return result if which == "near" else result[0]


def lines(ref, chunk):
    return lambda part, lanes: ref[part, chunk * CHUNK : (chunk + 1) * CHUNK, lanes]


def correlate_block(a_ref, b, pairs):
    taps = [a_ref[k, b] for k, _ in pairs]
    windows = [
        jnp.concatenate([window(0, tile_of(b)), window(1, tile_of(b))], axis=1)
        for _, window in pairs
    ]
    result = jnp.dot(
        jnp.concatenate(taps, axis=1),
        jnp.concatenate(windows, axis=0),
        preferred_element_type=F32,
    )
    top, bottom = result[:CHUNK], result[CHUNK:]
    return top[:, :LANES] + bottom[:, LANES:], top[:, LANES:] - bottom[:, :LANES]


def focus_outer_kernel(a_ref, near_ref, away_ref, part_ref, mid_part_ref):
    mids, steps, blocks = mid_part_ref.shape[0], a_ref.shape[0], a_ref.shape[1]

    def body(odd):
        first, final = (near_ref, away_ref) if odd else (away_ref, near_ref)
        order = {0: lines(first, 0), mids + 1: lines(final, 0)}
        jobs = [(part_ref.at[0], 0), (part_ref.at[1], mids + 1)]
        jobs += [(mid_part_ref.at[i], i + 1) for i in range(mids)]
        for out_ref, chunk in jobs:
            pairs = [
                (k, order[chunk + k - 1]) for k in range(steps) if chunk + k - 1 in order
            ]
            for b in range(blocks):
                out_ref[0, :, tile_of(b)], out_ref[1, :, tile_of(b)] = correlate_block(
                    a_ref, b, pairs
                )

    by_parity("az", body)


def focus_outer(a, near, away, mids):
    cells = near.shape[2]
    return pl.pallas_call(
        focus_outer_kernel,
        out_shape=(
            jax.ShapeDtypeStruct((2, 2, CHUNK, cells), F32),
            jax.ShapeDtypeStruct((mids, 2, CHUNK, cells), F32),
        ),
        in_specs=[pl.BlockSpec(memory_space=pltpu.VMEM)] * 3,
        out_specs=(pl.BlockSpec(memory_space=pltpu.VMEM),) * 2,
        compiler_params=params(),
        name="focus_outer",
    )(a, near, away)


def focus_mid_kernel(a_ref, mid_ref, part_ref, mid_part_ref, image_ref, end_ref, sum_ref, sems):
    mids, steps, blocks = mid_part_ref.shape[0], a_ref.shape[0], a_ref.shape[1]
    order = {i + 1: lines(mid_ref, i) for i in range(mids)}
    jobs = [(mid_part_ref.at[i], sum_ref.at[i], i + 1) for i in range(mids)]
    jobs += [(part_ref.at[0], end_ref.at[0], 0), (part_ref.at[1], end_ref.at[1], mids + 1)]
    copies = []
    for i, (before_ref, out_ref, chunk) in enumerate(jobs):
        pairs = [(k, order[chunk + k - 1]) for k in range(steps) if chunk + k - 1 in order]
        for b in range(blocks):
            real, imag = correlate_block(a_ref, b, pairs)
            out_ref[0, :, tile_of(b)] = before_ref[0, :, tile_of(b)] + real
            out_ref[1, :, tile_of(b)] = before_ref[1, :, tile_of(b)] + imag
        if i < mids:
            target = image_ref.at[:, pl.ds(chunk * CHUNK, CHUNK), :]
            copies.append(pltpu.make_async_copy(out_ref, target, sems.at[i]))
            copies[-1].start()
    for copy in copies:
        copy.wait()


def focus_mid(a, mid, part, mid_part):
    cells = mid.shape[2]
    mids = mid_part.shape[0]
    return pl.pallas_call(
        focus_mid_kernel,
        out_shape=(
            jax.ShapeDtypeStruct((2, (mids + 2) * CHUNK, cells), F32),
            jax.ShapeDtypeStruct(part.shape, F32),
        ),
        in_specs=[pl.BlockSpec(memory_space=pltpu.VMEM)] * 4,
        out_specs=(pl.BlockSpec(memory_space=pl.ANY), pl.BlockSpec(memory_space=pltpu.VMEM)),
        scratch_shapes=[pltpu.VMEM(mid_part.shape, F32), pltpu.SemaphoreType.DMA((mids,))],
        compiler_params=params(),
        name="focus_mid",
    )(a, mid, part, mid_part)


def add_halo(a_ref, end, part_ref, halo_ref, out_ref):
    for b in range(a_ref.shape[1]):
        real, imag = correlate_block(a_ref, b, [(2 * end, lines(halo_ref, 0))])
        out_ref[0, :, tile_of(b)] = part_ref[end, 0, :, tile_of(b)] + real
        out_ref[1, :, tile_of(b)] = part_ref[end, 1, :, tile_of(b)] + imag


def near_end_kernel(a_ref, part_ref, halo_ref, out_ref):
    by_parity("az", lambda odd: add_halo(a_ref, 1 - odd, part_ref, halo_ref, out_ref))


def near_end(a, part, halo):
    return pl.pallas_call(
        near_end_kernel,
        out_shape=jax.ShapeDtypeStruct(part.shape[1:], F32),
        in_specs=[pl.BlockSpec(memory_space=pltpu.VMEM)] * 3,
        out_specs=pl.BlockSpec(memory_space=pltpu.VMEM),
        compiler_params=params(),
        name="near_end",
    )(a, part, halo)


def ends_kernel(a_ref, part_ref, near_ref, halo_ref, _, image_ref, sum_ref, sems):
    rows = image_ref.shape[1]
    half = CHUNK // 2

    def body(odd):
        near_first, away_first = (1 - odd) * (rows - CHUNK), odd * (rows - CHUNK)
        copies = [
            pltpu.make_async_copy(
                near_ref, image_ref.at[:, pl.ds(near_first, CHUNK), :], sems.at[2]
            )
        ]
        copies[0].start()
        window = lines(halo_ref, 0)
        for h in range(2):
            picked = slice(h * half, (h + 1) * half)
            for b in range(a_ref.shape[1]):
                taps = jnp.concatenate(
                    [a_ref[2 * odd, b, base + h * half : base + (h + 1) * half] for base in (0, CHUNK)],
                    axis=0,
                )
                both = jnp.concatenate([window(0, tile_of(b)), window(1, tile_of(b))], axis=1)
                result = jnp.dot(taps, both, preferred_element_type=F32)
                top, bottom = result[:half], result[half:]
                real = top[:, :LANES] + bottom[:, LANES:]
                imag = top[:, LANES:] - bottom[:, :LANES]
                sum_ref[0, picked, tile_of(b)] = part_ref[odd, 0, picked, tile_of(b)] + real
                sum_ref[1, picked, tile_of(b)] = part_ref[odd, 1, picked, tile_of(b)] + imag
            target = image_ref.at[:, pl.ds(away_first + h * half, half), :]
            copies.append(pltpu.make_async_copy(sum_ref.at[:, picked, :], target, sems.at[h]))
            copies[-1].start()
        for copy in copies:
            copy.wait()

    by_parity("az", body)


def ends(a, part, near, halo, image):
    return pl.pallas_call(
        ends_kernel,
        out_shape=jax.ShapeDtypeStruct(image.shape, F32),
        in_specs=[pl.BlockSpec(memory_space=pltpu.VMEM)] * 4
        + [pl.BlockSpec(memory_space=pl.ANY)],
        out_specs=pl.BlockSpec(memory_space=pl.ANY),
        scratch_shapes=[pltpu.VMEM(near.shape, F32), pltpu.SemaphoreType.DMA((3,))],
        input_output_aliases={4: 0},
        compiler_params=params(),
        name="ends",
    )(a, part, near, halo, image)


def per_device(raw_echo, range_chirp, migration_taps, block_shift, azimuth_chirp):
    shifted, far_near, far_away, far_mid, core_outer, core_mid, w, taps, splat, azimuth_chirp = range_edges(
        raw_echo, range_chirp, migration_taps, block_shift, azimuth_chirp
    )
    core_outer = swap(core_outer, "rg", 0)
    core_mid = swap(core_mid, "rg", 0)
    far_near = swap(far_near, "rg", 1)
    far_away = swap(far_away, "rg", 1)
    far_mid = swap(far_mid, "rg", 1)
    near, m = compress("near", shifted, core_outer, far_near, w, taps, splat)
    near_halo = swap(near, "az", 0)
    core_outer, core_mid, near = lax.optimization_barrier((core_outer, core_mid, near))
    away = compress("away", shifted, core_outer, far_away, w, m)
    away_halo = swap(away, "az", 1)
    away, azimuth_chirp = lax.optimization_barrier((away, azimuth_chirp))
    a = azimuth_weights(azimuth_chirp)
    part, mid_part = focus_outer(a, near, away, raw_echo.shape[1] // CHUNK - 2)
    far_mid, part = lax.optimization_barrier((far_mid, part))
    mid = compress("mid", shifted, core_mid, far_mid, w, m)
    image, part = focus_mid(a, mid, part, mid_part)
    return ends(a, part, near_end(a, part, near_halo), away_halo, image)


def solution(mesh):
    placed = (P(None, "az", "rg"), P(), P(None, "rg"), P("rg"), P("rg", None, None))
    return jax.shard_map(
        per_device, mesh=mesh, in_specs=placed, out_specs=P(None, "az", "rg"), check_vma=False
    )
```

```python
import functools

import jax
import jax.numpy as jnp
from jax import lax
from jax.experimental import pallas as pl
from jax.experimental.pallas import tpu as pltpu
from jax.sharding import PartitionSpec as P

MAXS = 60
LANES = 128
HALF = 64
CHUNK = 256
PAD = 16
VMEM_LIMIT = 20 * 1024 * 1024
F32 = jnp.float32
BF16 = jnp.bfloat16


def params():
    return pltpu.CompilerParams(vmem_limit_bytes=VMEM_LIMIT)


def whole(shape):
    return pl.BlockSpec(shape, lambda *_: (0,) * len(shape))


def in_hbm(x):
    return pltpu.with_memory_space_constraint(x, pltpu.HBM)


def lane_roll(x):
    return pltpu.roll(x, HALF, 1)


def low_lanes(rows):
    return lax.broadcasted_iota(jnp.int16, (rows, LANES), 1) < HALF


def swap_pairs(count, first):
    pairs = []
    for i in range(first, count - 1, 2):
        pairs += [(i, i + 1), (i + 1, i)]
    return pairs


def swap(x, axis, first):
    return lax.ppermute(x, axis, swap_pairs(lax.axis_size(axis), first))


def by_parity(axis, body):
    odd = lax.rem(lax.axis_index(axis), 2)
    pl.when(odd == 0)(lambda: body(0))
    pl.when(odd == 1)(lambda: body(1))


def shifted_rows(row, lead, width):
    taps = row.shape[1]
    padded = jnp.concatenate([row, jnp.zeros((1, width - taps), F32)], axis=1)
    return pltpu.roll(
        jnp.broadcast_to(padded, (LANES, width)), lead, 1, stride=1, stride_axis=0
    )


def range_toeplitz(range_ref, w_ref):
    depth = w_ref.shape[0] // 2
    real = shifted_rows(range_ref[0:1, :].astype(F32), 0, depth)
    imag = shifted_rows(range_ref[1:2, :].astype(F32), 0, depth)
    real_t, imag_t = real.T.astype(BF16), imag.T.astype(BF16)
    w_ref[0:depth, 0:LANES] = real_t
    w_ref[0:depth, LANES:] = -imag_t
    w_ref[depth:, 0:LANES] = imag_t
    w_ref[depth:, LANES:] = real_t


def migration_bands(taps_ref, shift_ref, m_ref):
    span = m_ref.shape[1]
    blocks = m_ref.shape[0]
    cells = taps_ref.shape[1]
    tap_count = taps_ref.shape[0]
    first = lax.axis_index("rg") * cells - HALF
    total = lax.axis_size("rg") * cells
    for b in range(blocks):
        source = lax.broadcasted_iota(jnp.int32, (span, LANES), 0)
        column = lax.broadcasted_iota(jnp.int32, (span, LANES), 1)
        tap = source - column - (HALF - tap_count // 2) - shift_ref[b]
        place = source + first + b * LANES
        tap = jnp.where((place >= 0) & (place < total), tap, -1)
        matrix = jnp.zeros((span, LANES), F32)
        for k in range(tap_count):
            row = taps_ref[k : k + 1, b * LANES : (b + 1) * LANES].astype(F32)
            matrix = jnp.where(tap == k, row, matrix)
        m_ref[b] = matrix.astype(BF16)


def azimuth_weights_kernel(azimuth_ref, a_ref):
    steps, blocks, depth = a_ref.shape[0], a_ref.shape[1], a_ref.shape[3]
    gap = jnp.zeros((LANES, LANES), BF16)
    for b in range(blocks):
        for part in range(2):
            row = azimuth_ref[b, part : part + 1, :].astype(F32)
            rows = shifted_rows(row, 0, steps * depth - LANES).astype(BF16)
            upper = jnp.concatenate([rows, gap], axis=1)
            lower = jnp.concatenate([gap, rows], axis=1)
            base = part * CHUNK
            for k in range(steps):
                a_ref[k, b, base : base + LANES] = upper[:, k * depth : (k + 1) * depth]
                a_ref[k, b, base + LANES : base + CHUNK] = lower[:, k * depth : (k + 1) * depth]


def azimuth_weights(azimuth_chirp):
    blocks = azimuth_chirp.shape[0]
    steps = (azimuth_chirp.shape[2] + CHUNK) // CHUNK
    return pl.pallas_call(
        azimuth_weights_kernel,
        out_shape=jax.ShapeDtypeStruct((steps, blocks, 2 * CHUNK, CHUNK), BF16),
        in_specs=[pl.BlockSpec(memory_space=pltpu.VMEM)],
        out_specs=pl.BlockSpec(memory_space=pltpu.VMEM),
        compiler_params=params(),
        name="azimuth_weights",
    )(azimuth_chirp)


def tile_of(t):
    return slice(t * LANES, (t + 1) * LANES)


def write_edge(x_ref, start, out_ref, chunk, side):
    picked = pl.ds(start, CHUNK)
    half = CHUNK // 2
    low = low_lanes(half)
    last = x_ref.shape[2] // LANES - 1
    for part in range(2):
        for i, t in enumerate((0, 1) if side == 0 else (last - 1, last)):
            at = (2 * part + i) * CHUNK
            out_ref[chunk, at : at + CHUNK, :] = x_ref[part, picked, tile_of(t)]
        cells = x_ref[part, picked, tile_of(2 if side == 0 else last - 2)]
        top, bottom = cells[:half], cells[half:]
        at = 4 * CHUNK + part * half
        if side == 0:
            out_ref[chunk, at : at + half, :] = jnp.where(low, top, lane_roll(bottom))
        else:
            out_ref[chunk, at : at + half, :] = jnp.where(low, lane_roll(top), bottom)


def near_away_rows(rows):
    odd = lax.rem(lax.axis_index("az"), 2)
    last = rows - CHUNK
    near = pl.multiple_of((1 - odd) * last, CHUNK)
    away = pl.multiple_of(odd * last, CHUNK)
    return near, away


def edges_kernel(
    x_hbm, range_hbm, taps_hbm, shift_hbm, azimuth_hbm,
    x_ref, far_near_ref, far_away_ref, far_mid_ref, core_outer_ref, core_mid_ref,
    w_ref, m_ref, azimuth_ref, range_ref, taps_ref, shift_ref, sems,
):
    rows = x_ref.shape[1]
    near, away = near_away_rows(rows)
    starts = [near, away] + list(range(CHUNK, rows - CHUNK, CHUNK))
    moves = [
        (range_hbm, range_ref),
        (taps_hbm, taps_ref),
        (shift_hbm, shift_ref),
        (azimuth_hbm, azimuth_ref),
    ]
    small = len(moves)
    for start in starts:
        picked = pl.ds(start, CHUNK)
        moves.append((x_hbm.at[:, picked, :], x_ref.at[:, picked, :]))
    copies = [
        pltpu.make_async_copy(source, target, sems.at[i])
        for i, (source, target) in enumerate(moves)
    ]
    for copy in copies:
        copy.start()
    for copy in copies[:small]:
        copy.wait()
    for ref in (core_outer_ref, core_mid_ref):
        extra = ref.shape[1] - 5 * CHUNK
        ref[:, 5 * CHUNK :, :] = jnp.zeros((ref.shape[0], extra, LANES), BF16)
    range_toeplitz(range_ref, w_ref)
    migration_bands(taps_ref, shift_ref, m_ref)

    def body(odd):
        for i, start in enumerate(starts):
            copies[small + i].wait()
            far = [(far_near_ref, 0), (far_away_ref, 0)][i] if i < 2 else (far_mid_ref, i - 2)
            core = (core_outer_ref, i) if i < 2 else (core_mid_ref, i - 2)
            write_edge(x_ref, start, *core, 1 - odd)
            write_edge(x_ref, start, *far, odd)

    by_parity("rg", body)


def range_edges(raw, range_chirp, migration_taps, block_shift, azimuth_chirp):
    chunks = raw.shape[1] // CHUNK
    blocks = block_shift.shape[0]
    depth = range_chirp.shape[1] + LANES
    args = (raw, range_chirp, migration_taps, block_shift, azimuth_chirp)
    return pl.pallas_call(
        edges_kernel,
        out_shape=(jax.ShapeDtypeStruct(raw.shape, BF16),)
        + tuple(
            jax.ShapeDtypeStruct((n, 5 * CHUNK + extra, LANES), BF16)
            for n, extra in ((1, 0), (1, 0), (chunks - 2, 0), (2, 2 * PAD), (chunks - 2, PAD))
        )
        + (
            jax.ShapeDtypeStruct((2 * depth, 2 * LANES), BF16),
            jax.ShapeDtypeStruct((blocks, 2 * LANES, LANES), BF16),
            jax.ShapeDtypeStruct(azimuth_chirp.shape, BF16),
        ),
        in_specs=[pl.BlockSpec(memory_space=pltpu.HBM)] * len(args),
        out_specs=(pl.BlockSpec(memory_space=pltpu.VMEM),) * 9,
        scratch_shapes=[
            pltpu.VMEM(range_chirp.shape, BF16),
            pltpu.VMEM(migration_taps.shape, BF16),
            pltpu.SMEM(block_shift.shape, jnp.int32),
            pltpu.SemaphoreType.DMA((chunks + len(args) - 1,)),
        ],
        compiler_params=params(),
        name="range_edges",
    )(*(in_hbm(x) for x in args))


def window_tiles(x_ref, start, left, right, part):
    half = CHUNK // 2
    low = low_lanes(CHUNK)
    picked = pl.ds(start, CHUNK)

    def halo(edge):
        ref, chunk = edge
        at = 4 * CHUNK + part * half
        tiles = [ref[chunk, (2 * part + i) * CHUNK : (2 * part + i + 1) * CHUNK, :] for i in (0, 1)]
        return tiles, ref[chunk, at : at + half, :]

    before, first = halo(left)
    after, final = halo(right)
    own = [x_ref[part, picked, tile_of(t)] for t in range(x_ref.shape[2] // LANES)]
    rolled = [lane_roll(t) for t in before + own + after]
    rolled = (
        [jnp.concatenate([first, lane_roll(first)], axis=0)]
        + rolled
        + [jnp.concatenate([lane_roll(final), final], axis=0)]
    )
    return [jnp.where(low, rolled[i], rolled[i + 1]) for i in range(len(rolled) - 1)]


def compress_chunk(s_ref, start, left, right, w_ref, m_ref, out_ref, out_start, c_ref):
    rows = CHUNK
    taps = w_ref.shape[0] // (2 * LANES)
    tiles = [window_tiles(s_ref, start, left, right, part) for part in range(2)]
    for j in range(c_ref.shape[1] // LANES):
        window = jnp.concatenate(tiles[0][j : j + taps] + tiles[1][j : j + taps], axis=1)
        result = jnp.dot(window, w_ref[...], preferred_element_type=F32).astype(BF16)
        c_ref[0:rows, tile_of(j)] = result[:, :LANES]
        c_ref[rows:, tile_of(j)] = result[:, LANES:]
    for b in range(m_ref.shape[0]):
        window = c_ref[:, b * LANES : b * LANES + 2 * LANES]
        result = jnp.dot(window, m_ref[b], preferred_element_type=F32).astype(BF16)
        out_ref[0, out_start : out_start + rows, tile_of(b)] = result[:rows]
        out_ref[1, out_start : out_start + rows, tile_of(b)] = result[rows:]


def compress_kernel(which, s_ref, core_ref, far_ref, w_ref, *refs):
    near, away = near_away_rows(s_ref.shape[1])
    m_ref, out_ref, *c_refs = refs
    if which == "near":
        jobs = [(near, 0)]
    else:
        jobs = [(CHUNK * (i + 1), i) for i in range(out_ref.shape[1] // CHUNK)]
        if which == "away":
            jobs = [(away, 1)]

    def body(odd):
        for i, (start, chunk) in enumerate(jobs):
            core, far = (core_ref, chunk), (far_ref, chunk if which == "mid" else 0)
            left, right = (core, far) if odd else (far, core)
            compress_chunk(
                s_ref, start, left, right, w_ref, m_ref, out_ref, i * CHUNK, c_refs[i]
            )

    by_parity("rg", body)


def compress(which, echo, core, far, w, *bands):
    rows, cells = echo.shape[1], echo.shape[2]
    count = rows // CHUNK - 2 if which == "mid" else 1
    args = (echo, core, far, w) + bands
    out = (jax.ShapeDtypeStruct((2, count * CHUNK, cells), BF16),)
    result = pl.pallas_call(
        functools.partial(compress_kernel, which),
        out_shape=out,
        in_specs=[pl.BlockSpec(memory_space=pltpu.VMEM)] * len(args),
        out_specs=(pl.BlockSpec(memory_space=pltpu.VMEM),) * len(out),
        scratch_shapes=[pltpu.VMEM((2 * CHUNK, cells + LANES), BF16)] * count,
        compiler_params=params(),
        name="compress_" + which,
    )(*args)
    return result[0]


def lines(ref, chunk):
    return lambda part, lanes: ref[part, chunk * CHUNK : (chunk + 1) * CHUNK, lanes]


def correlate_block(a_ref, b, pairs):
    taps = [a_ref[k, b] for k, _ in pairs]
    windows = [
        jnp.concatenate([window(0, tile_of(b)), window(1, tile_of(b))], axis=1)
        for _, window in pairs
    ]
    result = jnp.dot(
        jnp.concatenate(taps, axis=1),
        jnp.concatenate(windows, axis=0),
        preferred_element_type=F32,
    )
    top, bottom = result[:CHUNK], result[CHUNK:]
    return top[:, :LANES] + bottom[:, LANES:], top[:, LANES:] - bottom[:, :LANES]


def focus_outer_kernel(a_ref, near_ref, away_ref, part_ref, mid_part_ref):
    mids, steps, blocks = mid_part_ref.shape[0], a_ref.shape[0], a_ref.shape[1]

    def body(odd):
        first, final = (near_ref, away_ref) if odd else (away_ref, near_ref)
        order = {0: lines(first, 0), mids + 1: lines(final, 0)}
        jobs = [(part_ref.at[0], 0), (part_ref.at[1], mids + 1)]
        jobs += [(mid_part_ref.at[i], i + 1) for i in range(mids)]
        for out_ref, chunk in jobs:
            pairs = [
                (k, order[chunk + k - 1]) for k in range(steps) if chunk + k - 1 in order
            ]
            for b in range(blocks):
                out_ref[0, :, tile_of(b)], out_ref[1, :, tile_of(b)] = correlate_block(
                    a_ref, b, pairs
                )

    by_parity("az", body)


def focus_outer(a, near, away, mids):
    cells = near.shape[2]
    return pl.pallas_call(
        focus_outer_kernel,
        out_shape=(
            jax.ShapeDtypeStruct((2, 2, CHUNK, cells), F32),
            jax.ShapeDtypeStruct((mids, 2, CHUNK, cells), F32),
        ),
        in_specs=[pl.BlockSpec(memory_space=pltpu.VMEM)] * 3,
        out_specs=(pl.BlockSpec(memory_space=pltpu.VMEM),) * 2,
        compiler_params=params(),
        name="focus_outer",
    )(a, near, away)


def focus_mid_kernel(a_ref, mid_ref, part_ref, mid_part_ref, image_ref, end_ref, sum_ref, sems):
    mids, steps, blocks = mid_part_ref.shape[0], a_ref.shape[0], a_ref.shape[1]
    order = {i + 1: lines(mid_ref, i) for i in range(mids)}
    jobs = [(mid_part_ref.at[i], sum_ref.at[i], i + 1) for i in range(mids)]
    jobs += [(part_ref.at[0], end_ref.at[0], 0), (part_ref.at[1], end_ref.at[1], mids + 1)]
    copies = []
    for i, (before_ref, out_ref, chunk) in enumerate(jobs):
        pairs = [(k, order[chunk + k - 1]) for k in range(steps) if chunk + k - 1 in order]
        for b in range(blocks):
            real, imag = correlate_block(a_ref, b, pairs)
            out_ref[0, :, tile_of(b)] = before_ref[0, :, tile_of(b)] + real
            out_ref[1, :, tile_of(b)] = before_ref[1, :, tile_of(b)] + imag
        if i < mids:
            target = image_ref.at[:, pl.ds(chunk * CHUNK, CHUNK), :]
            copies.append(pltpu.make_async_copy(out_ref, target, sems.at[i]))
            copies[-1].start()
    for copy in copies:
        copy.wait()


def focus_mid(a, mid, part, mid_part):
    cells = mid.shape[2]
    mids = mid_part.shape[0]
    return pl.pallas_call(
        focus_mid_kernel,
        out_shape=(
            jax.ShapeDtypeStruct((2, (mids + 2) * CHUNK, cells), F32),
            jax.ShapeDtypeStruct(part.shape, F32),
        ),
        in_specs=[pl.BlockSpec(memory_space=pltpu.VMEM)] * 4,
        out_specs=(pl.BlockSpec(memory_space=pl.ANY), pl.BlockSpec(memory_space=pltpu.VMEM)),
        scratch_shapes=[pltpu.VMEM(mid_part.shape, F32), pltpu.SemaphoreType.DMA((mids,))],
        compiler_params=params(),
        name="focus_mid",
    )(a, mid, part, mid_part)


def add_halo(a_ref, end, part_ref, halo_ref, out_ref):
    for b in range(a_ref.shape[1]):
        real, imag = correlate_block(a_ref, b, [(2 * end, lines(halo_ref, 0))])
        out_ref[0, :, tile_of(b)] = part_ref[end, 0, :, tile_of(b)] + real
        out_ref[1, :, tile_of(b)] = part_ref[end, 1, :, tile_of(b)] + imag


def near_end_kernel(a_ref, part_ref, halo_ref, out_ref):
    by_parity("az", lambda odd: add_halo(a_ref, 1 - odd, part_ref, halo_ref, out_ref))


def near_end(a, part, halo):
    return pl.pallas_call(
        near_end_kernel,
        out_shape=jax.ShapeDtypeStruct(part.shape[1:], F32),
        in_specs=[pl.BlockSpec(memory_space=pltpu.VMEM)] * 3,
        out_specs=pl.BlockSpec(memory_space=pltpu.VMEM),
        compiler_params=params(),
        name="near_end",
    )(a, part, halo)


def ends_kernel(a_ref, part_ref, near_ref, halo_ref, _, image_ref, sum_ref, sems):
    rows = image_ref.shape[1]
    half = CHUNK // 2

    def body(odd):
        near_first, away_first = (1 - odd) * (rows - CHUNK), odd * (rows - CHUNK)
        copies = [
            pltpu.make_async_copy(
                near_ref, image_ref.at[:, pl.ds(near_first, CHUNK), :], sems.at[2]
            )
        ]
        copies[0].start()
        window = lines(halo_ref, 0)
        for h in range(2):
            picked = slice(h * half, (h + 1) * half)
            for b in range(a_ref.shape[1]):
                taps = jnp.concatenate(
                    [a_ref[2 * odd, b, base + h * half : base + (h + 1) * half] for base in (0, CHUNK)],
                    axis=0,
                )
                both = jnp.concatenate([window(0, tile_of(b)), window(1, tile_of(b))], axis=1)
                result = jnp.dot(taps, both, preferred_element_type=F32)
                top, bottom = result[:half], result[half:]
                real = top[:, :LANES] + bottom[:, LANES:]
                imag = top[:, LANES:] - bottom[:, :LANES]
                sum_ref[0, picked, tile_of(b)] = part_ref[odd, 0, picked, tile_of(b)] + real
                sum_ref[1, picked, tile_of(b)] = part_ref[odd, 1, picked, tile_of(b)] + imag
            target = image_ref.at[:, pl.ds(away_first + h * half, half), :]
            copies.append(pltpu.make_async_copy(sum_ref.at[:, picked, :], target, sems.at[h]))
            copies[-1].start()
        for copy in copies:
            copy.wait()

    by_parity("az", body)


def ends(a, part, near, halo, image):
    return pl.pallas_call(
        ends_kernel,
        out_shape=jax.ShapeDtypeStruct(image.shape, F32),
        in_specs=[pl.BlockSpec(memory_space=pltpu.VMEM)] * 4
        + [pl.BlockSpec(memory_space=pl.ANY)],
        out_specs=pl.BlockSpec(memory_space=pl.ANY),
        scratch_shapes=[pltpu.VMEM(near.shape, F32), pltpu.SemaphoreType.DMA((3,))],
        input_output_aliases={4: 0},
        compiler_params=params(),
        name="ends",
    )(a, part, near, halo, image)


def per_device(raw_echo, range_chirp, migration_taps, block_shift, azimuth_chirp):
    echo, far_near, far_away, far_mid, core_outer, core_mid, w, m, azimuth_chirp = range_edges(
        raw_echo, range_chirp, migration_taps, block_shift, azimuth_chirp
    )
    core_outer = swap(core_outer, "rg", 0)
    core_mid = swap(core_mid, "rg", 0)
    far_near = swap(far_near, "rg", 1)
    far_away = swap(far_away, "rg", 1)
    far_mid = swap(far_mid, "rg", 1)
    near = compress("near", echo, core_outer, far_near, w, m)
    near_halo = swap(near, "az", 0)
    core_outer, core_mid, near = lax.optimization_barrier((core_outer, core_mid, near))
    away = compress("away", echo, core_outer, far_away, w, m)
    away_halo = swap(away, "az", 1)
    away, azimuth_chirp = lax.optimization_barrier((away, azimuth_chirp))
    a = azimuth_weights(azimuth_chirp)
    part, mid_part = focus_outer(a, near, away, raw_echo.shape[1] // CHUNK - 2)
    far_mid, part = lax.optimization_barrier((far_mid, part))
    mid = compress("mid", echo, core_mid, far_mid, w, m)
    image, part = focus_mid(a, mid, part, mid_part)
    return ends(a, part, near_end(a, part, near_halo), away_halo, image)


def solution(mesh):
    placed = (P(None, "az", "rg"), P(), P(None, "rg"), P("rg"), P("rg", None, None))
    return jax.shard_map(
        per_device, mesh=mesh, in_specs=placed, out_specs=P(None, "az", "rg"), check_vma=False
    )
```

```python
import functools

import jax
import jax.numpy as jnp
from jax import lax
from jax.experimental import pallas as pl
from jax.experimental.pallas import tpu as pltpu
from jax.sharding import PartitionSpec as P

MAXS = 60
LANES = 128
HALF = 64
CHUNK = 256
PAD = 16
VMEM_LIMIT = 20 * 1024 * 1024
F32 = jnp.float32
BF16 = jnp.bfloat16


def params():
    return pltpu.CompilerParams(vmem_limit_bytes=VMEM_LIMIT)


def whole(shape):
    return pl.BlockSpec(shape, lambda *_: (0,) * len(shape))


def in_hbm(x):
    return pltpu.with_memory_space_constraint(x, pltpu.HBM)


def lane_roll(x):
    return pltpu.roll(x, HALF, 1)


def low_lanes(rows):
    return lax.broadcasted_iota(jnp.int16, (rows, LANES), 1) < HALF


def swap_pairs(count, first):
    pairs = []
    for i in range(first, count - 1, 2):
        pairs += [(i, i + 1), (i + 1, i)]
    return pairs


def swap(x, axis, first):
    return lax.ppermute(x, axis, swap_pairs(lax.axis_size(axis), first))


def by_parity(axis, body):
    odd = lax.rem(lax.axis_index(axis), 2)
    pl.when(odd == 0)(lambda: body(0))
    pl.when(odd == 1)(lambda: body(1))


def shifted_rows(row, lead, width):
    taps = row.shape[1]
    padded = jnp.concatenate([row, jnp.zeros((1, width - taps), F32)], axis=1)
    return pltpu.roll(
        jnp.broadcast_to(padded, (LANES, width)), lead, 1, stride=1, stride_axis=0
    )


def range_toeplitz(range_ref, w_ref):
    depth = w_ref.shape[0] // 2
    real = shifted_rows(range_ref[0:1, :].astype(F32), 0, depth)
    imag = shifted_rows(range_ref[1:2, :].astype(F32), 0, depth)
    real_t, imag_t = real.T.astype(BF16), imag.T.astype(BF16)
    w_ref[0:depth, 0:LANES] = real_t
    w_ref[0:depth, LANES:] = -imag_t
    w_ref[depth:, 0:LANES] = imag_t
    w_ref[depth:, LANES:] = real_t


def migration_bands(taps_ref, shift_ref, m_ref):
    span = m_ref.shape[1]
    blocks = m_ref.shape[0]
    cells = taps_ref.shape[1]
    tap_count = taps_ref.shape[0]
    first = lax.axis_index("rg") * cells - HALF
    total = lax.axis_size("rg") * cells
    for b in range(blocks):
        source = lax.broadcasted_iota(jnp.int32, (span, LANES), 0)
        column = lax.broadcasted_iota(jnp.int32, (span, LANES), 1)
        tap = source - column - (HALF - tap_count // 2) - shift_ref[b][:1, :]
        place = source + first + b * LANES
        tap = jnp.where((place >= 0) & (place < total), tap, -1)
        matrix = jnp.zeros((span, LANES), F32)
        for k in range(tap_count):
            row = taps_ref[k : k + 1, b * LANES : (b + 1) * LANES].astype(F32)
            matrix = jnp.where(tap == k, row, matrix)
        m_ref[b] = matrix.astype(BF16)


def azimuth_weights_kernel(azimuth_ref, a_ref):
    steps, blocks, depth = a_ref.shape[0], a_ref.shape[1], a_ref.shape[3]
    gap = jnp.zeros((LANES, LANES), BF16)
    for b in range(blocks):
        for part in range(2):
            row = azimuth_ref[b, part : part + 1, :].astype(F32)
            rows = shifted_rows(row, 0, steps * depth - LANES).astype(BF16)
            upper = jnp.concatenate([rows, gap], axis=1)
            lower = jnp.concatenate([gap, rows], axis=1)
            base = part * CHUNK
            for k in range(steps):
                a_ref[k, b, base : base + LANES] = upper[:, k * depth : (k + 1) * depth]
                a_ref[k, b, base + LANES : base + CHUNK] = lower[:, k * depth : (k + 1) * depth]


def azimuth_weights(azimuth_chirp):
    blocks = azimuth_chirp.shape[0]
    steps = (azimuth_chirp.shape[2] + CHUNK) // CHUNK
    return pl.pallas_call(
        azimuth_weights_kernel,
        out_shape=jax.ShapeDtypeStruct((steps, blocks, 2 * CHUNK, CHUNK), BF16),
        in_specs=[pl.BlockSpec(memory_space=pltpu.VMEM)],
        out_specs=pl.BlockSpec(memory_space=pltpu.VMEM),
        compiler_params=params(),
        name="azimuth_weights",
    )(azimuth_chirp)


def tile_of(t):
    return slice(t * LANES, (t + 1) * LANES)


def write_edge(x_ref, start, out_ref, chunk, side):
    picked = pl.ds(start, CHUNK)
    half = CHUNK // 2
    low = low_lanes(half)
    last = x_ref.shape[2] // LANES - 1
    for part in range(2):
        for i, t in enumerate((0, 1) if side == 0 else (last - 1, last)):
            at = (2 * part + i) * CHUNK
            out_ref[chunk, at : at + CHUNK, :] = x_ref[part, picked, tile_of(t)]
        cells = x_ref[part, picked, tile_of(2 if side == 0 else last - 2)]
        top, bottom = cells[:half], cells[half:]
        at = 4 * CHUNK + part * half
        if side == 0:
            out_ref[chunk, at : at + half, :] = jnp.where(low, top, lane_roll(bottom))
        else:
            out_ref[chunk, at : at + half, :] = jnp.where(low, lane_roll(top), bottom)


def near_away_rows(rows):
    odd = lax.rem(lax.axis_index("az"), 2)
    last = rows - CHUNK
    near = pl.multiple_of((1 - odd) * last, CHUNK)
    away = pl.multiple_of(odd * last, CHUNK)
    return near, away


def edges_kernel(
    x_hbm, range_hbm, taps_hbm, shift_hbm, azimuth_hbm,
    x_ref, far_near_ref, far_away_ref, far_mid_ref, core_outer_ref, core_mid_ref,
    w_ref, taps_ref, splat_ref, azimuth_ref, range_ref, shift_ref, sems,
):
    rows = x_ref.shape[1]
    near, away = near_away_rows(rows)
    starts = [near, away] + list(range(CHUNK, rows - CHUNK, CHUNK))
    moves = [
        (range_hbm, range_ref),
        (taps_hbm, taps_ref),
        (shift_hbm, shift_ref),
        (azimuth_hbm, azimuth_ref),
    ]
    small = len(moves)
    for start in starts:
        picked = pl.ds(start, CHUNK)
        moves.append((x_hbm.at[:, picked, :], x_ref.at[:, picked, :]))
    copies = [
        pltpu.make_async_copy(source, target, sems.at[i])
        for i, (source, target) in enumerate(moves)
    ]
    for copy in copies:
        copy.start()
    for copy in copies[:small]:
        copy.wait()
    for ref in (core_outer_ref, core_mid_ref):
        extra = ref.shape[1] - 5 * CHUNK
        ref[:, 5 * CHUNK :, :] = jnp.zeros((ref.shape[0], extra, LANES), BF16)
    range_toeplitz(range_ref, w_ref)
    for b in range(splat_ref.shape[0]):
        splat_ref[b] = jnp.full(splat_ref.shape[1:], shift_ref[b], jnp.int32)

    def body(odd):
        for i, start in enumerate(starts):
            copies[small + i].wait()
            far = [(far_near_ref, 0), (far_away_ref, 0)][i] if i < 2 else (far_mid_ref, i - 2)
            core = (core_outer_ref, i) if i < 2 else (core_mid_ref, i - 2)
            write_edge(x_ref, start, *core, 1 - odd)
            write_edge(x_ref, start, *far, odd)

    by_parity("rg", body)


def range_edges(raw, range_chirp, migration_taps, block_shift, azimuth_chirp):
    chunks = raw.shape[1] // CHUNK
    blocks = block_shift.shape[0]
    depth = range_chirp.shape[1] + LANES
    args = (raw, range_chirp, migration_taps, block_shift, azimuth_chirp)
    return pl.pallas_call(
        edges_kernel,
        out_shape=(jax.ShapeDtypeStruct(raw.shape, BF16),)
        + tuple(
            jax.ShapeDtypeStruct((n, 5 * CHUNK + extra, LANES), BF16)
            for n, extra in ((1, 0), (1, 0), (chunks - 2, 0), (2, 2 * PAD), (chunks - 2, PAD))
        )
        + (
            jax.ShapeDtypeStruct((2 * depth, 2 * LANES), BF16),
            jax.ShapeDtypeStruct(migration_taps.shape, BF16),
            jax.ShapeDtypeStruct((blocks, 8, LANES), jnp.int32),
            jax.ShapeDtypeStruct(azimuth_chirp.shape, BF16),
        ),
        in_specs=[pl.BlockSpec(memory_space=pltpu.HBM)] * len(args),
        out_specs=(pl.BlockSpec(memory_space=pltpu.VMEM),) * 10,
        scratch_shapes=[
            pltpu.VMEM(range_chirp.shape, BF16),
            pltpu.SMEM(block_shift.shape, jnp.int32),
            pltpu.SemaphoreType.DMA((chunks + len(args) - 1,)),
        ],
        compiler_params=params(),
        name="range_edges",
    )(*(in_hbm(x) for x in args))


def window_tiles(x_ref, start, left, right, part):
    half = CHUNK // 2
    low = low_lanes(CHUNK)
    picked = pl.ds(start, CHUNK)

    def halo(edge):
        ref, chunk = edge
        at = 4 * CHUNK + part * half
        tiles = [ref[chunk, (2 * part + i) * CHUNK : (2 * part + i + 1) * CHUNK, :] for i in (0, 1)]
        return tiles, ref[chunk, at : at + half, :]

    before, first = halo(left)
    after, final = halo(right)
    own = [x_ref[part, picked, tile_of(t)] for t in range(x_ref.shape[2] // LANES)]
    rolled = [lane_roll(t) for t in before + own + after]
    rolled = (
        [jnp.concatenate([first, lane_roll(first)], axis=0)]
        + rolled
        + [jnp.concatenate([lane_roll(final), final], axis=0)]
    )
    return [jnp.where(low, rolled[i], rolled[i + 1]) for i in range(len(rolled) - 1)]


def compress_chunk(s_ref, start, left, right, w_ref, m_ref, out_ref, out_start, c_ref):
    rows = CHUNK
    taps = w_ref.shape[0] // (2 * LANES)
    tiles = [window_tiles(s_ref, start, left, right, part) for part in range(2)]
    for j in range(c_ref.shape[1] // LANES):
        window = jnp.concatenate(tiles[0][j : j + taps] + tiles[1][j : j + taps], axis=1)
        result = jnp.dot(window, w_ref[...], preferred_element_type=F32).astype(BF16)
        c_ref[0:rows, tile_of(j)] = result[:, :LANES]
        c_ref[rows:, tile_of(j)] = result[:, LANES:]
    for b in range(m_ref.shape[0]):
        window = c_ref[:, b * LANES : b * LANES + 2 * LANES]
        result = jnp.dot(window, m_ref[b], preferred_element_type=F32).astype(BF16)
        out_ref[0, out_start : out_start + rows, tile_of(b)] = result[:rows]
        out_ref[1, out_start : out_start + rows, tile_of(b)] = result[rows:]


def compress_kernel(which, s_ref, core_ref, far_ref, w_ref, *refs):
    near, away = near_away_rows(s_ref.shape[1])
    if which == "near":
        taps_ref, splat_ref, out_ref, m_ref, *c_refs = refs
        jobs = [(near, 0)]
    else:
        m_ref, out_ref, *c_refs = refs
        jobs = [(CHUNK * (i + 1), i) for i in range(out_ref.shape[1] // CHUNK)]
        if which == "away":
            jobs = [(away, 1)]

    def body(odd):
        if which == "near":
            migration_bands(taps_ref, splat_ref, m_ref)
        for i, (start, chunk) in enumerate(jobs):
            core, far = (core_ref, chunk), (far_ref, chunk if which == "mid" else 0)
            left, right = (core, far) if odd else (far, core)
            compress_chunk(
                s_ref, start, left, right, w_ref, m_ref, out_ref, i * CHUNK, c_refs[i]
            )

    by_parity("rg", body)


def compress(which, echo, core, far, w, *bands):
    rows, cells = echo.shape[1], echo.shape[2]
    count = rows // CHUNK - 2 if which == "mid" else 1
    args = (echo, core, far, w) + bands
    out = (jax.ShapeDtypeStruct((2, count * CHUNK, cells), BF16),)
    if which == "near":
        out += (jax.ShapeDtypeStruct((cells // LANES, 2 * LANES, LANES), BF16),)
    result = pl.pallas_call(
        functools.partial(compress_kernel, which),
        out_shape=out,
        in_specs=[pl.BlockSpec(memory_space=pltpu.VMEM)] * len(args),
        out_specs=(pl.BlockSpec(memory_space=pltpu.VMEM),) * len(out),
        scratch_shapes=[pltpu.VMEM((2 * CHUNK, cells + LANES), BF16)] * count,
        compiler_params=params(),
        name="compress_" + which,
    )(*args)
    return result if which == "near" else result[0]


def lines(ref, chunk):
    return lambda part, lanes: ref[part, chunk * CHUNK : (chunk + 1) * CHUNK, lanes]


def correlate_block(a_ref, b, pairs):
    taps = [a_ref[k, b] for k, _ in pairs]
    windows = [
        jnp.concatenate([window(0, tile_of(b)), window(1, tile_of(b))], axis=1)
        for _, window in pairs
    ]
    result = jnp.dot(
        jnp.concatenate(taps, axis=1),
        jnp.concatenate(windows, axis=0),
        preferred_element_type=F32,
    )
    top, bottom = result[:CHUNK], result[CHUNK:]
    return top[:, :LANES] + bottom[:, LANES:], top[:, LANES:] - bottom[:, :LANES]


def focus_outer_kernel(a_ref, near_ref, away_ref, part_ref, mid_part_ref):
    mids, steps, blocks = mid_part_ref.shape[0], a_ref.shape[0], a_ref.shape[1]

    def body(odd):
        first, final = (near_ref, away_ref) if odd else (away_ref, near_ref)
        order = {0: lines(first, 0), mids + 1: lines(final, 0)}
        jobs = [(part_ref.at[0], 0), (part_ref.at[1], mids + 1)]
        jobs += [(mid_part_ref.at[i], i + 1) for i in range(mids)]
        for out_ref, chunk in jobs:
            pairs = [
                (k, order[chunk + k - 1]) for k in range(steps) if chunk + k - 1 in order
            ]
            for b in range(blocks):
                out_ref[0, :, tile_of(b)], out_ref[1, :, tile_of(b)] = correlate_block(
                    a_ref, b, pairs
                )

    by_parity("az", body)


def focus_outer(a, near, away, mids):
    cells = near.shape[2]
    return pl.pallas_call(
        focus_outer_kernel,
        out_shape=(
            jax.ShapeDtypeStruct((2, 2, CHUNK, cells), F32),
            jax.ShapeDtypeStruct((mids, 2, CHUNK, cells), F32),
        ),
        in_specs=[pl.BlockSpec(memory_space=pltpu.VMEM)] * 3,
        out_specs=(pl.BlockSpec(memory_space=pltpu.VMEM),) * 2,
        compiler_params=params(),
        name="focus_outer",
    )(a, near, away)


def focus_mid_kernel(a_ref, mid_ref, part_ref, mid_part_ref, image_ref, end_ref, sum_ref, sems):
    mids, steps, blocks = mid_part_ref.shape[0], a_ref.shape[0], a_ref.shape[1]
    order = {i + 1: lines(mid_ref, i) for i in range(mids)}
    jobs = [(mid_part_ref.at[i], sum_ref.at[i], i + 1) for i in range(mids)]
    jobs += [(part_ref.at[0], end_ref.at[0], 0), (part_ref.at[1], end_ref.at[1], mids + 1)]
    copies = []
    for i, (before_ref, out_ref, chunk) in enumerate(jobs):
        pairs = [(k, order[chunk + k - 1]) for k in range(steps) if chunk + k - 1 in order]
        for b in range(blocks):
            real, imag = correlate_block(a_ref, b, pairs)
            out_ref[0, :, tile_of(b)] = before_ref[0, :, tile_of(b)] + real
            out_ref[1, :, tile_of(b)] = before_ref[1, :, tile_of(b)] + imag
        if i < mids:
            target = image_ref.at[:, pl.ds(chunk * CHUNK, CHUNK), :]
            copies.append(pltpu.make_async_copy(out_ref, target, sems.at[i]))
            copies[-1].start()
    for copy in copies:
        copy.wait()


def focus_mid(a, mid, part, mid_part):
    cells = mid.shape[2]
    mids = mid_part.shape[0]
    return pl.pallas_call(
        focus_mid_kernel,
        out_shape=(
            jax.ShapeDtypeStruct((2, (mids + 2) * CHUNK, cells), F32),
            jax.ShapeDtypeStruct(part.shape, F32),
        ),
        in_specs=[pl.BlockSpec(memory_space=pltpu.VMEM)] * 4,
        out_specs=(pl.BlockSpec(memory_space=pl.ANY), pl.BlockSpec(memory_space=pltpu.VMEM)),
        scratch_shapes=[pltpu.VMEM(mid_part.shape, F32), pltpu.SemaphoreType.DMA((mids,))],
        compiler_params=params(),
        name="focus_mid",
    )(a, mid, part, mid_part)


def add_halo(a_ref, end, part_ref, halo_ref, out_ref):
    for b in range(a_ref.shape[1]):
        real, imag = correlate_block(a_ref, b, [(2 * end, lines(halo_ref, 0))])
        out_ref[0, :, tile_of(b)] = part_ref[end, 0, :, tile_of(b)] + real
        out_ref[1, :, tile_of(b)] = part_ref[end, 1, :, tile_of(b)] + imag


def near_end_kernel(a_ref, part_ref, halo_ref, out_ref):
    by_parity("az", lambda odd: add_halo(a_ref, 1 - odd, part_ref, halo_ref, out_ref))


def near_end(a, part, halo):
    return pl.pallas_call(
        near_end_kernel,
        out_shape=jax.ShapeDtypeStruct(part.shape[1:], F32),
        in_specs=[pl.BlockSpec(memory_space=pltpu.VMEM)] * 3,
        out_specs=pl.BlockSpec(memory_space=pltpu.VMEM),
        compiler_params=params(),
        name="near_end",
    )(a, part, halo)


def ends_kernel(a_ref, part_ref, near_ref, halo_ref, _, image_ref, sum_ref, sems):
    rows = image_ref.shape[1]
    half = CHUNK // 2

    def body(odd):
        near_first, away_first = (1 - odd) * (rows - CHUNK), odd * (rows - CHUNK)
        copies = [
            pltpu.make_async_copy(
                near_ref, image_ref.at[:, pl.ds(near_first, CHUNK), :], sems.at[2]
            )
        ]
        copies[0].start()
        window = lines(halo_ref, 0)
        for h in range(2):
            picked = slice(h * half, (h + 1) * half)
            for b in range(a_ref.shape[1]):
                taps = jnp.concatenate(
                    [a_ref[2 * odd, b, base + h * half : base + (h + 1) * half] for base in (0, CHUNK)],
                    axis=0,
                )
                both = jnp.concatenate([window(0, tile_of(b)), window(1, tile_of(b))], axis=1)
                result = jnp.dot(taps, both, preferred_element_type=F32)
                top, bottom = result[:half], result[half:]
                real = top[:, :LANES] + bottom[:, LANES:]
                imag = top[:, LANES:] - bottom[:, :LANES]
                sum_ref[0, picked, tile_of(b)] = part_ref[odd, 0, picked, tile_of(b)] + real
                sum_ref[1, picked, tile_of(b)] = part_ref[odd, 1, picked, tile_of(b)] + imag
            target = image_ref.at[:, pl.ds(away_first + h * half, half), :]
            copies.append(pltpu.make_async_copy(sum_ref.at[:, picked, :], target, sems.at[h]))
            copies[-1].start()
        for copy in copies:
            copy.wait()

    by_parity("az", body)


def ends(a, part, near, halo, image):
    return pl.pallas_call(
        ends_kernel,
        out_shape=jax.ShapeDtypeStruct(image.shape, F32),
        in_specs=[pl.BlockSpec(memory_space=pltpu.VMEM)] * 4
        + [pl.BlockSpec(memory_space=pl.ANY)],
        out_specs=pl.BlockSpec(memory_space=pl.ANY),
        scratch_shapes=[pltpu.VMEM(near.shape, F32), pltpu.SemaphoreType.DMA((3,))],
        input_output_aliases={4: 0},
        compiler_params=params(),
        name="ends",
    )(a, part, near, halo, image)


def per_device(raw_echo, range_chirp, migration_taps, block_shift, azimuth_chirp):
    echo, far_near, far_away, far_mid, core_outer, core_mid, w, taps, splat, azimuth_chirp = range_edges(
        raw_echo, range_chirp, migration_taps, block_shift, azimuth_chirp
    )
    core_outer = swap(core_outer, "rg", 0)
    core_mid = swap(core_mid, "rg", 0)
    far_near = swap(far_near, "rg", 1)
    far_away = swap(far_away, "rg", 1)
    far_mid = swap(far_mid, "rg", 1)
    near, m = compress("near", echo, core_outer, far_near, w, taps, splat)
    near_halo = swap(near, "az", 0)
    core_outer, core_mid, near = lax.optimization_barrier((core_outer, core_mid, near))
    away = compress("away", echo, core_outer, far_away, w, m)
    away_halo = swap(away, "az", 1)
    away, azimuth_chirp = lax.optimization_barrier((away, azimuth_chirp))
    a = azimuth_weights(azimuth_chirp)
    part, mid_part = focus_outer(a, near, away, raw_echo.shape[1] // CHUNK - 2)
    far_mid, part = lax.optimization_barrier((far_mid, part))
    mid = compress("mid", echo, core_mid, far_mid, w, m)
    image, part = focus_mid(a, mid, part, mid_part)
    return ends(a, part, near_end(a, part, near_halo), away_halo, image)


def solution(mesh):
    placed = (P(None, "az", "rg"), P(), P(None, "rg"), P("rg"), P("rg", None, None))
    return jax.shard_map(
        per_device, mesh=mesh, in_specs=placed, out_specs=P(None, "az", "rg"), check_vma=False
    )
```
